32 devices in a mesh: seq: 16 (over z, y, core), head: 2 (over x).
Axes of the slice: x: 2, y: 2, z: 4, core: 2. Of those that a mesh axis runs over, the one named last changes fastest.
Arguments:
- att_q: bfloat16 [4096, 1280], P('seq', 'head'), may hold values from -150 to 150
- att_k: bfloat16 [4096, 1280], P('seq', 'head'), may hold values from -6 to 6
- att_v: bfloat16 [4096, 1280], P('seq', 'head'), may hold values from -6 to 6
- fast_q: bfloat16 [4096, 1280], P('seq', 'head'), may hold values from -6 to 6
- fast_k: bfloat16 [4096, 1280], P('seq', 'head'), may hold values from -6 to 6
- fast_v: bfloat16 [4096, 1280], P('seq', 'head'), may hold values from -6 to 6
- learn_rates: float32 [4096], P('seq'), may hold values from 0.0002 to 0.002
- w_gate: bfloat16 [640, 1280], P(None, 'head'), may hold values from -0.25 to 0.25
- w_up: bfloat16 [640, 1280], P(None, 'head'), may hold values from -0.25 to 0.25
- w_down: bfloat16 [640, 1280], P(None, 'head'), may hold values from -0.25 to 0.25
Outputs:
- attended: bfloat16 [4096, 1280], P('seq', 'head')
- fast_out: bfloat16 [4096, 1280], P('seq', 'head')
The draws below stay inside these ranges and needn't reach their ends.
All inputs are finite; a program needn't handle non-finite values.
Results may differ from the reference program's by a relative error of at most 0.007.
The reference program's roundings to bfloat16 on the way (of `softmax_w` and `hidden_q`) count: a program that leaves them out, or rounds other values in their place, can miss the bound.
Values may be sent and summed in bfloat16 or wider, within the bound.
No kernel may reach another device: no remote copies, remote signals or barrier semaphores. Data moves between devices by JAX's collectives and lax.ppermute only.
A program may use at most 64 MiB of HBM per device.

```python
import math
import jax
import jax.numpy as jnp
from jax import lax

TOK_DEV = 256
WINDOW = 1024
HEAD_DIM = 128
FAST_D = 640
FAST_HID = 640
TOKENS = 4096
AHEADS = 10
FHEADS = 2


def attention_pair(key):
    base_key = jax.random.fold_in(key, 31)
    arr_shape = (TOKENS, AHEADS * HEAD_DIM)
    query_all = jnp.clip(jax.random.normal(jax.random.fold_in(base_key, 1), arr_shape, jnp.float32), -5.0, 5.0)
    keys_all = jnp.clip(jax.random.normal(jax.random.fold_in(base_key, 2), arr_shape, jnp.float32), -5.0, 5.0)
    return (query_all, keys_all)


def draw_att_q(key, part):
    return attention_pair(key)[0].astype(jnp.bfloat16)


def draw_att_k(key, part):
    return attention_pair(key)[1].astype(jnp.bfloat16)


def shard_levels(key, extent, pieces, low, top_value):
    factor_of, own = 1.0, jax.random.fold_in(key, 6)
    for axis_at, blocks in pieces:
        draws = jnp.exp(jax.random.uniform(jax.random.fold_in(own, axis_at), (blocks,), jnp.float32, low / len(pieces), top_value / len(pieces)))
        factor_of = factor_of * jnp.repeat(draws, extent[axis_at] // blocks).reshape([-1 if axis == axis_at else 1 for axis in range(len(extent))])
    return factor_of


def centred(stream_key, dims, scale, limit, split=(), kind=jnp.bfloat16):
    values = jax.random.normal(stream_key, dims, jnp.float32) * scale
    if len(split) > 0:
        values = shard_levels(stream_key, dims, split, -0.22, 0.18) * values
    return jnp.clip(values, min=-limit, max=limit).astype(kind)


def setup_inputs(seed: int = 0) -> dict:
    splits = jax.random.split(jax.random.key(seed), 11)
    att_q = draw_att_q(jax.random.fold_in(splits[10], 71), 0)
    att_k = draw_att_k(jax.random.fold_in(splits[10], 71), 0)
    att_v = centred(splits[2], (TOKENS, AHEADS * HEAD_DIM), 1.0, 6.0, ((0, 16), (1, 2)))
    fast_q = centred(splits[3], (TOKENS, FHEADS * FAST_D), 1.0, 6.0, ((0, 16), (1, 2)))
    fast_k = centred(splits[4], (TOKENS, FHEADS * FAST_D), 1.0, 6.0, ((0, 16), (1, 2)))
    fast_v = centred(splits[5], (TOKENS, FHEADS * FAST_D), 1.0, 6.0, ((0, 16), (1, 2)))
    learn_rates = jnp.clip(jnp.exp(math.log(0.002) - 2.3025852 * jax.random.uniform(splits[6], (TOKENS,), jnp.float32) ** shard_levels(splits[6], (TOKENS,), ((0, 16),), -0.2, 0.2)), 0.0002, 0.002)
    w_gate = centred(splits[7], (FAST_D, FHEADS * FAST_HID), FAST_D ** -0.5, 0.25, ((1, 2),))
    w_up = centred(splits[8], (FAST_D, FHEADS * FAST_HID), FAST_D ** -0.5, 0.25, ((1, 2),))
    w_down = centred(splits[9], (FAST_D, FHEADS * FAST_HID), FAST_HID ** -0.5, 0.25, ((1, 2),))
    return {"att_q": att_q, "att_k": att_k, "att_v": att_v, "fast_q": fast_q, "fast_k": fast_k, "fast_v": fast_v, "learn_rates": learn_rates, "w_gate": w_gate, "w_up": w_up, "w_down": w_down}


norm_eps = 1e-06

def silu_slope(pre_act):
    sigmoid_v = jax.nn.sigmoid(pre_act)
    return sigmoid_v * (1.0 + pre_act * (1.0 - sigmoid_v))

def window_attention(att_q, att_k, att_v):
    token_count = att_q.shape[0]
    zero_pad = jnp.zeros((WINDOW, att_k.shape[1]), att_k.dtype)
    keys_all = jnp.concatenate([zero_pad, att_k], 0)
    values_all = jnp.concatenate([zero_pad, att_v], 0)
    block_count = token_count // TOK_DEV

    def one_block(block_index):
        row_start = (block_index * TOK_DEV).astype(jnp.int32)
        query_block = lax.dynamic_slice_in_dim(att_q, row_start, TOK_DEV, 0).reshape(TOK_DEV, AHEADS, HEAD_DIM)
        key_block = lax.dynamic_slice_in_dim(keys_all, row_start, WINDOW + TOK_DEV, 0).reshape(WINDOW + TOK_DEV, AHEADS, HEAD_DIM)
        val_block = lax.dynamic_slice_in_dim(values_all, row_start, WINDOW + TOK_DEV, 0).reshape(WINDOW + TOK_DEV, AHEADS, HEAD_DIM)
        scores = jnp.einsum('qhd,khd->hqk', query_block.astype(jnp.float32), key_block.astype(jnp.float32)) * HEAD_DIM ** (-0.5)
        query_pos = row_start + jnp.arange(TOK_DEV, dtype=jnp.int32)
        key_pos = row_start - WINDOW + jnp.arange(WINDOW + TOK_DEV, dtype=jnp.int32)
        allowed = (key_pos[None, :] <= query_pos[:, None]) & (key_pos[None, :] > query_pos[:, None] - WINDOW) & (key_pos[None, :] >= 0)
        scores = jnp.where(allowed[None], scores, jnp.float32(-1e+30))
        row_max = lax.optimization_barrier(jnp.max(scores, axis=-1, keepdims=True))
        expd = jnp.exp(scores - row_max)
        softmax_w = (expd / lax.optimization_barrier(jnp.sum(expd, axis=-1, keepdims=True))).astype(jnp.bfloat16)
        result = jnp.einsum('hqk,khd->qhd', softmax_w.astype(jnp.float32), val_block.astype(jnp.float32))
        return result.reshape(TOK_DEV, AHEADS * HEAD_DIM).astype(jnp.bfloat16)
    blocks = lax.map(one_block, jnp.arange(block_count, dtype=jnp.int32))
    return blocks.reshape(token_count, AHEADS * HEAD_DIM)

def renorm(old_weights, gradient):
    old_f = old_weights.astype(jnp.float32)
    updated = old_f + gradient
    old_norm = jnp.sqrt(lax.optimization_barrier(jnp.sum(old_f * old_f, axis=0, keepdims=True)))
    new_sq = lax.optimization_barrier(jnp.sum(updated * updated, axis=0, keepdims=True))
    return (updated * (old_norm / jnp.sqrt(new_sq + norm_eps))).astype(jnp.bfloat16)

def reference(att_q, att_k, att_v, fast_q, fast_k, fast_v, learn_rates, w_gate, w_up, w_down):
    attended = window_attention(att_q, att_k, att_v)
    rate_col = learn_rates[:, None]
    outputs = []
    for fast_head in range(FHEADS):
        feat_lo = fast_head * FAST_D
        hid_lo = fast_head * FAST_HID
        key_rows = fast_k[:, feat_lo:feat_lo + FAST_D]
        val_rows = fast_v[:, feat_lo:feat_lo + FAST_D]
        query_rows = fast_q[:, feat_lo:feat_lo + FAST_D]
        gate_w = w_gate[:, hid_lo:hid_lo + FAST_HID]
        up_w = w_up[:, hid_lo:hid_lo + FAST_HID]
        down_w = w_down[:, hid_lo:hid_lo + FAST_HID]
        pre_gate = jnp.dot(key_rows, gate_w, preferred_element_type=jnp.float32)
        pre_up = jnp.dot(key_rows, up_w, preferred_element_type=jnp.float32)
        back_proj = jnp.dot(val_rows, down_w, preferred_element_type=jnp.float32)
        gate_term = (rate_col * back_proj * pre_up * silu_slope(pre_gate)).astype(jnp.bfloat16)
        up_term = (rate_col * back_proj * jax.nn.silu(pre_gate)).astype(jnp.bfloat16)
        down_term = (rate_col * jax.nn.silu(pre_gate) * pre_up).astype(jnp.bfloat16)
        grad_gate = jnp.dot(key_rows.T, gate_term, preferred_element_type=jnp.float32)
        grad_up = jnp.dot(key_rows.T, up_term, preferred_element_type=jnp.float32)
        grad_down = jnp.dot(val_rows.T, down_term, preferred_element_type=jnp.float32)
        new_gate = renorm(gate_w, grad_gate)
        new_up = renorm(up_w, grad_up)
        new_down = renorm(down_w, grad_down)
        gate_q = jnp.dot(query_rows, new_gate, preferred_element_type=jnp.float32)
        up_q = jnp.dot(query_rows, new_up, preferred_element_type=jnp.float32)
        hidden_q = (jax.nn.silu(gate_q) * up_q).astype(jnp.bfloat16)
        outputs.append(jnp.dot(hidden_q, new_down.T, preferred_element_type=jnp.float32).astype(jnp.bfloat16))
    fast_out = jnp.concatenate(outputs, axis=1)
    return (attended, fast_out)
```

```python
import functools

import jax
import jax.numpy as jnp
from jax import lax
from jax.experimental import pallas as pl
from jax.experimental.pallas import tpu as pltpu
from jax.sharding import PartitionSpec as P

WINDOW = 1024
HEAD_DIM = 128
norm_eps = 1e-06
f32 = jnp.float32
bf16 = jnp.bfloat16


def swapped(value, bit):
    count = lax.axis_size("seq")
    return lax.ppermute(value, "seq", [(at, at ^ bit) for at in range(count)])


def moved(value, pairs):
    return lax.ppermute(value, "seq", pairs)


def silu_slope(pre_act):
    sigmoid_v = jax.nn.sigmoid(pre_act)
    return sigmoid_v * (1.0 + pre_act * (1.0 - sigmoid_v))


def attention_kernel(blocks, place_ref, q_ref, *refs):
    keys, vals, out_ref = refs[:blocks], refs[blocks : 2 * blocks], refs[2 * blocks]
    rows = q_ref.shape[0]
    place = place_ref[0]
    query = q_ref[...]
    q_at = lax.broadcasted_iota(jnp.int32, (rows, rows), 0)
    k_at = lax.broadcasted_iota(jnp.int32, (rows, rows), 1)
    scores = []
    for at in range(blocks):
        back = blocks - 1 - at
        part = lax.dot_general(
            query, keys[at][...], (((1,), (1,)), ((), ())), preferred_element_type=f32
        ) * HEAD_DIM ** (-0.5)
        if back == 0:
            part = jnp.where(k_at <= q_at, part, -1e30)
        elif back == blocks - 1:
            part = jnp.where((k_at > q_at) & (place >= back), part, -1e30)
        else:
            part = jnp.where(place >= back, part, -1e30)
        scores.append(part)
    row_max = functools.reduce(jnp.maximum, [jnp.max(s, axis=1, keepdims=True) for s in scores])
    expd = [jnp.exp(s - row_max) for s in scores]
    total = functools.reduce(jnp.add, [jnp.sum(e, axis=1, keepdims=True) for e in expd])
    scale = 1.0 / total
    result = jnp.zeros(out_ref.shape, f32)
    for at in range(blocks):
        result += jnp.dot(
            (expd[at] * scale).astype(bf16), vals[at][...], preferred_element_type=f32
        )
    out_ref[...] = result.astype(bf16)


def attention(place, query, keys, vals):
    rows, width = query.shape
    blocks = len(keys)
    spec = pl.BlockSpec((rows, HEAD_DIM), lambda head, place: (0, head))
    return pl.pallas_call(
        functools.partial(attention_kernel, blocks),
        out_shape=jax.ShapeDtypeStruct((rows, width), bf16),
        grid_spec=pltpu.PrefetchScalarGridSpec(
            num_scalar_prefetch=1,
            grid=(width // HEAD_DIM,),
            in_specs=[spec] * (1 + 2 * blocks),
            out_specs=spec,
        ),
        compiler_params=pltpu.CompilerParams(vmem_limit_bytes=32 << 20),
        cost_estimate=pl.CostEstimate(
            flops=4 * rows * rows * blocks * width,
            bytes_accessed=2 * rows * width * (2 + 2 * blocks),
            transcendentals=rows * rows * blocks * width // HEAD_DIM,
        ),
    )(place[None], query, *keys, *vals)


def window_blocks(own, place):
    count = lax.axis_size("seq")
    hops = WINDOW // own.shape[0]
    if hops != 4:
        return [
            moved(own, [(at, at + hop) for at in range(count - hop)])
            for hop in range(hops, 0, -1)
        ] + [own]
    core, half = place % 2, (place // 2) % 2
    back4 = moved(own, [(at, at + 4) for at in range(count - 4)])
    back2 = swapped(jnp.where(half == 0, own, back4), 2)
    near = swapped(jnp.where(core == 0, own, back2), 1)
    far = swapped(jnp.where(core == 0, back2, back4), 1)
    return [back4, far, back2, near, own]


def body(att_q, att_k, att_v, fast_q, fast_k, fast_v, learn_rates, w_gate, w_up, w_down):
    count = lax.axis_size("seq")
    place = lax.axis_index("seq")
    core = place % 2
    feats, hidden = w_gate.shape
    bits = [1 << at for at in range(1, count.bit_length() - 1)]
    depth = len(bits)
    units = hidden // count

    key_blocks = window_blocks(att_k, place)
    val_blocks = window_blocks(att_v, place)

    other_k, other_v = swapped(fast_k, 1), swapped(fast_v, 1)
    other_r = swapped(learn_rates, 1)
    keys2 = jnp.concatenate([fast_k, other_k], axis=0)
    vals2 = jnp.concatenate([fast_v, other_v], axis=0)
    rate = jnp.concatenate([learn_rates, other_r])[None, :]

    def half_t(weights):
        return lax.dynamic_slice_in_dim(weights.T, core * (hidden // 2), hidden // 2, 0)

    gate_t, up_t, down_t = half_t(w_gate), half_t(w_up), half_t(w_down)

    def project(weights_t, rows):
        return lax.dot_general(
            weights_t, rows, (((1,), (1,)), ((), ())), preferred_element_type=f32
        )

    pre_gate = project(gate_t, keys2)
    pre_up = project(up_t, keys2)
    back = project(down_t, vals2)
    gate_term = (rate * back * pre_up * silu_slope(pre_gate)).astype(bf16)
    up_term = (rate * back * jax.nn.silu(pre_gate)).astype(bf16)
    down_term = (rate * jax.nn.silu(pre_gate) * pre_up).astype(bf16)
    grads = jnp.stack(
        [
            jnp.dot(gate_term, keys2, preferred_element_type=f32),
            jnp.dot(up_term, keys2, preferred_element_type=f32),
            jnp.dot(down_term, vals2, preferred_element_type=f32),
        ]
    )
    split = (feats * 3 // 5) // 128 * 128
    grads = grads.reshape((3,) + (2,) * depth + (units, feats))
    orders = [bits, [bits[1], bits[0]] + bits[2:]]

    def axis_of(bit, left):
        return 1 + sorted(left, reverse=True).index(bit)

    parts = [grads[..., :split], grads[..., split:]]
    left = [list(bits), list(bits)]
    for step in range(depth):
        for which in range(2):
            bit = orders[which][step]
            own_bit = (place // bit) % 2
            axis = axis_of(bit, left[which])
            send = lax.dynamic_index_in_dim(parts[which], 1 - own_bit, axis, keepdims=False)
            keep = lax.dynamic_index_in_dim(parts[which], own_bit, axis, keepdims=False)
            parts[which] = keep + swapped(send.astype(bf16), bit).astype(f32)
            left[which].remove(bit)
    summed = jnp.concatenate(parts, axis=-1)

    old = jnp.stack(
        [
            lax.dynamic_slice_in_dim(w, (place // 2) * units, units, 0)
            for w in (gate_t, up_t, down_t)
        ]
    ).astype(f32)
    updated = old + summed
    old_norm = jnp.sqrt(jnp.sum(old * old, axis=-1, keepdims=True))
    squares = jnp.sum(updated * updated, axis=-1, keepdims=True)
    fresh = (updated * (old_norm / jnp.sqrt(squares + norm_eps))).astype(bf16)

    parts = [fresh[..., :split], fresh[..., split:]]
    have = [[], []]
    for step in reversed(range(depth)):
        for which in range(2):
            bit = orders[which][step]
            own_bit = (place // bit) % 2
            have[which].append(bit)
            axis = axis_of(bit, have[which])
            got = swapped(parts[which], bit)
            mine = jnp.where(own_bit == 0, 0, 1)
            parts[which] = jnp.stack(
                [
                    jnp.where(mine == 0, parts[which], got),
                    jnp.where(mine == 0, got, parts[which]),
                ],
                axis,
            )
    half_w = jnp.concatenate(parts, axis=-1).reshape(3, hidden // 2, feats)
    other_w = swapped(half_w, 1)
    new = [jnp.concatenate([half_w[at], other_w[at]], axis=0) for at in range(3)]
    gate_q = lax.dot_general(
        fast_q, new[0], (((1,), (1,)), ((), ())), preferred_element_type=f32
    )
    up_q = lax.dot_general(
        fast_q, new[1], (((1,), (1,)), ((), ())), preferred_element_type=f32
    )
    hidden_q = (jax.nn.silu(gate_q) * up_q).astype(bf16)
    fast_out = jnp.dot(hidden_q, new[2], preferred_element_type=f32).astype(bf16)
    attended = attention(place, att_q, key_blocks, val_blocks)
    return (attended, fast_out)


def solution(mesh):
    tokens = P("seq", "head")
    weights = P(None, "head")
    return jax.shard_map(
        body,
        mesh=mesh,
        in_specs=(tokens,) * 6 + (P("seq"),) + (weights,) * 3,
        out_specs=(tokens, tokens),
        check_vma=False,
    )
```

```python
import functools

import jax
import jax.numpy as jnp
from jax import lax
from jax.experimental import pallas as pl
from jax.experimental.pallas import tpu as pltpu
from jax.sharding import PartitionSpec as P

WINDOW = 1024
HEAD_DIM = 128
norm_eps = 1e-06
f32 = jnp.float32
bf16 = jnp.bfloat16

SMEM = pl.BlockSpec(memory_space=pltpu.SMEM)
VMEM = pl.BlockSpec(memory_space=pltpu.VMEM)
PARAMS = pltpu.CompilerParams(vmem_limit_bytes=40 << 20)


def swapped(value, bit):
    count = lax.axis_size("seq")
    return lax.ppermute(value, "seq", [(at, at ^ bit) for at in range(count)])


def cost(flops, moved_bytes, exps=0):
    return pl.CostEstimate(flops=flops, bytes_accessed=moved_bytes, transcendentals=exps)


def attention_kernel(place_ref, q_ref, own_ref, back2_ref, back4_ref, pair_ref, out_ref):
    rows = q_ref.shape[0]
    place = place_ref[0]
    query = q_ref[...]
    blocks = [back4_ref, pair_ref.at[1], back2_ref, pair_ref.at[0], own_ref]
    q_at = lax.broadcasted_iota(jnp.int32, (rows, rows), 0)
    k_at = lax.broadcasted_iota(jnp.int32, (rows, rows), 1)
    scores = []
    for at, block in enumerate(blocks):
        back = len(blocks) - 1 - at
        part = lax.dot_general(
            query, block[0], (((1,), (1,)), ((), ())), preferred_element_type=f32
        ) * HEAD_DIM ** (-0.5)
        if back == 0:
            part = jnp.where(k_at <= q_at, part, -1e30)
        elif at == 0:
            part = jnp.where((k_at > q_at) & (place >= back), part, -1e30)
        else:
            part = jnp.where(place >= back, part, -1e30)
        scores.append(part)
    row_max = functools.reduce(jnp.maximum, [jnp.max(s, axis=1, keepdims=True) for s in scores])
    expd = [jnp.exp(s - row_max) for s in scores]
    total = functools.reduce(jnp.add, [jnp.sum(e, axis=1, keepdims=True) for e in expd])
    scale = 1.0 / total
    result = jnp.zeros(out_ref.shape, f32)
    for part, block in zip(expd, blocks):
        result += jnp.dot((part * scale).astype(bf16), block[1], preferred_element_type=f32)
    out_ref[...] = result.astype(bf16)


def attention(place, query, own, back2, back4, pair):
    rows, width = query.shape
    flat = pl.BlockSpec((rows, HEAD_DIM), lambda head: (0, head))
    two = pl.BlockSpec((2, rows, HEAD_DIM), lambda head: (0, 0, head))
    four = pl.BlockSpec((2, 2, rows, HEAD_DIM), lambda head: (0, 0, 0, head))
    return pl.pallas_call(
        attention_kernel,
        out_shape=jax.ShapeDtypeStruct((rows, width), bf16),
        grid=(width // HEAD_DIM,),
        in_specs=[SMEM, flat, two, two, two, four],
        out_specs=flat,
        compiler_params=PARAMS,
        cost_estimate=cost(20 * rows * rows * width, 24 * rows * width, 5 * rows * rows * 5),
        name="attention",
    )(place[None], query, own, back2, back4, pair)


def window_blocks(att_k, att_v, place):
    count = lax.axis_size("seq")
    own = jnp.stack([att_k, att_v])
    back4 = lax.ppermute(own, "seq", [(at, at + 4) for at in range(count - 4)])
    back2 = swapped(jnp.where((place // 2) % 2 == 0, own, back4), 2)
    first = place % 2 == 0
    pair = swapped(
        jnp.stack([jnp.where(first, own, back2), jnp.where(first, back2, back4)]), 1
    )
    return own, back2, back4, pair


def turn_kernel(place_ref, gate_ref, up_ref, down_ref, out_ref, hold_ref):
    hidden = gate_ref.shape[1]
    half = hidden // 2
    window = hold_ref.shape[0]
    core = place_ref[0] % 2
    low = pl.multiple_of(core * (hidden - window), 128)
    off = pl.multiple_of(core * (half - hidden + window), 64)
    for at, ref in enumerate((gate_ref, up_ref, down_ref)):
        hold_ref[...] = ref[:, pl.ds(low, window)].T
        out_ref[at] = hold_ref[pl.ds(off, half), :]


def turned(place, w_gate, w_up, w_down):
    feats, hidden = w_gate.shape
    half = hidden // 2
    window = -(-half // 128) * 128
    return pl.pallas_call(
        turn_kernel,
        out_shape=jax.ShapeDtypeStruct((3, half, feats), bf16),
        in_specs=[SMEM, VMEM, VMEM, VMEM],
        out_specs=VMEM,
        scratch_shapes=[pltpu.VMEM((window, feats), bf16)],
        compiler_params=PARAMS,
        cost_estimate=cost(0, 9 * feats * hidden),
        name="turn",
    )(place[None], w_gate, w_up, w_down)


def grad_kernel(
    place_ref, turned_ref, k0_ref, k1_ref, v0_ref, v1_ref, r0_ref, r1_ref,
    send_a, keep_a, send_b, keep_b, hold,
):
    def project(at, rows):
        return lax.dot_general(
            turned_ref[at], rows, (((1,), (1,)), ((), ())), preferred_element_type=f32
        )

    terms = []
    for keys, vals, rate_ref in ((k0_ref, v0_ref, r0_ref), (k1_ref, v1_ref, r1_ref)):
        rate = rate_ref[...]
        pre_gate = project(0, keys[...])
        pre_up = project(1, keys[...])
        back = rate * project(2, vals[...])
        sigmoid_v = jax.nn.sigmoid(pre_gate)
        silu = pre_gate * sigmoid_v
        slope = sigmoid_v * (1.0 + pre_gate * (1.0 - sigmoid_v))
        terms.append(
            (
                (back * pre_up * slope).astype(bf16),
                (back * silu).astype(bf16),
                (rate * silu * pre_up).astype(bf16),
            )
        )
    sources = ((k0_ref, k1_ref), (k0_ref, k1_ref), (v0_ref, v1_ref))
    for at in range(3):
        hold[at] = jnp.dot(
            terms[0][at], sources[at][0][...], preferred_element_type=f32
        ) + jnp.dot(terms[1][at], sources[at][1][...], preferred_element_type=f32)
    split = send_a.shape[-1]
    quart = send_a.shape[-2]
    row0 = (place_ref[0] // 2) % 2
    row1 = (place_ref[0] // 4) % 2
    for at in range(3):
        for other in range(2):
            there = pl.multiple_of((2 * (1 - row0) + other) * quart, quart)
            here = pl.multiple_of((2 * row0 + other) * quart, quart)
            send_a[at, other] = hold[at, pl.ds(there, quart), :split].astype(bf16)
            keep_a[at, other] = hold[at, pl.ds(here, quart), :split]
            there = pl.multiple_of((2 * other + 1 - row1) * quart, quart)
            here = pl.multiple_of((2 * other + row1) * quart, quart)
            send_b[at, other] = hold[at, pl.ds(there, quart), split:].astype(bf16)
            keep_b[at, other] = hold[at, pl.ds(here, quart), split:]


def gradients(place, turned_w, split, k0, k1, v0, v1, r0, r1):
    _, half, feats = turned_w.shape
    rows = k0.shape[0]
    quart = half // 4
    return pl.pallas_call(
        grad_kernel,
        out_shape=[
            jax.ShapeDtypeStruct((3, 2, quart, width), kind)
            for width in (split, feats - split)
            for kind in (bf16, f32)
        ],
        in_specs=[SMEM] + [VMEM] * 7,
        out_specs=[VMEM] * 4,
        scratch_shapes=[pltpu.VMEM((3, half, feats), f32)],
        compiler_params=PARAMS,
        cost_estimate=cost(24 * rows * half * feats, 20 * half * feats, 2 * half * rows),
        name="gradients",
    )(place[None], turned_w, k0, k1, v0, v1, r0, r1)


def last_kernel(q_ref, a0, a1, b0, b1, c0, c1, d0, d1, attended, out_ref, kept, hold):
    quart = a0.shape[1] // 2
    split = a0.shape[2]
    half = 4 * quart
    for base, (first0, first1, rest0, rest1) in ((0, (a0, a1, b0, b1)), (half, (c0, c1, d0, d1))):
        for at in range(3):
            hold[at, base : base + 2 * quart, :split] = first0[at]
            hold[at, base + 2 * quart : base + half, :split] = first1[at]
            hold[at, base : base + quart, split:] = rest0[at, :quart]
            hold[at, base + quart : base + 2 * quart, split:] = rest1[at, :quart]
            hold[at, base + 2 * quart : base + 3 * quart, split:] = rest0[at, quart:]
            hold[at, base + 3 * quart : base + half, split:] = rest1[at, quart:]
    query = q_ref[...]
    gate_q = lax.dot_general(
        query, hold[0], (((1,), (1,)), ((), ())), preferred_element_type=f32
    )
    up_q = lax.dot_general(query, hold[1], (((1,), (1,)), ((), ())), preferred_element_type=f32)
    hidden_q = (gate_q * jax.nn.sigmoid(gate_q) * up_q).astype(bf16)
    out_ref[...] = jnp.dot(hidden_q, hold[2], preferred_element_type=f32).astype(bf16)


def last_step(query, pieces, attended):
    rows, feats = query.shape
    half = 2 * pieces[0].shape[1]
    anywhere = pl.BlockSpec(memory_space=pl.ANY)
    return pl.pallas_call(
        last_kernel,
        out_shape=[
            jax.ShapeDtypeStruct((rows, feats), bf16),
            jax.ShapeDtypeStruct(attended.shape, bf16),
        ],
        in_specs=[VMEM] * 9 + [anywhere],
        out_specs=[VMEM, anywhere],
        input_output_aliases={9: 1},
        scratch_shapes=[pltpu.VMEM((3, 2 * half, feats), bf16)],
        compiler_params=PARAMS,
        cost_estimate=cost(12 * rows * half * feats, 12 * half * feats, 2 * half * rows),
        name="last",
    )(query, *pieces, attended)


def body(att_q, att_k, att_v, fast_q, fast_k, fast_v, learn_rates, w_gate, w_up, w_down):
    count = lax.axis_size("seq")
    place = lax.axis_index("seq")
    feats, hidden = w_gate.shape
    half = hidden // 2
    quart = half // 4
    units = hidden // count
    split = (feats * 3 // 5) // 128 * 128
    later = [1 << at for at in range(3, count.bit_length() - 1)]
    own_bit = {bit: (place // bit) % 2 for bit in [2, 4] + later}

    rates = learn_rates[None, :]
    other_k, other_v, other_r = swapped(fast_k, 1), swapped(fast_v, 1), swapped(rates, 1)
    own, back2, back4, pair = window_blocks(att_k, att_v, place)
    turned_w = turned(place, w_gate, w_up, w_down)
    send_a, keep_a, send_b, keep_b = gradients(
        place, turned_w, split, fast_k, other_k, fast_v, other_v, rates, other_r
    )

    def halved(keep, got, bit):
        total = keep + got.astype(f32)
        send = lax.dynamic_index_in_dim(total, 1 - own_bit[bit], 1, keepdims=False)
        return send.astype(bf16), lax.dynamic_index_in_dim(total, own_bit[bit], 1, keepdims=False)

    send_a, keep_a = halved(keep_a, swapped(send_a, 2), 4)
    send_b, keep_b = halved(keep_b, swapped(send_b, 4), 2)
    grads = jnp.concatenate(
        [
            keep_a + swapped(send_a, 4).astype(f32),
            keep_b + swapped(send_b, 2).astype(f32),
        ],
        axis=-1,
    )
    start = own_bit[2] * 2 * quart + own_bit[4] * quart
    rest = quart
    for bit in later:
        rest //= 2
        grads = grads.reshape(3, 2, rest, feats)
        send = lax.dynamic_index_in_dim(grads, 1 - own_bit[bit], 1, keepdims=False)
        keep = lax.dynamic_index_in_dim(grads, own_bit[bit], 1, keepdims=False)
        grads = keep + swapped(send.astype(bf16), bit).astype(f32)
        start += own_bit[bit] * rest

    old = lax.dynamic_slice_in_dim(turned_w, start, units, 1).astype(f32)
    updated = old + grads
    old_norm = jnp.sqrt(jnp.sum(old * old, axis=-1, keepdims=True))
    squares = jnp.sum(updated * updated, axis=-1, keepdims=True)
    fresh = (updated * (old_norm / jnp.sqrt(squares + norm_eps))).astype(bf16)

    for bit in reversed(later):
        fresh = jnp.concatenate([fresh, swapped(fresh, bit)], axis=1)
    a_part, b_part = fresh[..., :split], fresh[..., split:]
    a_near = jnp.concatenate([a_part, swapped(a_part, 4)], axis=1)
    b_near = jnp.concatenate([b_part, swapped(b_part, 2)], axis=1)
    a_far, b_far = swapped(a_near, 2), swapped(b_near, 4)
    pieces = [a_near, a_far, b_near, b_far]
    pieces += [swapped(piece, 1) for piece in pieces]
    attended = attention(place, att_q, own, back2, back4, pair)
    fast_out, attended = last_step(fast_q, pieces, attended)
    return (attended, fast_out)


def solution(mesh):
    tokens = P("seq", "head")
    weights = P(None, "head")
    return jax.shard_map(
        body,
        mesh=mesh,
        in_specs=(tokens,) * 6 + (P("seq"),) + (weights,) * 3,
        out_specs=(tokens, tokens),
        check_vma=False,
    )
```

```python
import functools

import jax
import jax.numpy as jnp
from jax import lax
from jax.experimental import pallas as pl
from jax.experimental.pallas import tpu as pltpu
from jax.sharding import PartitionSpec as P

WINDOW = 1024
HEAD_DIM = 128
norm_eps = 1e-06
f32 = jnp.float32
bf16 = jnp.bfloat16

SMEM = pl.BlockSpec(memory_space=pltpu.SMEM)
VMEM = pl.BlockSpec(memory_space=pltpu.VMEM)
HBM = pl.BlockSpec(memory_space=pltpu.HBM)
ANY = pl.BlockSpec(memory_space=pl.ANY)
PARAMS = pltpu.CompilerParams(vmem_limit_bytes=16 << 20)


def swapped(value, bit):
    count = lax.axis_size("seq")
    return lax.ppermute(value, "seq", [(at, at ^ bit) for at in range(count)])


def cost(flops, moved_bytes, exps=0):
    return pl.CostEstimate(flops=flops, bytes_accessed=moved_bytes, transcendentals=exps)


def attention_kernel(
    place_ref, q_ref, own_ref, back2_ref, back4_ref, pair_ref, tied, out_ref
):
    del tied
    rows = q_ref.shape[0]
    place = place_ref[0]
    query = q_ref[...]
    blocks = [back4_ref, pair_ref.at[1], back2_ref, pair_ref.at[0], own_ref]
    q_at = lax.broadcasted_iota(jnp.int32, (rows, rows), 0)
    k_at = lax.broadcasted_iota(jnp.int32, (rows, rows), 1)
    scores = []
    for at, block in enumerate(blocks):
        back = len(blocks) - 1 - at
        part = lax.dot_general(
            query, block[0], (((1,), (1,)), ((), ())), preferred_element_type=f32
        ) * HEAD_DIM ** (-0.5)
        if back == 0:
            part = jnp.where(k_at <= q_at, part, -1e30)
        elif at == 0:
            part = jnp.where((k_at > q_at) & (place >= back), part, -1e30)
        else:
            part = jnp.where(place >= back, part, -1e30)
        scores.append(part)
    row_max = functools.reduce(jnp.maximum, [jnp.max(s, axis=1, keepdims=True) for s in scores])
    expd = [jnp.exp(s - row_max) for s in scores]
    total = functools.reduce(jnp.add, [jnp.sum(e, axis=1, keepdims=True) for e in expd])
    scale = 1.0 / total
    result = jnp.zeros(out_ref.shape, f32)
    for part, block in zip(expd, blocks):
        result += jnp.dot((part * scale).astype(bf16), block[1], preferred_element_type=f32)
    out_ref[...] = result.astype(bf16)


def attention(place, query, own, back2, back4, pair, tied):
    rows, width = query.shape
    flat = pl.BlockSpec((rows, HEAD_DIM), lambda head: (0, head))
    two = pl.BlockSpec((2, rows, HEAD_DIM), lambda head: (0, 0, head))
    four = pl.BlockSpec((2, 2, rows, HEAD_DIM), lambda head: (0, 0, 0, head))
    return pl.pallas_call(
        attention_kernel,
        out_shape=jax.ShapeDtypeStruct((rows, width), bf16),
        grid=(width // HEAD_DIM,),
        in_specs=[SMEM, flat, two, two, two, four, ANY],
        out_specs=flat,
        compiler_params=PARAMS,
        cost_estimate=cost(20 * rows * rows * width, 24 * rows * width, 5 * rows * rows * 5),
        name="attention",
    )(place[None], query, own, back2, back4, pair, tied)


def prepare_kernel(
    place_ref, gate_ref, up_ref, down_ref, key_ref, val_ref, out_ref, own_ref, wide, hold, sems
):
    hidden = gate_ref.shape[1]
    half = hidden // 2
    window = hold.shape[0]
    core = place_ref[0] % 2
    low = pl.multiple_of(core * (hidden - window), 128)
    off = pl.multiple_of(core * (half - hidden + window), 64)
    copies = [
        pltpu.make_async_copy(ref.at[:, pl.ds(low, window)], wide.at[at], sems.at[at])
        for at, ref in enumerate((gate_ref, up_ref, down_ref))
    ] + [
        pltpu.make_async_copy(ref, own_ref.at[at], sems.at[3 + at])
        for at, ref in enumerate((key_ref, val_ref))
    ]
    for copy in copies:
        copy.start()
    for at in range(3):
        copies[at].wait()
        hold[...] = wide[at].T
        out_ref[at] = hold[pl.ds(off, half), :]
    for copy in copies[3:]:
        copy.wait()


def prepared(place, w_gate, w_up, w_down, att_k, att_v):
    feats, hidden = w_gate.shape
    half = hidden // 2
    window = -(-half // 128) * 128
    return pl.pallas_call(
        prepare_kernel,
        out_shape=[
            jax.ShapeDtypeStruct((3, half, feats), bf16),
            jax.ShapeDtypeStruct((2,) + att_k.shape, bf16),
        ],
        in_specs=[SMEM] + [HBM] * 5,
        out_specs=[VMEM] * 2,
        scratch_shapes=[
            pltpu.VMEM((3, feats, window), bf16),
            pltpu.VMEM((window, feats), bf16),
            pltpu.SemaphoreType.DMA((5,)),
        ],
        compiler_params=PARAMS,
        cost_estimate=cost(0, 9 * feats * hidden),
        name="prepare",
    )(place[None], w_gate, w_up, w_down, att_k, att_v)


def grad_kernel(
    place_ref, turned_ref, k0_ref, k1_ref, v0_ref, v1_ref, r0_ref, r1_ref,
    send_a, keep_a, send_b, keep_b, hold,
):
    def project(at, rows):
        return lax.dot_general(
            turned_ref[at], rows, (((1,), (1,)), ((), ())), preferred_element_type=f32
        )

    terms = []
    for keys, vals, rate_ref in ((k0_ref, v0_ref, r0_ref), (k1_ref, v1_ref, r1_ref)):
        rate = rate_ref[...]
        pre_gate = project(0, keys[...])
        pre_up = project(1, keys[...])
        back = rate * project(2, vals[...])
        sigmoid_v = jax.nn.sigmoid(pre_gate)
        silu = pre_gate * sigmoid_v
        slope = sigmoid_v * (1.0 + pre_gate * (1.0 - sigmoid_v))
        terms.append(
            (
                (back * pre_up * slope).astype(bf16),
                (back * silu).astype(bf16),
                (rate * silu * pre_up).astype(bf16),
            )
        )
    sources = ((k0_ref, k1_ref), (k0_ref, k1_ref), (v0_ref, v1_ref))
    for at in range(3):
        hold[at] = jnp.dot(
            terms[0][at], sources[at][0][...], preferred_element_type=f32
        ) + jnp.dot(terms[1][at], sources[at][1][...], preferred_element_type=f32)
    split = send_a.shape[-1]
    quart = send_a.shape[-2]
    row0 = (place_ref[0] // 2) % 2
    row1 = (place_ref[0] // 4) % 2
    for at in range(3):
        for other in range(2):
            there = pl.multiple_of((2 * (1 - row0) + other) * quart, quart)
            here = pl.multiple_of((2 * row0 + other) * quart, quart)
            send_a[at, other] = hold[at, pl.ds(there, quart), :split].astype(bf16)
            keep_a[at, other] = hold[at, pl.ds(here, quart), :split]
            there = pl.multiple_of((2 * other + 1 - row1) * quart, quart)
            here = pl.multiple_of((2 * other + row1) * quart, quart)
            send_b[at, other] = hold[at, pl.ds(there, quart), split:].astype(bf16)
            keep_b[at, other] = hold[at, pl.ds(here, quart), split:]


def gradients(place, turned_w, split, k0, k1, v0, v1, r0, r1):
    _, half, feats = turned_w.shape
    rows = k0.shape[0]
    quart = half // 4
    return pl.pallas_call(
        grad_kernel,
        out_shape=[
            jax.ShapeDtypeStruct((3, 2, quart, width), kind)
            for width in (split, feats - split)
            for kind in (bf16, f32)
        ],
        in_specs=[SMEM] + [VMEM] * 7,
        out_specs=[VMEM] * 4,
        scratch_shapes=[pltpu.VMEM((3, half, feats), f32)],
        compiler_params=PARAMS,
        cost_estimate=cost(24 * rows * half * feats, 20 * half * feats, 2 * half * rows),
        name="gradients",
    )(place[None], turned_w, k0, k1, v0, v1, r0, r1)


def second_kernel(
    place_ref, keep_a, got_a, keep_b, got_b, tied, send_a, kept_a, send_b, kept_b
):
    del tied
    row0 = (place_ref[0] // 2) % 2
    row1 = (place_ref[0] // 4) % 2
    for at in range(3):
        for keep, got, row, send, kept in (
            (keep_a, got_a, row1, send_a, kept_a),
            (keep_b, got_b, row0, send_b, kept_b),
        ):
            send[at] = (keep[at, 1 - row] + got[at, 1 - row].astype(f32)).astype(bf16)
            kept[at] = keep[at, row] + got[at, row].astype(f32)


def second_sum(place, keep_a, got_a, keep_b, got_b, tied):
    shapes = [part.shape[:1] + part.shape[2:] for part in (keep_a, keep_b)]
    return pl.pallas_call(
        second_kernel,
        out_shape=[
            jax.ShapeDtypeStruct(shape, kind) for shape in shapes for kind in (bf16, f32)
        ],
        in_specs=[SMEM] + [VMEM] * 4 + [ANY],
        out_specs=[VMEM] * 4,
        compiler_params=PARAMS,
        cost_estimate=cost(keep_a.size * 2, keep_a.size * 16),
        name="second",
    )(place[None], keep_a, got_a, keep_b, got_b, tied)


def third_kernel(
    place_ref, keep_a, got_a, keep_b, got_b, own_ref, back_ref, send, kept, window_ref
):
    split = keep_a.shape[2]
    rows = keep_a.shape[1] // 2
    far = (place_ref[0] // 8) % 2
    for at in range(3):
        for keep, got, low, high in (
            (keep_a, got_a, 0, split),
            (keep_b, got_b, split, send.shape[2]),
        ):
            total = keep[at] + got[at].astype(f32)
            first, rest = total[:rows], total[rows:]
            send[at, :, low:high] = jnp.where(far == 0, rest, first).astype(bf16)
            kept[at, :, low:high] = jnp.where(far == 0, first, rest)
    early = (place_ref[0] // 2) % 2 == 0

    @pl.when(early)
    def _():
        window_ref[...] = own_ref[...]

    @pl.when(jnp.logical_not(early))
    def _():
        window_ref[...] = back_ref[...]


def third_sum(place, keep_a, got_a, keep_b, got_b, own, back4):
    feats = keep_a.shape[2] + keep_b.shape[2]
    shape = (3, keep_a.shape[1] // 2, feats)
    return pl.pallas_call(
        third_kernel,
        out_shape=[
            jax.ShapeDtypeStruct(shape, bf16),
            jax.ShapeDtypeStruct(shape, f32),
            jax.ShapeDtypeStruct(own.shape, bf16),
        ],
        in_specs=[SMEM] + [VMEM] * 6,
        out_specs=[VMEM] * 3,
        compiler_params=PARAMS,
        cost_estimate=cost(keep_a.size * 2, keep_a.size * 16),
        name="third",
    )(place[None], keep_a, got_a, keep_b, got_b, own, back4)


def renorm_kernel(old_ref, keep, got, fresh):
    for at in range(3):
        old = old_ref[at].astype(f32)
        updated = old + (keep[at] + got[at].astype(f32))
        old_norm = jnp.sqrt(jnp.sum(old * old, axis=1, keepdims=True))
        squares = jnp.sum(updated * updated, axis=1, keepdims=True)
        fresh[at] = (updated * (old_norm / jnp.sqrt(squares + norm_eps))).astype(bf16)


def renormed(old, keep, got):
    return pl.pallas_call(
        renorm_kernel,
        out_shape=jax.ShapeDtypeStruct(old.shape, bf16),
        in_specs=[VMEM] * 3,
        out_specs=VMEM,
        compiler_params=PARAMS,
        cost_estimate=cost(old.size * 8, old.size * 10),
        name="renorm",
    )(old, keep, got)


def fork_kernel(place_ref, fresh, got, own_ref, back2_ref, back4_ref, part_a, part_b, pair):
    split = part_a.shape[2]
    for at in range(3):
        both = jnp.concatenate([fresh[at].astype(f32), got[at].astype(f32)], axis=0).astype(bf16)
        part_a[at] = both[:, :split]
        part_b[at] = both[:, split:]
    even = place_ref[0] % 2 == 0

    @pl.when(even)
    def _():
        pair[0] = own_ref[...]
        pair[1] = back2_ref[...]

    @pl.when(jnp.logical_not(even))
    def _():
        pair[0] = back2_ref[...]
        pair[1] = back4_ref[...]


def forked(place, split, fresh, got, own, back2, back4):
    _, rows, feats = fresh.shape
    return pl.pallas_call(
        fork_kernel,
        out_shape=[
            jax.ShapeDtypeStruct((3, 2 * rows, split), bf16),
            jax.ShapeDtypeStruct((3, 2 * rows, feats - split), bf16),
            jax.ShapeDtypeStruct((2,) + own.shape, bf16),
        ],
        in_specs=[SMEM] + [VMEM] * 5,
        out_specs=[VMEM] * 3,
        compiler_params=PARAMS,
        cost_estimate=cost(0, fresh.size * 8 + own.size * 10),
        name="fork",
    )(place[None], fresh, got, own, back2, back4)


def near_kernel(part_a, got_a, part_b, got_b, near_a, near_b, near):
    rows, split = part_a.shape[1:]
    for at in range(3):
        for part, got, out, low, high in (
            (part_a, got_a, near_a, 0, split),
            (part_b, got_b, near_b, split, near.shape[2]),
        ):
            out[at, :rows] = part[at]
            out[at, rows:] = got[at]
            near[at, :rows, low:high] = part[at]
            near[at, rows:, low:high] = got[at]


def near_rows(part_a, got_a, part_b, got_b):
    rows = 2 * part_a.shape[1]
    widths = [part_a.shape[2], part_b.shape[2]]
    return pl.pallas_call(
        near_kernel,
        out_shape=[
            jax.ShapeDtypeStruct((3, rows, width), bf16) for width in widths + [sum(widths)]
        ],
        in_specs=[VMEM] * 4,
        out_specs=[VMEM] * 3,
        compiler_params=PARAMS,
        cost_estimate=cost(0, part_a.size * 14),
        name="near",
    )(part_a, got_a, part_b, got_b)


def far_kernel(got_a, got_b, attended, far, passed):
    del attended, passed
    split = got_a.shape[2]
    for at in range(3):
        far[at, :, :split] = got_a[at]
        far[at, :, split:] = got_b[at]


def far_rows(got_a, got_b, attended):
    shape = (3, got_a.shape[1], got_a.shape[2] + got_b.shape[2])
    return pl.pallas_call(
        far_kernel,
        out_shape=[
            jax.ShapeDtypeStruct(shape, bf16),
            jax.ShapeDtypeStruct(attended.shape, bf16),
        ],
        in_specs=[VMEM] * 2 + [ANY],
        out_specs=[VMEM, ANY],
        input_output_aliases={2: 1},
        compiler_params=PARAMS,
        cost_estimate=cost(0, got_a.size * 8),
        name="far",
    )(got_a, got_b, attended)


def last_kernel(q_ref, near, far, near_other, far_other, out_ref, hold, *, split):
    quart = near.shape[1] // 2
    for base, first, second in ((0, near, far), (4 * quart, near_other, far_other)):
        for at in range(3):
            hold[at, base : base + 2 * quart, :split] = first[at, :, :split]
            hold[at, base + 2 * quart : base + 4 * quart, :split] = second[at, :, :split]
            hold[at, base : base + quart, split:] = first[at, :quart, split:]
            hold[at, base + quart : base + 2 * quart, split:] = second[at, :quart, split:]
            hold[at, base + 2 * quart : base + 3 * quart, split:] = first[at, quart:, split:]
            hold[at, base + 3 * quart : base + 4 * quart, split:] = second[at, quart:, split:]
    query = q_ref[...]
    gate_q = lax.dot_general(
        query, hold[0], (((1,), (1,)), ((), ())), preferred_element_type=f32
    )
    up_q = lax.dot_general(query, hold[1], (((1,), (1,)), ((), ())), preferred_element_type=f32)
    hidden_q = (gate_q * jax.nn.sigmoid(gate_q) * up_q).astype(bf16)
    out_ref[...] = jnp.dot(hidden_q, hold[2], preferred_element_type=f32).astype(bf16)


def last_step(split, query, near, far, near_other, far_other):
    rows, feats = query.shape
    half = 2 * near.shape[1]
    return pl.pallas_call(
        functools.partial(last_kernel, split=split),
        out_shape=jax.ShapeDtypeStruct((rows, feats), bf16),
        in_specs=[VMEM] * 5,
        out_specs=VMEM,
        scratch_shapes=[pltpu.VMEM((3, 2 * half, feats), bf16)],
        compiler_params=PARAMS,
        cost_estimate=cost(12 * rows * half * feats, 12 * half * feats, 2 * half * rows),
        name="last",
    )(query, near, far, near_other, far_other)


def body(att_q, att_k, att_v, fast_q, fast_k, fast_v, learn_rates, w_gate, w_up, w_down):
    count = lax.axis_size("seq")
    place = lax.axis_index("seq")
    feats, hidden = w_gate.shape
    half = hidden // 2
    quart = half // 4
    units = hidden // count
    split = (feats * 3 // 5) // 128 * 128
    later = [1 << at for at in range(3, count.bit_length() - 1)]
    own_bit = {bit: (place // bit) % 2 for bit in [2, 4] + later}

    rates = learn_rates[None, :]
    other_k, other_v, other_r = swapped(fast_k, 1), swapped(fast_v, 1), swapped(rates, 1)
    turned_w, own = prepared(place, w_gate, w_up, w_down, att_k, att_v)
    back4 = lax.ppermute(own, "seq", [(at, at + 4) for at in range(count - 4)])
    send_a, keep_a, send_b, keep_b = gradients(
        place, turned_w, split, fast_k, other_k, fast_v, other_v, rates, other_r
    )
    send_a, keep_a, send_b, keep_b = second_sum(
        place, keep_a, swapped(send_a, 2), keep_b, swapped(send_b, 4), back4
    )
    send, grads, window = third_sum(
        place, keep_a, swapped(send_a, 4), keep_b, swapped(send_b, 2), own, back4
    )
    back2 = swapped(window, 2)
    got = swapped(send, later[0])
    rest = quart // 2
    start = own_bit[2] * 2 * quart + own_bit[4] * quart + own_bit[later[0]] * rest
    for bit in later[1:]:
        rest //= 2
        grads = (grads + got.astype(f32)).reshape(3, 2, rest, feats)
        send = lax.dynamic_index_in_dim(grads, 1 - own_bit[bit], 1, keepdims=False)
        grads = lax.dynamic_index_in_dim(grads, own_bit[bit], 1, keepdims=False)
        got = swapped(send.astype(bf16), bit)
        start += own_bit[bit] * rest
    old = lax.dynamic_slice_in_dim(turned_w, start, units, 1)
    fresh = renormed(old, grads, got)

    for bit in reversed(later[1:]):
        fresh = jnp.concatenate([fresh, swapped(fresh, bit)], axis=1)
    part_a, part_b, pair = forked(
        place, split, fresh, swapped(fresh, later[0]), own, back2, back4
    )
    pair = swapped(pair, 1)
    near_a, near_b, near = near_rows(part_a, swapped(part_a, 4), part_b, swapped(part_b, 2))
    got_a, got_b = swapped(near_a, 2), swapped(near_b, 4)
    near_other = swapped(near, 1)
    attended = attention(place, att_q, own, back2, back4, pair, near)
    far, attended = far_rows(got_a, got_b, attended)
    fast_out = last_step(split, fast_q, near, far, near_other, swapped(far, 1))
    return (attended, fast_out)


def solution(mesh):
    tokens = P("seq", "head")
    weights = P(None, "head")
    return jax.shard_map(
        body,
        mesh=mesh,
        in_specs=(tokens,) * 6 + (P("seq"),) + (weights,) * 3,
        out_specs=(tokens, tokens),
        check_vma=False,
    )
```

```python
import functools
import math

import jax
import jax.numpy as jnp
from jax import lax
from jax.experimental import pallas as pl
from jax.experimental.pallas import tpu as pltpu
from jax.sharding import PartitionSpec as P

WINDOW = 1024
HEAD_DIM = 128
norm_eps = 1e-06
f32 = jnp.float32
bf16 = jnp.bfloat16

SMEM = pl.BlockSpec(memory_space=pltpu.SMEM)
VMEM = pl.BlockSpec(memory_space=pltpu.VMEM)
HBM = pl.BlockSpec(memory_space=pltpu.HBM)
ANY = pl.BlockSpec(memory_space=pl.ANY)
PARAMS = pltpu.CompilerParams(vmem_limit_bytes=16 << 20)


def swapped(value, bit):
    count = lax.axis_size("seq")
    return lax.ppermute(value, "seq", [(at, at ^ bit) for at in range(count)])


def cost(flops, moved_bytes, exps=0):
    return pl.CostEstimate(flops=flops, bytes_accessed=moved_bytes, transcendentals=exps)


def attention_kernel(
    place_ref, q_ref, own_ref, back2_ref, back4_ref, pair_ref, tied, out_ref
):
    del tied
    rows = q_ref.shape[0]
    place = place_ref[0]
    query = q_ref[...]
    q_at = lax.broadcasted_iota(jnp.int32, (rows, rows), 0)
    k_at = lax.broadcasted_iota(jnp.int32, (rows, rows), 1)
    inside = k_at <= q_at
    factor = HEAD_DIM ** (-0.5) * math.log2(math.e)

    def score(block):
        return lax.dot_general(
            query, block[0], (((1,), (1,)), ((), ())), preferred_element_type=f32
        )

    def attend(masked):
        def seen(part, back):
            return jnp.where(place >= back, part, -1e30) if masked else part

        parts = [
            jnp.where(inside, score(own_ref), seen(score(back4_ref), 4)),
            seen(score(pair_ref.at[0]), 1),
            seen(score(back2_ref), 2),
            seen(score(pair_ref.at[1]), 3),
        ]
        row_max = functools.reduce(
            jnp.maximum, [jnp.max(part, axis=1, keepdims=True) for part in parts]
        )
        shift = row_max * factor
        parts = [jnp.exp2(part * factor - shift) for part in parts]
        total = functools.reduce(jnp.add, [jnp.sum(e, axis=1, keepdims=True) for e in parts])
        scale = 1.0 / total
        parts = [(part * scale).astype(bf16) for part in parts]
        zero = jnp.zeros_like(parts[0])
        parts = [jnp.where(inside, parts[0], zero), jnp.where(inside, zero, parts[0])] + parts[1:]
        blocks = [own_ref, back4_ref, pair_ref.at[0], back2_ref, pair_ref.at[1]]
        result = jnp.zeros(out_ref.shape, f32)
        for part, block in zip(parts, blocks):
            result += jnp.dot(part, block[1], preferred_element_type=f32)
        out_ref[...] = result.astype(bf16)

    pl.when(place >= 4)(lambda: attend(False))
    pl.when(place < 4)(lambda: attend(True))


def attention(place, query, own, back2, back4, pair, tied):
    rows, width = query.shape
    flat = pl.BlockSpec((rows, HEAD_DIM), lambda head: (0, head))
    two = pl.BlockSpec((2, rows, HEAD_DIM), lambda head: (0, 0, head))
    four = pl.BlockSpec((2, 2, rows, HEAD_DIM), lambda head: (0, 0, 0, head))
    return pl.pallas_call(
        attention_kernel,
        out_shape=jax.ShapeDtypeStruct((rows, width), bf16),
        grid=(width // HEAD_DIM,),
        in_specs=[SMEM, flat, two, two, two, four, ANY],
        out_specs=flat,
        compiler_params=PARAMS,
        cost_estimate=cost(20 * rows * rows * width, 24 * rows * width, 5 * rows * rows * 5),
        name="attention",
    )(place[None], query, own, back2, back4, pair, tied)


def prepare_kernel(
    place_ref, gate_ref, up_ref, down_ref, key_ref, val_ref, out_ref, own_ref, wide, hold, sems
):
    hidden = gate_ref.shape[1]
    half = hidden // 2
    window = hold.shape[0]
    core = place_ref[0] % 2
    low = pl.multiple_of(core * (hidden - window), 128)
    off = pl.multiple_of(core * (half - hidden + window), 64)
    copies = [
        pltpu.make_async_copy(ref.at[:, pl.ds(low, window)], wide.at[at], sems.at[at])
        for at, ref in enumerate((gate_ref, up_ref, down_ref))
    ] + [
        pltpu.make_async_copy(ref, own_ref.at[at], sems.at[3 + at])
        for at, ref in enumerate((key_ref, val_ref))
    ]
    for copy in copies:
        copy.start()
    for at in range(3):
        copies[at].wait()
        hold[...] = wide[at].T
        out_ref[at] = hold[pl.ds(off, half), :]
    for copy in copies[3:]:
        copy.wait()


def prepared(place, w_gate, w_up, w_down, att_k, att_v):
    feats, hidden = w_gate.shape
    half = hidden // 2
    window = -(-half // 128) * 128
    return pl.pallas_call(
        prepare_kernel,
        out_shape=[
            jax.ShapeDtypeStruct((3, half, feats), bf16),
            jax.ShapeDtypeStruct((2,) + att_k.shape, bf16),
        ],
        in_specs=[SMEM] + [HBM] * 5,
        out_specs=[VMEM] * 2,
        scratch_shapes=[
            pltpu.VMEM((3, feats, window), bf16),
            pltpu.VMEM((window, feats), bf16),
            pltpu.SemaphoreType.DMA((5,)),
        ],
        compiler_params=pltpu.CompilerParams(vmem_limit_bytes=60 << 20),
        cost_estimate=cost(0, 9 * feats * hidden),
        name="prepare",
    )(place[None], w_gate, w_up, w_down, att_k, att_v)


def grad_kernel(
    place_ref, turned_ref, k0_ref, k1_ref, v0_ref, v1_ref, r0_ref, r1_ref,
    send_a, keep_a, send_b, keep_b, hold,
):
    def project(at, rows):
        return lax.dot_general(
            turned_ref[at], rows, (((1,), (1,)), ((), ())), preferred_element_type=f32
        )

    terms = []
    for keys, vals, rate_ref in ((k0_ref, v0_ref, r0_ref), (k1_ref, v1_ref, r1_ref)):
        rate = rate_ref[...]
        pre_gate = project(0, keys[...])
        pre_up = project(1, keys[...])
        back = rate * project(2, vals[...])
        sigmoid_v = jax.nn.sigmoid(pre_gate)
        silu = pre_gate * sigmoid_v
        slope = sigmoid_v * (1.0 + pre_gate * (1.0 - sigmoid_v))
        terms.append(
            (
                (back * pre_up * slope).astype(bf16),
                (back * silu).astype(bf16),
                (rate * silu * pre_up).astype(bf16),
            )
        )
    sources = ((k0_ref, k1_ref), (k0_ref, k1_ref), (v0_ref, v1_ref))
    for at in range(3):
        hold[at] = jnp.dot(
            terms[0][at], sources[at][0][...], preferred_element_type=f32
        ) + jnp.dot(terms[1][at], sources[at][1][...], preferred_element_type=f32)
    rows_a, rows_b = send_a.shape[2], send_b.shape[2]
    quart = rows_a + rows_b
    row0 = (place_ref[0] // 2) % 2
    row1 = (place_ref[0] // 4) % 2

    def piece(at, bit0, bit1, low, rows):
        first = pl.multiple_of((2 * bit0 + bit1) * quart + low, 8)
        return hold[at, pl.ds(first, rows), :]

    for at in range(3):
        for other in range(2):
            send_a[at, other] = piece(at, 1 - row0, other, 0, rows_a).astype(bf16)
            keep_a[at, other] = piece(at, row0, other, 0, rows_a)
            send_b[at, other] = piece(at, other, 1 - row1, rows_a, rows_b).astype(bf16)
            keep_b[at, other] = piece(at, other, row1, rows_a, rows_b)


def gradients(place, turned_w, rows_a, k0, k1, v0, v1, r0, r1):
    _, half, feats = turned_w.shape
    rows = k0.shape[0]
    return pl.pallas_call(
        grad_kernel,
        out_shape=[
            jax.ShapeDtypeStruct((3, 2, part, feats), kind)
            for part in (rows_a, half // 4 - rows_a)
            for kind in (bf16, f32)
        ],
        in_specs=[SMEM] + [VMEM] * 7,
        out_specs=[VMEM] * 4,
        scratch_shapes=[pltpu.VMEM((3, half, feats), f32)],
        compiler_params=PARAMS,
        cost_estimate=cost(24 * rows * half * feats, 20 * half * feats, 2 * half * rows),
        name="gradients",
    )(place[None], turned_w, k0, k1, v0, v1, r0, r1)


def second_kernel(
    place_ref, keep_a, got_a, keep_b, got_b, tied, send_a, kept_a, send_b, kept_b
):
    del tied
    row0 = (place_ref[0] // 2) % 2
    row1 = (place_ref[0] // 4) % 2
    for at in range(3):
        for keep, got, row, send, kept in (
            (keep_a, got_a, row1, send_a, kept_a),
            (keep_b, got_b, row0, send_b, kept_b),
        ):
            send[at] = (keep[at, 1 - row] + got[at, 1 - row].astype(f32)).astype(bf16)
            kept[at] = keep[at, row] + got[at, row].astype(f32)


def second_sum(place, keep_a, got_a, keep_b, got_b, tied):
    shapes = [part.shape[:1] + part.shape[2:] for part in (keep_a, keep_b)]
    return pl.pallas_call(
        second_kernel,
        out_shape=[
            jax.ShapeDtypeStruct(shape, kind) for shape in shapes for kind in (bf16, f32)
        ],
        in_specs=[SMEM] + [VMEM] * 4 + [ANY],
        out_specs=[VMEM] * 4,
        compiler_params=PARAMS,
        cost_estimate=cost(keep_a.size * 2, keep_a.size * 16),
        name="second",
    )(place[None], keep_a, got_a, keep_b, got_b, tied)


def third_kernel(
    place_ref, keep_a, got_a, keep_b, got_b, own_ref, back_ref, total, send, window_ref
):
    rows = keep_a.shape[1]
    for at in range(3):
        for keep, got, low, high in (
            (keep_a, got_a, 0, rows),
            (keep_b, got_b, rows, total.shape[1]),
        ):
            summed = keep[at] + got[at].astype(f32)
            total[at, low:high] = summed
            send[at, low:high] = summed.astype(bf16)
    early = (place_ref[0] // 2) % 2 == 0

    @pl.when(early)
    def _():
        window_ref[...] = own_ref[...]

    @pl.when(jnp.logical_not(early))
    def _():
        window_ref[...] = back_ref[...]


def third_sum(place, keep_a, got_a, keep_b, got_b, own, back4):
    shape = (3, keep_a.shape[1] + keep_b.shape[1], keep_a.shape[2])
    return pl.pallas_call(
        third_kernel,
        out_shape=[
            jax.ShapeDtypeStruct(shape, f32),
            jax.ShapeDtypeStruct(shape, bf16),
            jax.ShapeDtypeStruct(own.shape, bf16),
        ],
        in_specs=[SMEM] + [VMEM] * 6,
        out_specs=[VMEM] * 3,
        compiler_params=PARAMS,
        cost_estimate=cost(keep_a.size * 2, keep_a.size * 16),
        name="third",
    )(place[None], keep_a, got_a, keep_b, got_b, own, back4)


def renorm_kernel(
    place_ref, old_ref, keep, got, own_ref, back2_ref, back4_ref, part_a, part_b, pair
):
    rows = part_a.shape[1]
    for at in range(3):
        old = old_ref[at].astype(f32)
        updated = old + (keep[at] + got[at].astype(f32))
        old_norm = jnp.sqrt(jnp.sum(old * old, axis=1, keepdims=True))
        squares = jnp.sum(updated * updated, axis=1, keepdims=True)
        fresh = updated * (old_norm / jnp.sqrt(squares + norm_eps))
        part_a[at] = fresh[:rows].astype(bf16)
        part_b[at] = fresh[rows:].astype(bf16)
    even = place_ref[0] % 2 == 0

    @pl.when(even)
    def _():
        pair[0] = own_ref[...]
        pair[1] = back2_ref[...]

    @pl.when(jnp.logical_not(even))
    def _():
        pair[0] = back2_ref[...]
        pair[1] = back4_ref[...]


def renormed(place, old, keep, got, own, back2, back4):
    part = jax.ShapeDtypeStruct((3, old.shape[1] // 2, old.shape[2]), bf16)
    return pl.pallas_call(
        renorm_kernel,
        out_shape=[part, part, jax.ShapeDtypeStruct((2,) + own.shape, bf16)],
        in_specs=[SMEM] + [VMEM] * 6,
        out_specs=[VMEM] * 3,
        compiler_params=PARAMS,
        cost_estimate=cost(old.size * 8, old.size * 10),
        name="renorm",
    )(place[None], old, keep, got, own, back2, back4)


def near_kernel(part_a, got_a, part_b, got_b, near_a, near_b, near):
    rows = part_a.shape[1]
    for at in range(3):
        for part, got, out, low in (
            (part_a, got_a, near_a, 0),
            (part_b, got_b, near_b, 2 * rows),
        ):
            both = jnp.concatenate([part[at].astype(f32), got[at].astype(f32)], axis=0)
            out[at] = both.astype(bf16)
            near[at, low : low + 2 * rows] = both.astype(bf16)


def near_rows(part_a, got_a, part_b, got_b):
    rows, feats = part_a.shape[1:]
    return pl.pallas_call(
        near_kernel,
        out_shape=[
            jax.ShapeDtypeStruct((3, size * rows, feats), bf16) for size in (2, 2, 4)
        ],
        in_specs=[VMEM] * 4,
        out_specs=[VMEM] * 3,
        compiler_params=PARAMS,
        cost_estimate=cost(0, part_a.size * 14),
        name="near",
    )(part_a, got_a, part_b, got_b)


def fast_output(query, hold):
    gate_q = lax.dot_general(
        query, hold[0], (((1,), (1,)), ((), ())), preferred_element_type=f32
    )
    up_q = lax.dot_general(query, hold[1], (((1,), (1,)), ((), ())), preferred_element_type=f32)
    hidden_q = (gate_q * jax.nn.sigmoid(gate_q) * up_q).astype(bf16)
    return jnp.dot(hidden_q, hold[2], preferred_element_type=f32)


def first_kernel(q_ref, near, near_other, out_ref, hold):
    rows = near.shape[1]
    hold[:, :rows] = near[...]
    hold[:, rows:] = near_other[...]
    out_ref[...] = fast_output(q_ref[...], hold)


def first_half(query, near, near_other):
    rows, feats = query.shape
    units = 2 * near.shape[1]
    return pl.pallas_call(
        first_kernel,
        out_shape=jax.ShapeDtypeStruct((rows, feats), f32),
        in_specs=[VMEM] * 3,
        out_specs=VMEM,
        scratch_shapes=[pltpu.VMEM((3, units, feats), bf16)],
        compiler_params=PARAMS,
        cost_estimate=cost(6 * rows * units * feats, 12 * units * feats, units * rows),
        name="first_half",
    )(query, near, near_other)


def far_kernel(got_a, got_b, attended, half_out, far, passed, passed_half):
    del attended, half_out, passed, passed_half
    rows = got_a.shape[1]
    far[:, :rows] = got_a[...]
    far[:, rows:] = got_b[...]


def far_rows(got_a, got_b, attended, half_out):
    shape = (3, 2 * got_a.shape[1], got_a.shape[2])
    return pl.pallas_call(
        far_kernel,
        out_shape=[
            jax.ShapeDtypeStruct(shape, bf16),
            jax.ShapeDtypeStruct(attended.shape, bf16),
            jax.ShapeDtypeStruct(half_out.shape, f32),
        ],
        in_specs=[VMEM] * 2 + [ANY] * 2,
        out_specs=[VMEM, ANY, ANY],
        input_output_aliases={2: 1, 3: 2},
        compiler_params=PARAMS,
        cost_estimate=cost(0, got_a.size * 8),
        name="far",
    )(got_a, got_b, attended, half_out)


def last_kernel(q_ref, half_out, far, far_other, out_ref, hold):
    rows = far.shape[1]
    hold[:, :rows] = far[...]
    hold[:, rows:] = far_other[...]
    out_ref[...] = (half_out[...] + fast_output(q_ref[...], hold)).astype(bf16)


def last_half(query, half_out, far, far_other):
    rows, feats = query.shape
    units = 2 * far.shape[1]
    return pl.pallas_call(
        last_kernel,
        out_shape=jax.ShapeDtypeStruct((rows, feats), bf16),
        in_specs=[VMEM] * 4,
        out_specs=VMEM,
        scratch_shapes=[pltpu.VMEM((3, units, feats), bf16)],
        compiler_params=PARAMS,
        cost_estimate=cost(6 * rows * units * feats, 12 * units * feats, units * rows),
        name="last_half",
    )(query, half_out, far, far_other)


def body(att_q, att_k, att_v, fast_q, fast_k, fast_v, learn_rates, w_gate, w_up, w_down):
    count = lax.axis_size("seq")
    place = lax.axis_index("seq")
    feats, hidden = w_gate.shape
    quart = hidden // 8
    rows_a = quart * 3 // 5
    later = [1 << at for at in range(3, count.bit_length() - 1)]
    own_bit = {bit: (place // bit) % 2 for bit in [2, 4] + later}

    other_k, other_v = swapped(fast_k, 1), swapped(fast_v, 1)
    other_r = swapped(learn_rates, 1)
    turned_w, own = prepared(place, w_gate, w_up, w_down, att_k, att_v)
    back4 = lax.ppermute(own, "seq", [(at, (at + 4) % count) for at in range(count)])
    send_a, keep_a, send_b, keep_b = gradients(
        place, turned_w, rows_a, fast_k, other_k, fast_v, other_v,
        learn_rates[None, :], other_r[None, :],
    )
    send_a, keep_a, send_b, keep_b = second_sum(
        place, keep_a, swapped(send_a, 2), keep_b, swapped(send_b, 4), back4
    )
    grads, send, window = third_sum(
        place, keep_a, swapped(send_a, 4), keep_b, swapped(send_b, 2), own, back4
    )
    rest = quart
    start = own_bit[2] * 2 * quart + own_bit[4] * quart
    for bit in later[:-1]:
        rest //= 2
        grads = grads.reshape(3, 2, rest, feats)
        send = lax.dynamic_index_in_dim(grads, 1 - own_bit[bit], 1, keepdims=False)
        grads = lax.dynamic_index_in_dim(grads, own_bit[bit], 1, keepdims=False)
        grads = grads + swapped(send.astype(bf16), bit).astype(f32)
        send = grads.astype(bf16)
        start += own_bit[bit] * rest
    got = swapped(send, later[-1])
    back2 = swapped(window, 2)
    old = lax.dynamic_slice_in_dim(turned_w, start, rest, 1)
    part_a, part_b, pair = renormed(place, old, grads, got, own, back2, back4)
    pair = swapped(pair, 1)

    for bit in reversed(later[:-1]):
        part_a = jnp.concatenate([part_a, swapped(part_a, bit)], axis=1)
        part_b = jnp.concatenate([part_b, swapped(part_b, bit)], axis=1)
    near_a, near_b, near = near_rows(part_a, swapped(part_a, 4), part_b, swapped(part_b, 2))
    got_a, got_b = swapped(near_a, 2), swapped(near_b, 4)
    near_other = swapped(near, 1)
    attended = attention(place, att_q, own, back2, back4, pair, near)
    half_out = first_half(fast_q, near, near_other)
    far, attended, half_out = far_rows(got_a, got_b, attended, half_out)
    fast_out = last_half(fast_q, half_out, far, swapped(far, 1))
    return (attended, fast_out)


def solution(mesh):
    tokens = P("seq", "head")
    weights = P(None, "head")
    return jax.shard_map(
        body,
        mesh=mesh,
        in_specs=(tokens,) * 6 + (P("seq"),) + (weights,) * 3,
        out_specs=(tokens, tokens),
        check_vma=False,
    )
```

```python
import functools
import math

import jax
import jax.numpy as jnp
from jax import lax
from jax.experimental import pallas as pl
from jax.experimental.pallas import tpu as pltpu
from jax.sharding import PartitionSpec as P

WINDOW = 1024
HEAD_DIM = 128
norm_eps = 1e-06
f32 = jnp.float32
bf16 = jnp.bfloat16

SMEM = pl.BlockSpec(memory_space=pltpu.SMEM)
VMEM = pl.BlockSpec(memory_space=pltpu.VMEM)
HBM = pl.BlockSpec(memory_space=pltpu.HBM)
ANY = pl.BlockSpec(memory_space=pl.ANY)
PARAMS = pltpu.CompilerParams(vmem_limit_bytes=16 << 20)


def swapped(value, bit):
    count = lax.axis_size("seq")
    return lax.ppermute(value, "seq", [(at, at ^ bit) for at in range(count)])


def cost(flops, moved_bytes, exps=0):
    return pl.CostEstimate(flops=flops, bytes_accessed=moved_bytes, transcendentals=exps)


def attention_kernel(place_ref, q_ref, own_ref, back2_ref, back4_ref, pair_ref, out_ref):
    rows, width = q_ref.shape
    place = place_ref[0]
    factor = HEAD_DIM ** (-0.5) * math.log2(math.e)
    q_at = lax.broadcasted_iota(jnp.int32, (rows, rows), 0)
    k_at = lax.broadcasted_iota(jnp.int32, (rows, rows), 1)
    inside = k_at <= q_at

    def attend(cols, masked):
        query = q_ref[:, cols]

        def score(ref, *at):
            return lax.dot_general(
                query, ref[(*at, 0, slice(None), cols)], (((1,), (1,)), ((), ())),
                preferred_element_type=f32,
            )

        def seen(part, back):
            return jnp.where(place >= back, part, -1e30) if masked else part

        parts = [
            jnp.where(inside, score(own_ref), seen(score(back4_ref), 4)),
            seen(score(pair_ref, 0), 1),
            seen(score(back2_ref), 2),
            seen(score(pair_ref, 1), 3),
        ]
        row_max = functools.reduce(
            jnp.maximum, [jnp.max(part, axis=1, keepdims=True) for part in parts]
        )
        shift = row_max * factor
        parts = [jnp.exp2(part * factor - shift) for part in parts]
        total = functools.reduce(jnp.add, [jnp.sum(e, axis=1, keepdims=True) for e in parts])
        scale = 1.0 / total
        parts = [(part * scale).astype(bf16) for part in parts]
        zero = jnp.zeros_like(parts[0])
        parts = [jnp.where(inside, parts[0], zero), jnp.where(inside, zero, parts[0])] + parts[1:]
        result = jnp.zeros((rows, HEAD_DIM), f32)
        for part, ref, at in zip(
            parts, (own_ref, back4_ref, pair_ref, back2_ref, pair_ref), ((), (), (0,), (), (1,))
        ):
            result += jnp.dot(
                part, ref[(*at, 1, slice(None), cols)], preferred_element_type=f32
            )
        out_ref[:, cols] = result.astype(bf16)

    def every(masked):
        for head in range(width // HEAD_DIM):
            attend(slice(head * HEAD_DIM, (head + 1) * HEAD_DIM), masked)

    pl.when(place >= 4)(lambda: every(False))
    pl.when(place < 4)(lambda: every(True))


def attention(place, query, own, back2, back4, pair):
    rows, width = query.shape
    return pl.pallas_call(
        attention_kernel,
        out_shape=jax.ShapeDtypeStruct((rows, width), bf16),
        in_specs=[SMEM] + [VMEM] * 5,
        out_specs=VMEM,
        compiler_params=PARAMS,
        cost_estimate=cost(20 * rows * rows * width, 24 * rows * width, 5 * rows * rows * 5),
        name="attention",
    )(place[None], query, own, back2, back4, pair)


def prepare_kernel(place_ref, gate_ref, up_ref, down_ref, out_ref, wide, hold, sems):
    feats, hidden = gate_ref.shape
    half = hidden // 2
    window = hold.shape[0]
    core = place_ref[0] % 2
    low = pl.multiple_of(core * (hidden - window), 128)
    off = pl.multiple_of(core * (half - hidden + window), 64)
    pieces = sems.shape[1]
    step = feats // pieces
    copies = [
        [
            pltpu.make_async_copy(
                ref.at[pl.ds(piece * step, step), pl.ds(low, window)],
                wide.at[at, pl.ds(piece * step, step), :],
                sems.at[at, piece],
            )
            for piece in range(pieces)
        ]
        for at, ref in enumerate((gate_ref, up_ref, down_ref))
    ]
    for group in copies:
        for copy in group:
            copy.start()
    for at, group in enumerate(copies):
        for copy in group:
            copy.wait()
        hold[...] = wide[at].T
        out_ref[at] = hold[pl.ds(off, half), :]


def prepared(place, w_gate, w_up, w_down):
    feats, hidden = w_gate.shape
    half = hidden // 2
    window = -(-half // 128) * 128
    return pl.pallas_call(
        prepare_kernel,
        out_shape=jax.ShapeDtypeStruct((3, half, feats), bf16),
        in_specs=[SMEM] + [HBM] * 3,
        out_specs=VMEM,
        scratch_shapes=[
            pltpu.VMEM((3, feats, window), bf16),
            pltpu.VMEM((window, feats), bf16),
            pltpu.SemaphoreType.DMA((3, feats // 128)),
        ],
        compiler_params=pltpu.CompilerParams(vmem_limit_bytes=60 << 20),
        cost_estimate=cost(0, 9 * feats * hidden),
        name="prepare",
    )(place[None], w_gate, w_up, w_down)


def grad_kernel(
    place_ref, turned_ref, k0_ref, k1_ref, v0_ref, v1_ref, r0_ref, r1_ref, key_ref, val_ref,
    send, keep, own_ref, hold,
):
    own_ref[0] = key_ref[...]
    own_ref[1] = val_ref[...]

    def project(at, rows):
        return lax.dot_general(
            turned_ref[at], rows, (((1,), (1,)), ((), ())), preferred_element_type=f32
        )

    terms = []
    for keys, vals, rate_ref in ((k0_ref, v0_ref, r0_ref), (k1_ref, v1_ref, r1_ref)):
        rate = rate_ref[...]
        pre_gate = project(0, keys[...])
        pre_up = project(1, keys[...])
        back = rate * project(2, vals[...])
        sigmoid_v = jax.nn.sigmoid(pre_gate)
        silu = pre_gate * sigmoid_v
        slope = sigmoid_v * (1.0 + pre_gate * (1.0 - sigmoid_v))
        terms.append(
            (
                (back * pre_up * slope).astype(bf16),
                (back * silu).astype(bf16),
                (rate * silu * pre_up).astype(bf16),
            )
        )
    sources = ((k0_ref, k1_ref), (k0_ref, k1_ref), (v0_ref, v1_ref))
    for at in range(3):
        hold[at] = jnp.dot(
            terms[0][at], sources[at][0][...], preferred_element_type=f32
        ) + jnp.dot(terms[1][at], sources[at][1][...], preferred_element_type=f32)
    quart = send.shape[2]
    row = (place_ref[0] // 2) % 2
    for at in range(3):
        for other in range(2):
            there = pl.multiple_of((2 * (1 - row) + other) * quart, 8)
            here = pl.multiple_of((2 * row + other) * quart, 8)
            send[at, other] = hold[at, pl.ds(there, quart), :].astype(bf16)
            keep[at, other] = hold[at, pl.ds(here, quart), :]


def gradients(place, turned_w, k0, k1, v0, v1, r0, r1, att_k, att_v):
    _, half, feats = turned_w.shape
    rows = k0.shape[0]
    shape = (3, 2, half // 4, feats)
    return pl.pallas_call(
        grad_kernel,
        out_shape=[
            jax.ShapeDtypeStruct(shape, bf16),
            jax.ShapeDtypeStruct(shape, f32),
            jax.ShapeDtypeStruct((2,) + att_k.shape, bf16),
        ],
        in_specs=[SMEM] + [VMEM] * 9,
        out_specs=[VMEM] * 3,
        scratch_shapes=[pltpu.VMEM((3, half, feats), f32)],
        compiler_params=PARAMS,
        cost_estimate=cost(24 * rows * half * feats, 20 * half * feats, 2 * half * rows),
        name="gradients",
    )(place[None], turned_w, k0, k1, v0, v1, r0, r1, att_k, att_v)


def second_kernel(place_ref, keep, got, send, kept):
    row = (place_ref[0] // 4) % 2
    for at in range(3):
        send[at] = (keep[at, 1 - row] + got[at, 1 - row].astype(f32)).astype(bf16)
        kept[at] = keep[at, row] + got[at, row].astype(f32)


def second_sum(place, keep, got):
    shape = keep.shape[:1] + keep.shape[2:]
    return pl.pallas_call(
        second_kernel,
        out_shape=[jax.ShapeDtypeStruct(shape, bf16), jax.ShapeDtypeStruct(shape, f32)],
        in_specs=[SMEM] + [VMEM] * 2,
        out_specs=[VMEM] * 2,
        compiler_params=PARAMS,
        cost_estimate=cost(keep.size * 2, keep.size * 8),
        name="second",
    )(place[None], keep, got)


def third_kernel(keep, got, tied, total, send):
    del tied
    for at in range(3):
        summed = keep[at] + got[at].astype(f32)
        total[at] = summed
        send[at] = summed.astype(bf16)


def third_sum(keep, got, tied):
    return pl.pallas_call(
        third_kernel,
        out_shape=[
            jax.ShapeDtypeStruct(keep.shape, f32),
            jax.ShapeDtypeStruct(keep.shape, bf16),
        ],
        in_specs=[VMEM] * 2 + [ANY],
        out_specs=[VMEM] * 2,
        compiler_params=PARAMS,
        cost_estimate=cost(keep.size * 2, keep.size * 8),
        name="third",
    )(keep, got, tied)


def window_kernel(place_ref, own_ref, back_ref, tied, out_ref):
    del tied
    early = (place_ref[0] // 2) % 2 == 0

    @pl.when(early)
    def _():
        out_ref[...] = own_ref[...]

    @pl.when(jnp.logical_not(early))
    def _():
        out_ref[...] = back_ref[...]


def window_step(place, own, back4, tied):
    return pl.pallas_call(
        window_kernel,
        out_shape=jax.ShapeDtypeStruct(own.shape, bf16),
        in_specs=[SMEM] + [VMEM] * 2 + [ANY],
        out_specs=VMEM,
        compiler_params=PARAMS,
        cost_estimate=cost(0, own.size * 4),
        name="window",
    )(place[None], own, back4, tied)


def renorm_kernel(old_ref, keep, got, part_a, part_b):
    rows = part_a.shape[1]
    for at in range(3):
        old = old_ref[at].astype(f32)
        updated = old + (keep[at] + got[at].astype(f32))
        old_norm = jnp.sqrt(jnp.sum(old * old, axis=1, keepdims=True))
        squares = jnp.sum(updated * updated, axis=1, keepdims=True)
        fresh = updated * (old_norm / jnp.sqrt(squares + norm_eps))
        part_a[at] = fresh[:rows].astype(bf16)
        part_b[at] = fresh[rows:].astype(bf16)


def renormed(old, keep, got):
    part = jax.ShapeDtypeStruct((3, old.shape[1] // 2, old.shape[2]), bf16)
    return pl.pallas_call(
        renorm_kernel,
        out_shape=[part, part],
        in_specs=[VMEM] * 3,
        out_specs=[VMEM] * 2,
        compiler_params=PARAMS,
        cost_estimate=cost(old.size * 8, old.size * 10),
        name="renorm",
    )(old, keep, got)


def near_kernel(
    place_ref, part_a, got_a, part_b, got_b, own_ref, back2_ref, back4_ref,
    near_a, near_b, near, pair,
):
    rows = part_a.shape[1]
    for at in range(3):
        for part, got, out, low in (
            (part_a, got_a, near_a, 0),
            (part_b, got_b, near_b, 2 * rows),
        ):
            both = jnp.concatenate([part[at].astype(f32), got[at].astype(f32)], axis=0)
            out[at] = both.astype(bf16)
            near[at, low : low + 2 * rows] = both.astype(bf16)
    even = place_ref[0] % 2 == 0

    @pl.when(even)
    def _():
        pair[0] = own_ref[...]
        pair[1] = back2_ref[...]

    @pl.when(jnp.logical_not(even))
    def _():
        pair[0] = back2_ref[...]
        pair[1] = back4_ref[...]


def near_rows(place, part_a, got_a, part_b, got_b, own, back2, back4):
    rows, feats = part_a.shape[1:]
    return pl.pallas_call(
        near_kernel,
        out_shape=[
            jax.ShapeDtypeStruct((3, size * rows, feats), bf16) for size in (2, 2, 4)
        ]
        + [jax.ShapeDtypeStruct((2,) + own.shape, bf16)],
        in_specs=[SMEM] + [VMEM] * 7,
        out_specs=[VMEM] * 4,
        compiler_params=PARAMS,
        cost_estimate=cost(0, part_a.size * 14 + own.size * 8),
        name="near",
    )(place[None], part_a, got_a, part_b, got_b, own, back2, back4)


def fast_output(query, hold):
    gate_q = lax.dot_general(
        query, hold[0], (((1,), (1,)), ((), ())), preferred_element_type=f32
    )
    up_q = lax.dot_general(query, hold[1], (((1,), (1,)), ((), ())), preferred_element_type=f32)
    hidden_q = (gate_q * jax.nn.sigmoid(gate_q) * up_q).astype(bf16)
    return jnp.dot(hidden_q, hold[2], preferred_element_type=f32)


def first_kernel(q_ref, near, near_other, out_ref, hold):
    rows = near.shape[1]
    hold[:, :rows] = near[...]
    hold[:, rows:] = near_other[...]
    out_ref[...] = fast_output(q_ref[...], hold)


def first_half(query, near, near_other):
    rows, feats = query.shape
    units = 2 * near.shape[1]
    return pl.pallas_call(
        first_kernel,
        out_shape=jax.ShapeDtypeStruct((rows, feats), f32),
        in_specs=[VMEM] * 3,
        out_specs=VMEM,
        scratch_shapes=[pltpu.VMEM((3, units, feats), bf16)],
        compiler_params=PARAMS,
        cost_estimate=cost(6 * rows * units * feats, 12 * units * feats, units * rows),
        name="first_half",
    )(query, near, near_other)


def far_kernel(got_a, got_b, attended, half_out, far, passed, passed_half):
    del attended, half_out, passed, passed_half
    rows = got_a.shape[1]
    far[:, :rows] = got_a[...]
    far[:, rows:] = got_b[...]


def far_rows(got_a, got_b, attended, half_out):
    shape = (3, 2 * got_a.shape[1], got_a.shape[2])
    return pl.pallas_call(
        far_kernel,
        out_shape=[
            jax.ShapeDtypeStruct(shape, bf16),
            jax.ShapeDtypeStruct(attended.shape, bf16),
            jax.ShapeDtypeStruct(half_out.shape, f32),
        ],
        in_specs=[VMEM] * 2 + [ANY] * 2,
        out_specs=[VMEM, ANY, ANY],
        input_output_aliases={2: 1, 3: 2},
        compiler_params=PARAMS,
        cost_estimate=cost(0, got_a.size * 8),
        name="far",
    )(got_a, got_b, attended, half_out)


def last_kernel(q_ref, half_out, far, far_other, out_ref, hold):
    rows = far.shape[1]
    hold[:, :rows] = far[...]
    hold[:, rows:] = far_other[...]
    out_ref[...] = (half_out[...] + fast_output(q_ref[...], hold)).astype(bf16)


def last_half(query, half_out, far, far_other):
    rows, feats = query.shape
    units = 2 * far.shape[1]
    return pl.pallas_call(
        last_kernel,
        out_shape=jax.ShapeDtypeStruct((rows, feats), bf16),
        in_specs=[VMEM] * 4,
        out_specs=VMEM,
        scratch_shapes=[pltpu.VMEM((3, units, feats), bf16)],
        compiler_params=PARAMS,
        cost_estimate=cost(6 * rows * units * feats, 12 * units * feats, units * rows),
        name="last_half",
    )(query, half_out, far, far_other)


def body(att_q, att_k, att_v, fast_q, fast_k, fast_v, learn_rates, w_gate, w_up, w_down):
    count = lax.axis_size("seq")
    place = lax.axis_index("seq")
    feats, hidden = w_gate.shape
    quart = hidden // 8
    later = [1 << at for at in range(3, count.bit_length() - 1)]
    own_bit = {bit: (place // bit) % 2 for bit in [2, 4] + later}

    other_k, other_v = swapped(fast_k, 1), swapped(fast_v, 1)
    other_r = swapped(learn_rates, 1)
    turned_w = prepared(place, w_gate, w_up, w_down)
    send, keep, own = gradients(
        place, turned_w, fast_k, other_k, fast_v, other_v,
        learn_rates[None, :], other_r[None, :], att_k, att_v,
    )
    back4 = lax.ppermute(own, "seq", [(at, (at + 4) % count) for at in range(count)])
    send, keep = second_sum(place, keep, swapped(send, 2))
    window = window_step(place, own, back4, send)
    back2 = swapped(window, 2)
    grads, send = third_sum(keep, swapped(send, 4), window)
    rest = quart
    start = own_bit[2] * 2 * quart + own_bit[4] * quart
    for bit in later[:-1]:
        rest //= 2
        grads = grads.reshape(3, 2, rest, feats)
        send = lax.dynamic_index_in_dim(grads, 1 - own_bit[bit], 1, keepdims=False)
        grads = lax.dynamic_index_in_dim(grads, own_bit[bit], 1, keepdims=False)
        grads = grads + swapped(send.astype(bf16), bit).astype(f32)
        send = grads.astype(bf16)
        start += own_bit[bit] * rest
    got = swapped(send, later[-1])
    old = lax.dynamic_slice_in_dim(turned_w, start, rest, 1)
    part_a, part_b = renormed(old, grads, got)

    for bit in reversed(later[:-1]):
        part_a = jnp.concatenate([part_a, swapped(part_a, bit)], axis=1)
        part_b = jnp.concatenate([part_b, swapped(part_b, bit)], axis=1)
    near_a, near_b, near, pair = near_rows(
        place, part_a, swapped(part_a, 4), part_b, swapped(part_b, 2), own, back2, back4
    )
    got_a, got_b = swapped(near_a, 2), swapped(near_b, 4)
    near_other = swapped(near, 1)
    pair = swapped(pair, 1)
    attended = attention(place, att_q, own, back2, back4, pair)
    half_out = first_half(fast_q, near, near_other)
    far, attended, half_out = far_rows(got_a, got_b, attended, half_out)
    fast_out = last_half(fast_q, half_out, far, swapped(far, 1))
    return (attended, fast_out)


def solution(mesh):
    tokens = P("seq", "head")
    weights = P(None, "head")
    return jax.shard_map(
        body,
        mesh=mesh,
        in_specs=(tokens,) * 6 + (P("seq"),) + (weights,) * 3,
        out_specs=(tokens, tokens),
        check_vma=False,
    )
```

```python
import functools
import math

import jax
import jax.numpy as jnp
from jax import lax
from jax.experimental import pallas as pl
from jax.experimental.pallas import tpu as pltpu
from jax.sharding import PartitionSpec as P

WINDOW = 1024
HEAD_DIM = 128
norm_eps = 1e-06
f32 = jnp.float32
bf16 = jnp.bfloat16

SMEM = pl.BlockSpec(memory_space=pltpu.SMEM)
VMEM = pl.BlockSpec(memory_space=pltpu.VMEM)
ANY = pl.BlockSpec(memory_space=pl.ANY)
PARAMS = pltpu.CompilerParams(vmem_limit_bytes=16 << 20)


def swapped(value, bit):
    count = lax.axis_size("seq")
    return lax.ppermute(value, "seq", [(at, at ^ bit) for at in range(count)])


def kernel_call(kernel, operands, tied=(), in_specs=None, name=None, **rest):
    given = len(operands)

    def run(*refs):
        kernel(*refs[:given], *refs[given + len(tied) :])

    return pl.pallas_call(
        run, in_specs=list(in_specs) + [ANY] * len(tied), name=name, **rest
    )(*operands, *tied)


def cost(flops, moved_bytes, exps=0):
    return pl.CostEstimate(flops=flops, bytes_accessed=moved_bytes, transcendentals=exps)


def attention_kernel(place_ref, q_ref, own_ref, back2_ref, back4_ref, pair_ref, out_ref):
    rows, width = q_ref.shape
    place = place_ref[0]
    factor = HEAD_DIM ** (-0.5) * math.log2(math.e)
    q_at = lax.broadcasted_iota(jnp.int32, (rows, rows), 0)
    k_at = lax.broadcasted_iota(jnp.int32, (rows, rows), 1)
    inside = k_at <= q_at

    def attend(cols, masked):
        query = q_ref[:, cols]

        def score(ref, *at):
            return lax.dot_general(
                query, ref[(*at, 0, slice(None), cols)], (((1,), (1,)), ((), ())),
                preferred_element_type=f32,
            )

        def seen(part, back):
            return jnp.where(place >= back, part, -1e30) if masked else part

        parts = [
            jnp.where(inside, score(own_ref), seen(score(back4_ref), 4)),
            seen(score(pair_ref, 0), 1),
            seen(score(back2_ref), 2),
            seen(score(pair_ref, 1), 3),
        ]
        row_max = functools.reduce(
            jnp.maximum, [jnp.max(part, axis=1, keepdims=True) for part in parts]
        )
        shift = row_max * factor
        parts = [jnp.exp2(part * factor - shift) for part in parts]
        total = functools.reduce(jnp.add, [jnp.sum(e, axis=1, keepdims=True) for e in parts])
        scale = 1.0 / total
        parts = [(part * scale).astype(bf16) for part in parts]
        zero = jnp.zeros_like(parts[0])
        parts = [jnp.where(inside, parts[0], zero), jnp.where(inside, zero, parts[0])] + parts[1:]
        result = jnp.zeros((rows, HEAD_DIM), f32)
        for part, ref, at in zip(
            parts, (own_ref, back4_ref, pair_ref, back2_ref, pair_ref), ((), (), (0,), (), (1,))
        ):
            result += jnp.dot(
                part, ref[(*at, 1, slice(None), cols)], preferred_element_type=f32
            )
        out_ref[:, cols] = result.astype(bf16)

    def every(masked):
        for head in range(width // HEAD_DIM):
            attend(slice(head * HEAD_DIM, (head + 1) * HEAD_DIM), masked)

    pl.when(place >= 4)(lambda: every(False))
    pl.when(place < 4)(lambda: every(True))


def attention(place, query, own, back2, back4, pair, *tied):
    rows, width = query.shape
    return kernel_call(
        attention_kernel,
        (place[None], query, own, back2, back4, pair),
        tied,
        out_shape=jax.ShapeDtypeStruct((rows, width), bf16),
        in_specs=[SMEM] + [VMEM] * 5,
        out_specs=VMEM,
        compiler_params=PARAMS,
        cost_estimate=cost(20 * rows * rows * width, 24 * rows * width, 5 * rows * rows * 5),
        name="attention",
    )


def prepare_kernel(place_ref, gate_ref, up_ref, down_ref, out_ref, hold):
    hidden = gate_ref.shape[1]
    half = hidden // 2
    window = hold.shape[0]
    core = place_ref[0] % 2
    low = pl.multiple_of(core * (hidden - window), 128)
    off = pl.multiple_of(core * (half - hidden + window), 64)
    for at, ref in enumerate((gate_ref, up_ref, down_ref)):
        hold[...] = ref[:, pl.ds(low, window)].T
        out_ref[at] = hold[pl.ds(off, half), :]


def prepared(place, w_gate, w_up, w_down):
    feats, hidden = w_gate.shape
    half = hidden // 2
    window = -(-half // 128) * 128
    return pl.pallas_call(
        prepare_kernel,
        out_shape=jax.ShapeDtypeStruct((3, half, feats), bf16),
        in_specs=[SMEM] + [VMEM] * 3,
        out_specs=VMEM,
        scratch_shapes=[pltpu.VMEM((window, feats), bf16)],
        compiler_params=PARAMS,
        cost_estimate=cost(0, 9 * feats * hidden),
        name="prepare",
    )(place[None], w_gate, w_up, w_down)


def pack_kernel(key_ref, val_ref, own_ref):
    own_ref[0] = key_ref[...]
    own_ref[1] = val_ref[...]


def packed(att_k, att_v, *tied):
    return kernel_call(
        pack_kernel,
        (att_k, att_v),
        tied,
        out_shape=jax.ShapeDtypeStruct((2,) + att_k.shape, bf16),
        in_specs=[VMEM] * 2,
        out_specs=VMEM,
        compiler_params=PARAMS,
        cost_estimate=cost(0, 0),
        name="pack",
    )


def grad_kernel(
    place_ref, turned_ref, k0_ref, k1_ref, v0_ref, v1_ref, r0_ref, r1_ref, *outs_and_hold
):
    sends, keeps, hold = outs_and_hold[:3], outs_and_hold[3:6], outs_and_hold[6]

    def project(at, rows):
        return lax.dot_general(
            turned_ref[at], rows, (((1,), (1,)), ((), ())), preferred_element_type=f32
        )

    terms = []
    for keys, vals, rate_ref in ((k0_ref, v0_ref, r0_ref), (k1_ref, v1_ref, r1_ref)):
        rate = rate_ref[...]
        pre_gate = project(0, keys[...])
        pre_up = project(1, keys[...])
        back = rate * project(2, vals[...])
        sigmoid_v = jax.nn.sigmoid(pre_gate)
        silu = pre_gate * sigmoid_v
        slope = sigmoid_v * (1.0 + pre_gate * (1.0 - sigmoid_v))
        terms.append(
            (
                (back * pre_up * slope).astype(bf16),
                (back * silu).astype(bf16),
                (rate * silu * pre_up).astype(bf16),
            )
        )
    sources = ((k0_ref, k1_ref), (k0_ref, k1_ref), (v0_ref, v1_ref))
    for at in range(3):
        hold[at] = jnp.dot(
            terms[0][at], sources[at][0][...], preferred_element_type=f32
        ) + jnp.dot(terms[1][at], sources[at][1][...], preferred_element_type=f32)
    quart = sends[0].shape[1]
    row = (place_ref[0] // 2) % 2
    for at in range(3):
        for other in range(2):
            there = pl.multiple_of((2 * (1 - row) + other) * quart, 8)
            here = pl.multiple_of((2 * row + other) * quart, 8)
            sends[at][other] = hold[at, pl.ds(there, quart), :].astype(bf16)
            keeps[at][other] = hold[at, pl.ds(here, quart), :]


def gradients(place, turned_w, k0, k1, v0, v1, r0, r1):
    _, half, feats = turned_w.shape
    rows = k0.shape[0]
    shape = (2, half // 4, feats)
    outs = pl.pallas_call(
        grad_kernel,
        out_shape=[jax.ShapeDtypeStruct(shape, kind) for kind in (bf16, f32) for _ in range(3)],
        in_specs=[SMEM] + [VMEM] * 7,
        out_specs=[VMEM] * 6,
        scratch_shapes=[pltpu.VMEM((3, half, feats), f32)],
        compiler_params=PARAMS,
        cost_estimate=cost(24 * rows * half * feats, 20 * half * feats, 2 * half * rows),
        name="gradients",
    )(place[None], turned_w, k0, k1, v0, v1, r0, r1)
    return outs[:3], outs[3:]


def second_kernel(place_ref, keep, got, send, kept):
    row = (place_ref[0] // 4) % 2
    send[...] = (keep[1 - row] + got[1 - row].astype(f32)).astype(bf16)
    kept[...] = keep[row] + got[row].astype(f32)


def second_sum(place, keep, got, *tied):
    shape = keep.shape[1:]
    return kernel_call(
        second_kernel,
        (place[None], keep, got),
        tied,
        out_shape=[jax.ShapeDtypeStruct(shape, bf16), jax.ShapeDtypeStruct(shape, f32)],
        in_specs=[SMEM] + [VMEM] * 2,
        out_specs=[VMEM] * 2,
        compiler_params=PARAMS,
        cost_estimate=cost(0, 0),
        name="second",
    )


def third_kernel(keep, got, total, send):
    summed = keep[...] + got[...].astype(f32)
    total[...] = summed
    send[...] = summed.astype(bf16)


def third_sum(keep, got, *tied):
    return kernel_call(
        third_kernel,
        (keep, got),
        tied,
        out_shape=[
            jax.ShapeDtypeStruct(keep.shape, f32),
            jax.ShapeDtypeStruct(keep.shape, bf16),
        ],
        in_specs=[VMEM] * 2,
        out_specs=[VMEM] * 2,
        compiler_params=PARAMS,
        cost_estimate=cost(0, 0),
        name="third",
    )


def window_kernel(place_ref, own_ref, back_ref, out_ref):
    early = (place_ref[0] // 2) % 2 == 0

    @pl.when(early)
    def _():
        out_ref[...] = own_ref[...]

    @pl.when(jnp.logical_not(early))
    def _():
        out_ref[...] = back_ref[...]


def window_step(place, own, back4, *tied):
    return kernel_call(
        window_kernel,
        (place[None], own, back4),
        tied,
        out_shape=jax.ShapeDtypeStruct(own.shape, bf16),
        in_specs=[SMEM] + [VMEM] * 2,
        out_specs=VMEM,
        compiler_params=PARAMS,
        cost_estimate=cost(0, 0),
        name="window",
    )


def pair_kernel(place_ref, own_ref, back2_ref, back4_ref, pair):
    even = place_ref[0] % 2 == 0

    @pl.when(even)
    def _():
        pair[0] = own_ref[...]
        pair[1] = back2_ref[...]

    @pl.when(jnp.logical_not(even))
    def _():
        pair[0] = back2_ref[...]
        pair[1] = back4_ref[...]


def pair_step(place, own, back2, back4, *tied):
    return kernel_call(
        pair_kernel,
        (place[None], own, back2, back4),
        tied,
        out_shape=jax.ShapeDtypeStruct((2,) + own.shape, bf16),
        in_specs=[SMEM] + [VMEM] * 3,
        out_specs=VMEM,
        compiler_params=PARAMS,
        cost_estimate=cost(0, 0),
        name="pair",
    )


def renorm_kernel(at, old_ref, keep, got, fresh):
    old = old_ref[at].astype(f32)
    updated = old + (keep[...] + got[...].astype(f32))
    old_norm = jnp.sqrt(jnp.sum(old * old, axis=1, keepdims=True))
    squares = jnp.sum(updated * updated, axis=1, keepdims=True)
    fresh[...] = (updated * (old_norm / jnp.sqrt(squares + norm_eps))).astype(bf16)


def renormed(at, old, keep, got, *tied):
    return kernel_call(
        functools.partial(renorm_kernel, at),
        (old, keep, got),
        tied,
        out_shape=jax.ShapeDtypeStruct(keep.shape, bf16),
        in_specs=[VMEM] * 3,
        out_specs=VMEM,
        compiler_params=PARAMS,
        cost_estimate=cost(0, 0),
        name="renorm",
    )


def join_kernel(order, *refs):
    out = refs[-1]
    low = 0
    for which, first, rows in order:
        out[low : low + rows] = refs[which][first : first + rows]
        low += rows


def joined(order, parts, *tied):
    rows = sum(piece[2] for piece in order)
    return kernel_call(
        functools.partial(join_kernel, order),
        parts,
        tied,
        out_shape=jax.ShapeDtypeStruct((rows, parts[0].shape[1]), bf16),
        in_specs=[VMEM] * len(parts),
        out_specs=VMEM,
        compiler_params=PARAMS,
        cost_estimate=cost(0, 0),
        name="join",
    )


def hidden_kernel(q_ref, gate0, gate1, up0, up1, out_ref):
    query = q_ref[...]
    units = gate0.shape[0]

    def project(rows):
        return lax.dot_general(
            query, rows, (((1,), (1,)), ((), ())), preferred_element_type=f32
        )

    for at, (gate, up) in enumerate(((gate0, up0), (gate1, up1))):
        gate_q = project(gate[...])
        up_q = project(up[...])
        out_ref[at] = (gate_q * jax.nn.sigmoid(gate_q) * up_q).astype(bf16)


def hidden_step(query, gate0, gate1, up0, up1, *tied):
    rows, feats = query.shape
    units = gate0.shape[0]
    return kernel_call(
        hidden_kernel,
        (query, gate0, gate1, up0, up1),
        tied,
        out_shape=jax.ShapeDtypeStruct((2, rows, units), bf16),
        in_specs=[VMEM] * 5,
        out_specs=VMEM,
        compiler_params=PARAMS,
        cost_estimate=cost(8 * rows * units * feats, 8 * units * feats, 2 * units * rows),
        name="hidden",
    )


def gate_keeper(*refs):
    del refs


def after(value, *others):
    return pl.pallas_call(
        gate_keeper,
        out_shape=[jax.ShapeDtypeStruct(part.shape, part.dtype) for part in (value, *others)],
        in_specs=[ANY] * (1 + len(others)),
        out_specs=[ANY] * (1 + len(others)),
        input_output_aliases={at: at for at in range(1 + len(others))},
        compiler_params=PARAMS,
        cost_estimate=cost(0, 0),
        name="after",
    )(value, *others)


def last_kernel(hidden_ref, near, far, near_other, far_other, out_ref, hold):
    rows = near.shape[0]
    total = None
    for at, parts in enumerate(((near, far), (near_other, far_other))):
        hold[at, :rows] = parts[0][...]
        hold[at, rows:] = parts[1][...]
        part = jnp.dot(hidden_ref[at], hold[at], preferred_element_type=f32)
        total = part if total is None else total + part
    out_ref[...] = total.astype(bf16)


def last_step(hidden_q, near, far, near_other, far_other):
    rows = hidden_q.shape[1]
    units, feats = near.shape
    return pl.pallas_call(
        last_kernel,
        out_shape=jax.ShapeDtypeStruct((rows, feats), bf16),
        in_specs=[VMEM] * 5,
        out_specs=VMEM,
        scratch_shapes=[pltpu.VMEM((2, 2 * units, feats), bf16)],
        compiler_params=PARAMS,
        cost_estimate=cost(8 * rows * units * feats, 12 * units * feats),
        name="last",
    )(hidden_q, near, far, near_other, far_other)


def scattered(total, send, later, own_bit):
    for bit in later[:-1]:
        total = total.reshape(2, -1, total.shape[-1])
        send = lax.dynamic_index_in_dim(total, 1 - own_bit[bit], 0, keepdims=False)
        total = lax.dynamic_index_in_dim(total, own_bit[bit], 0, keepdims=False)
        total = total + swapped(send.astype(bf16), bit).astype(f32)
        send = total.astype(bf16)
    return total, send


def gathered(part, later):
    for bit in reversed(later[:-1]):
        part = jnp.concatenate([part, swapped(part, bit)], axis=0)
    return part


def body(att_q, att_k, att_v, fast_q, fast_k, fast_v, learn_rates, w_gate, w_up, w_down):
    count = lax.axis_size("seq")
    place = lax.axis_index("seq")
    feats, hidden = w_gate.shape
    quart = hidden // 8
    later = [1 << at for at in range(3, count.bit_length() - 1)]
    own_bit = {bit: (place // bit) % 2 for bit in [2, 4] + later}
    rest = quart
    start = own_bit[2] * 2 * quart + own_bit[4] * quart
    for bit in later[:-1]:
        rest //= 2
        start += own_bit[bit] * rest

    other_k, other_v = swapped(fast_k, 1), swapped(fast_v, 1)
    other_r = swapped(learn_rates, 1)
    turned_w = prepared(place, w_gate, w_up, w_down)
    own = packed(att_k, att_v, turned_w)
    back4 = lax.ppermute(own, "seq", [(at, (at + 4) % count) for at in range(count)])
    sends, keeps = gradients(
        place, turned_w, fast_k, other_k, fast_v, other_v,
        learn_rates[None, :], other_r[None, :],
    )
    old = lax.dynamic_slice_in_dim(turned_w, start, rest, 1)

    first = [swapped(send, 2) for send in sends]
    send_g, keep_g = second_sum(place, keeps[0], first[0])
    got_g = swapped(send_g, 4)
    send_u, keep_u = second_sum(place, keeps[1], first[1], send_g)
    got_u = swapped(send_u, 4)
    grad_g, send = third_sum(keep_g, got_g, send_u)
    grad_g, send = scattered(grad_g, send, later, own_bit)
    last_g = swapped(send, later[-1])
    send_d, keep_d = second_sum(place, keeps[2], first[2], send)
    got_d = swapped(send_d, 4)
    window = window_step(place, own, back4, send_d)
    back2 = swapped(window, 2)
    grad_u, send = third_sum(keep_u, got_u, window)
    grad_u, send = scattered(grad_u, send, later, own_bit)
    last_u = swapped(send, later[-1])
    grad_d, send = third_sum(keep_d, got_d, send)
    grad_d, send = scattered(grad_d, send, later, own_bit)
    last_d = swapped(send, later[-1])

    one, two = quart, 2 * quart
    both, halves = ((0, 0, one), (1, 0, one)), ((0, 0, two), (1, 0, two))
    gate = gathered(renormed(0, old, grad_g, last_g, send), later)
    gate_z = swapped(gate, 4)
    up = gathered(renormed(1, old, grad_u, last_u, gate), later)
    up_y = swapped(up, 2)
    gate = joined(both, (gate, gate_z), up)
    gate_y = swapped(gate, 2)
    down = gathered(renormed(2, old, grad_d, last_d, gate), later)
    down_z = swapped(down, 4)
    up = joined(both, (up, up_y), down)
    up_z = swapped(up, 4)
    pair = swapped(pair_step(place, own, back2, back4, up), 1)
    gate = joined(halves, (gate, gate_y), up)
    near = joined(both, (down, down_z), gate)
    far, near_other = swapped(near, 2), swapped(near, 1)
    up = joined(
        ((0, 0, one), (1, 0, one), (0, one, one), (1, one, one)), (up, up_z), near
    )
    gate_other, up_other = swapped(gate, 1), swapped(up, 1)
    attended = attention(place, att_q, own, back2, back4, pair, up)
    hidden_q = hidden_step(fast_q, gate, gate_other, up, up_other)
    far, attended, hidden_q = after(far, attended, hidden_q)
    fast_out = last_step(hidden_q, near, far, near_other, swapped(far, 1))
    return (attended, fast_out)


def solution(mesh):
    tokens = P("seq", "head")
    weights = P(None, "head")
    return jax.shard_map(
        body,
        mesh=mesh,
        in_specs=(tokens,) * 6 + (P("seq"),) + (weights,) * 3,
        out_specs=(tokens, tokens),
        check_vma=False,
    )
```

```python
import functools
import math

import jax
import jax.numpy as jnp
from jax import lax
from jax.experimental import pallas as pl
from jax.experimental.pallas import tpu as pltpu
from jax.sharding import PartitionSpec as P

WINDOW = 1024
HEAD_DIM = 128
norm_eps = 1e-06
f32 = jnp.float32
bf16 = jnp.bfloat16

SMEM = pl.BlockSpec(memory_space=pltpu.SMEM)
VMEM = pl.BlockSpec(memory_space=pltpu.VMEM)
ANY = pl.BlockSpec(memory_space=pl.ANY)
PARAMS = pltpu.CompilerParams(vmem_limit_bytes=16 << 20)


def swapped(value, bit):
    count = lax.axis_size("seq")
    return lax.ppermute(value, "seq", [(at, at ^ bit) for at in range(count)])


def kernel_call(kernel, operands, tied=(), in_specs=None, name=None, **rest):
    given = len(operands)

    def run(*refs):
        kernel(*refs[:given], *refs[given + len(tied) :])

    return pl.pallas_call(
        run, in_specs=list(in_specs) + [ANY] * len(tied), name=name, **rest
    )(*operands, *tied)


def cost(flops, moved_bytes, exps=0):
    return pl.CostEstimate(flops=flops, bytes_accessed=moved_bytes, transcendentals=exps)


def attention_kernel(heads, place_ref, q_ref, own_ref, back2_ref, back4_ref, pair_ref, out_ref):
    rows = q_ref.shape[0]
    place = place_ref[0]
    factor = HEAD_DIM ** (-0.5) * math.log2(math.e)
    q_at = lax.broadcasted_iota(jnp.int32, (rows, rows), 0)
    k_at = lax.broadcasted_iota(jnp.int32, (rows, rows), 1)
    inside = k_at <= q_at

    def attend(head, masked):
        cols = slice(head * HEAD_DIM, (head + 1) * HEAD_DIM)
        query = q_ref[:, cols]

        def score(ref, *at):
            return lax.dot_general(
                query, ref[(*at, 0, slice(None), cols)], (((1,), (1,)), ((), ())),
                preferred_element_type=f32,
            )

        def seen(part, back):
            return jnp.where(place >= back, part, -1e30) if masked else part

        parts = [
            jnp.where(inside, score(own_ref), seen(score(back4_ref), 4)),
            seen(score(pair_ref, 0), 1),
            seen(score(back2_ref), 2),
            seen(score(pair_ref, 1), 3),
        ]
        row_max = functools.reduce(
            jnp.maximum, [jnp.max(part, axis=1, keepdims=True) for part in parts]
        )
        shift = row_max * factor
        parts = [jnp.exp2(part * factor - shift) for part in parts]
        total = functools.reduce(jnp.add, [jnp.sum(e, axis=1, keepdims=True) for e in parts])
        scale = 1.0 / total
        parts = [(part * scale).astype(bf16) for part in parts]
        zero = jnp.zeros_like(parts[0])
        parts = [jnp.where(inside, parts[0], zero), jnp.where(inside, zero, parts[0])] + parts[1:]
        result = jnp.zeros((rows, HEAD_DIM), f32)
        for part, ref, at in zip(
            parts, (own_ref, back4_ref, pair_ref, back2_ref, pair_ref), ((), (), (0,), (), (1,))
        ):
            result += jnp.dot(
                part, ref[(*at, 1, slice(None), cols)], preferred_element_type=f32
            )
        out = slice((head - heads[0]) * HEAD_DIM, (head + 1 - heads[0]) * HEAD_DIM)
        out_ref[:, out] = result.astype(bf16)

    def every(masked):
        for head in heads:
            attend(head, masked)

    pl.when(place >= 4)(lambda: every(False))
    pl.when(place < 4)(lambda: every(True))


def attention(heads, place, query, own, back2, back4, pair, *tied):
    rows = query.shape[0]
    width = len(heads) * HEAD_DIM
    return kernel_call(
        functools.partial(attention_kernel, heads),
        (place[None], query, own, back2, back4, pair),
        tied,
        out_shape=jax.ShapeDtypeStruct((rows, width), bf16),
        in_specs=[SMEM] + [VMEM] * 5,
        out_specs=VMEM,
        compiler_params=PARAMS,
        cost_estimate=cost(20 * rows * rows * width, 24 * rows * width, 5 * rows * rows * 5),
        name="attention",
    )


def prepare_kernel(place_ref, gate_ref, up_ref, down_ref, out_ref, hold):
    hidden = gate_ref.shape[1]
    half = hidden // 2
    window = hold.shape[0]
    core = place_ref[0] % 2
    low = pl.multiple_of(core * (hidden - window), 128)
    off = pl.multiple_of(core * (half - hidden + window), 64)
    for at, ref in enumerate((gate_ref, up_ref, down_ref)):
        hold[...] = ref[:, pl.ds(low, window)].T
        out_ref[at] = hold[pl.ds(off, half), :]


def prepared(place, w_gate, w_up, w_down):
    feats, hidden = w_gate.shape
    half = hidden // 2
    window = -(-half // 128) * 128
    return pl.pallas_call(
        prepare_kernel,
        out_shape=jax.ShapeDtypeStruct((3, half, feats), bf16),
        in_specs=[SMEM] + [VMEM] * 3,
        out_specs=VMEM,
        scratch_shapes=[pltpu.VMEM((window, feats), bf16)],
        compiler_params=PARAMS,
        cost_estimate=cost(0, 9 * feats * hidden),
        name="prepare",
    )(place[None], w_gate, w_up, w_down)


def pack_kernel(key_ref, val_ref, own_ref):
    own_ref[0] = key_ref[...]
    own_ref[1] = val_ref[...]


def packed(att_k, att_v, *tied):
    return kernel_call(
        pack_kernel,
        (att_k, att_v),
        tied,
        out_shape=jax.ShapeDtypeStruct((2,) + att_k.shape, bf16),
        in_specs=[VMEM] * 2,
        out_specs=VMEM,
        compiler_params=PARAMS,
        cost_estimate=cost(0, 0),
        name="pack",
    )


def grad_kernel(
    place_ref, turned_ref, k0_ref, v0_ref, r0_ref, r1_ref, k1_any, v1_any,
    send_p, send_q, keep_p, keep_q, hold, k1_ref, v1_ref, sems,
):
    copies = [
        pltpu.make_async_copy(k1_any, k1_ref, sems.at[0]),
        pltpu.make_async_copy(v1_any, v1_ref, sems.at[1]),
    ]
    for copy in copies:
        copy.start()

    def project(at, rows):
        return lax.dot_general(
            turned_ref[at], rows, (((1,), (1,)), ((), ())), preferred_element_type=f32
        )

    terms = []
    for keys, vals, rate_ref in ((k0_ref, v0_ref, r0_ref), (k1_ref, v1_ref, r1_ref)):
        if rate_ref is r1_ref:
            for copy in copies:
                copy.wait()
        rate = rate_ref[...]
        pre_gate = project(0, keys[...])
        pre_up = project(1, keys[...])
        back = rate * project(2, vals[...])
        sigmoid_v = jax.nn.sigmoid(pre_gate)
        silu = pre_gate * sigmoid_v
        slope = sigmoid_v * (1.0 + pre_gate * (1.0 - sigmoid_v))
        terms.append(
            (
                (back * pre_up * slope).astype(bf16),
                (back * silu).astype(bf16),
                (rate * silu * pre_up).astype(bf16),
            )
        )
    sources = ((k0_ref, k1_ref), (k0_ref, k1_ref), (v0_ref, v1_ref))
    for at in range(3):
        hold[at] = jnp.dot(
            terms[0][at], sources[at][0][...], preferred_element_type=f32
        ) + jnp.dot(terms[1][at], sources[at][1][...], preferred_element_type=f32)
    quart = send_p.shape[2]
    row = (place_ref[0] // 2) % 2
    for at in range(3):
        send, keep = (send_p.at[at], keep_p.at[at]) if at < 2 else (send_q.at[0], keep_q.at[0])
        for other in range(2):
            there = pl.multiple_of((2 * (1 - row) + other) * quart, 8)
            here = pl.multiple_of((2 * row + other) * quart, 8)
            send[other] = hold[at, pl.ds(there, quart), :].astype(bf16)
            keep[other] = hold[at, pl.ds(here, quart), :]


def gradients(place, turned_w, k0, k1, v0, v1, r0, r1, *tied):
    _, half, feats = turned_w.shape
    rows = k0.shape[0]
    return kernel_call(
        grad_kernel,
        (place[None], turned_w, k0, v0, r0, r1, k1, v1),
        tied,
        out_shape=[
            jax.ShapeDtypeStruct((count, 2, half // 4, feats), kind)
            for kind in (bf16, f32)
            for count in (2, 1)
        ],
        in_specs=[SMEM] + [VMEM] * 5 + [ANY] * 2,
        out_specs=[VMEM] * 4,
        scratch_shapes=[
            pltpu.VMEM((3, half, feats), f32),
            pltpu.VMEM(k0.shape, bf16),
            pltpu.VMEM(k0.shape, bf16),
            pltpu.SemaphoreType.DMA((2,)),
        ],
        compiler_params=PARAMS,
        cost_estimate=cost(24 * rows * half * feats, 20 * half * feats, 2 * half * rows),
        name="gradients",
    )


def stage(kernel, operands, outs, name, *tied):
    return kernel_call(
        kernel,
        (operands[0][None], *operands[1:]),
        tied,
        out_shape=[jax.ShapeDtypeStruct(shape, kind) for shape, kind in outs],
        in_specs=[SMEM] + [VMEM] * (len(operands) - 1),
        out_specs=[VMEM] * len(outs),
        compiler_params=PARAMS,
        cost_estimate=cost(0, 0),
        name=name,
    )


def halve(place_ref, keep, got, send, kept):
    row = (place_ref[0] // 4) % 2
    for at in range(keep.shape[0]):
        send[at] = (keep[at, 1 - row] + got[at, 1 - row].astype(f32)).astype(bf16)
        kept[at] = keep[at, row] + got[at, row].astype(f32)


def add(keep, got, total, send):
    for at in range(keep.shape[0]):
        summed = keep[at] + got[at].astype(f32)
        total[at] = summed
        send[at] = summed.astype(bf16)


def renorm(first, old_ref, keep, got, part_a, part_b):
    rows = part_a.shape[1]
    for at in range(keep.shape[0]):
        old = old_ref[first + at].astype(f32)
        updated = old + (keep[at] + got[at].astype(f32))
        old_norm = jnp.sqrt(jnp.sum(old * old, axis=1, keepdims=True))
        squares = jnp.sum(updated * updated, axis=1, keepdims=True)
        fresh = updated * (old_norm / jnp.sqrt(squares + norm_eps))
        part_a[at] = fresh[:rows].astype(bf16)
        part_b[at] = fresh[rows:].astype(bf16)


def join(at, part, got, *outs):
    rows = part.shape[1]
    both = jnp.concatenate([part[at].astype(f32), got[at].astype(f32)], axis=0).astype(bf16)
    for out, low in outs:
        out[at, low : low + 2 * rows] = both


def third_kernel(place_ref, keep_p, got_p, keep_q, got_q, total_p, send_p, send_q, kept_q):
    add(keep_p, got_p, total_p, send_p)
    halve(place_ref, keep_q, got_q, send_q, kept_q)


def fourth_kernel(
    place_ref, old_ref, keep_p, got_p, keep_q, got_q, p_a, p_b, total_q, send_q
):
    add(keep_q, got_q, total_q, send_q)
    renorm(0, old_ref, keep_p, got_p, p_a, p_b)


def fifth_kernel(
    place_ref, old_ref, p_a, got_a, p_b, got_b, keep_q, got_q, near_a, near_b, q_a, q_b
):
    for at in range(2):
        join(at, p_a, got_a, (near_a, 0))
        join(at, p_b, got_b, (near_b, 0))
    renorm(2, old_ref, keep_q, got_q, q_a, q_b)


def sixth_kernel(
    place_ref, near_a, far_a, near_b, far_b, q_a, got_qa, q_b, got_qb,
    whole, near_qa, near_qb, near_q,
):
    rows = near_a.shape[1]
    join(0, q_a, got_qa, (near_qa, 0), (near_q, 0))
    join(0, q_b, got_qb, (near_qb, 0), (near_q, rows))
    for at in range(2):
        for which, part in enumerate((near_a, far_a, near_b, far_b)):
            whole[at, which * rows : (which + 1) * rows] = part[at]


def far_kernel(got_a, got_b, *rest):
    far = rest[-1]
    rows = got_a.shape[1]
    far[:, :rows] = got_a[...]
    far[:, rows:] = got_b[...]


def far_rows(got_a, got_b, *tied):
    return kernel_call(
        far_kernel,
        (got_a, got_b),
        tied,
        out_shape=jax.ShapeDtypeStruct((1, 2 * got_a.shape[1], got_a.shape[2]), bf16),
        in_specs=[VMEM] * 2,
        out_specs=VMEM,
        compiler_params=PARAMS,
        cost_estimate=cost(0, 0),
        name="far",
    )


def hidden_kernel(q_ref, own_ref, other_ref, out_ref):
    query = q_ref[...]

    def project(rows):
        return lax.dot_general(
            query, rows, (((1,), (1,)), ((), ())), preferred_element_type=f32
        )

    for at, ref in enumerate((own_ref, other_ref)):
        gate_q = project(ref[0])
        up_q = project(ref[1])
        out_ref[at] = (gate_q * jax.nn.sigmoid(gate_q) * up_q).astype(bf16)


def hidden_step(query, own, other, *tied):
    rows, feats = query.shape
    units = own.shape[1]
    return kernel_call(
        hidden_kernel,
        (query, own, other),
        tied,
        out_shape=jax.ShapeDtypeStruct((2, rows, units), bf16),
        in_specs=[VMEM] * 3,
        out_specs=VMEM,
        compiler_params=PARAMS,
        cost_estimate=cost(8 * rows * units * feats, 8 * units * feats, 2 * units * rows),
        name="hidden",
    )


def last_kernel(hidden_ref, near, far, near_other, far_other, out_ref, hold):
    rows = near.shape[1] // 2
    total = None
    for at, (first, second) in enumerate(((near, far), (near_other, far_other))):
        for which in range(2):
            here = slice(which * rows, (which + 1) * rows)
            hold[at, 2 * which * rows : (2 * which + 1) * rows] = first[0, here]
            hold[at, (2 * which + 1) * rows : (2 * which + 2) * rows] = second[0, here]
        part = jnp.dot(hidden_ref[at], hold[at], preferred_element_type=f32)
        total = part if total is None else total + part
    out_ref[...] = total.astype(bf16)


def last_step(hidden_q, near, far, near_other, far_other):
    rows = hidden_q.shape[1]
    _, units, feats = near.shape
    return pl.pallas_call(
        last_kernel,
        out_shape=jax.ShapeDtypeStruct((rows, feats), bf16),
        in_specs=[VMEM] * 5,
        out_specs=VMEM,
        scratch_shapes=[pltpu.VMEM((2, 2 * units, feats), bf16)],
        compiler_params=PARAMS,
        cost_estimate=cost(8 * rows * units * feats, 12 * units * feats),
        name="last",
    )(hidden_q, near, far, near_other, far_other)


def window_kernel(place_ref, own_ref, back_ref, out_ref):
    early = (place_ref[0] // 2) % 2 == 0

    @pl.when(early)
    def _():
        out_ref[...] = own_ref[...]

    @pl.when(jnp.logical_not(early))
    def _():
        out_ref[...] = back_ref[...]


def window_step(place, own, back4, *tied):
    return kernel_call(
        window_kernel,
        (place[None], own, back4),
        tied,
        out_shape=jax.ShapeDtypeStruct(own.shape, bf16),
        in_specs=[SMEM] + [VMEM] * 2,
        out_specs=VMEM,
        compiler_params=PARAMS,
        cost_estimate=cost(0, 0),
        name="window",
    )


def pair_kernel(place_ref, own_ref, back2_ref, back4_ref, pair):
    even = place_ref[0] % 2 == 0

    @pl.when(even)
    def _():
        pair[0] = own_ref[...]
        pair[1] = back2_ref[...]

    @pl.when(jnp.logical_not(even))
    def _():
        pair[0] = back2_ref[...]
        pair[1] = back4_ref[...]


def pair_step(place, own, back2, back4, *tied):
    return kernel_call(
        pair_kernel,
        (place[None], own, back2, back4),
        tied,
        out_shape=jax.ShapeDtypeStruct((2,) + own.shape, bf16),
        in_specs=[SMEM] + [VMEM] * 3,
        out_specs=VMEM,
        compiler_params=PARAMS,
        cost_estimate=cost(0, 0),
        name="pair",
    )


def scattered(total, send, later, own_bit):
    for bit in later[:-1]:
        total = total.reshape(total.shape[0], 2, -1, total.shape[-1])
        send = lax.dynamic_index_in_dim(total, 1 - own_bit[bit], 1, keepdims=False)
        total = lax.dynamic_index_in_dim(total, own_bit[bit], 1, keepdims=False)
        total = total + swapped(send.astype(bf16), bit).astype(f32)
        send = total.astype(bf16)
    return total, send


def gathered(part, later):
    for bit in reversed(later[:-1]):
        part = jnp.concatenate([part, swapped(part, bit)], axis=1)
    return part


def body(att_q, att_k, att_v, fast_q, fast_k, fast_v, learn_rates, w_gate, w_up, w_down):
    count = lax.axis_size("seq")
    place = lax.axis_index("seq")
    feats, hidden = w_gate.shape
    heads = range(att_q.shape[1] // HEAD_DIM)
    early_heads = 3 * len(heads) // 5
    quart = hidden // 8
    later = [1 << at for at in range(3, count.bit_length() - 1)]
    own_bit = {bit: (place // bit) % 2 for bit in [2, 4] + later}
    rest = quart
    start = own_bit[2] * 2 * quart + own_bit[4] * quart
    for bit in later[:-1]:
        rest //= 2
        start += own_bit[bit] * rest

    def shape(rows, matrices):
        return (matrices, rows, feats)

    other_k, other_v = swapped(fast_k, 1), swapped(fast_v, 1)
    other_r = swapped(learn_rates, 1)
    turned_w = prepared(place, w_gate, w_up, w_down)
    own = packed(att_k, att_v, turned_w, other_r)
    back4 = lax.ppermute(own, "seq", [(at, (at + 4) % count) for at in range(count)])
    send_p, send_q, keep_p, keep_q = gradients(
        place, turned_w, fast_k, other_k, fast_v, other_v,
        learn_rates[None, :], other_r[None, :], own,
    )
    old = lax.dynamic_slice_in_dim(turned_w, start, rest, 1)

    got_p, got_q = swapped(send_p, 2), swapped(send_q, 2)
    send_p, keep_p = stage(
        halve, (place, keep_p, got_p), [(shape(quart, 2), bf16), (shape(quart, 2), f32)], "second"
    )
    window = window_step(place, own, back4, send_p)
    back2 = swapped(window, 2)
    total_p, send_p, send_q, keep_q = stage(
        third_kernel,
        (place, keep_p, swapped(send_p, 4), keep_q, got_q),
        [
            (shape(quart, 2), f32), (shape(quart, 2), bf16),
            (shape(quart, 1), bf16), (shape(quart, 1), f32),
        ],
        "third",
        window,
    )
    total_p, send_p = scattered(total_p, send_p, later, own_bit)
    p_a, p_b, total_q, send_q = stage(
        fourth_kernel,
        (place, old, total_p, swapped(send_p, later[-1]), keep_q, swapped(send_q, 4)),
        [
            (shape(rest // 2, 2), bf16), (shape(rest // 2, 2), bf16),
            (shape(quart, 1), f32), (shape(quart, 1), bf16),
        ],
        "fourth",
    )
    total_q, send_q = scattered(total_q, send_q, later, own_bit)
    p_a, p_b = gathered(p_a, later), gathered(p_b, later)
    pair = pair_step(place, own, back2, back4, p_a)
    near_a, near_b, q_a, q_b = stage(
        fifth_kernel,
        (
            place, old, p_a, swapped(p_a, 4), p_b, swapped(p_b, 2),
            total_q, swapped(send_q, later[-1]),
        ),
        [
            (shape(quart, 2), bf16), (shape(quart, 2), bf16),
            (shape(rest // 2, 1), bf16), (shape(rest // 2, 1), bf16),
        ],
        "fifth",
        pair,
    )
    pair = swapped(pair, 1)
    q_a, q_b = gathered(q_a, later), gathered(q_b, later)
    first_heads = attention(heads[:early_heads], place, att_q, own, back2, back4, pair)
    whole, near_qa, near_qb, near_q = stage(
        sixth_kernel,
        (
            place, near_a, swapped(near_a, 2), near_b, swapped(near_b, 4),
            q_a, swapped(q_a, 4), q_b, swapped(q_b, 2),
        ),
        [
            (shape(4 * quart, 2), bf16), (shape(quart, 1), bf16),
            (shape(quart, 1), bf16), (shape(2 * quart, 1), bf16),
        ],
        "sixth",
        first_heads,
    )
    far_a, far_b = swapped(near_qa, 2), swapped(near_qb, 4)
    whole_other, near_other = swapped(whole, 1), swapped(near_q, 1)
    other_heads = attention(heads[early_heads:], place, att_q, own, back2, back4, pair, whole)
    hidden_q = hidden_step(fast_q, whole, whole_other)
    far = far_rows(far_a, far_b, other_heads, hidden_q)
    fast_out = last_step(hidden_q, near_q, far, near_other, swapped(far, 1))
    return (jnp.concatenate([first_heads, other_heads], axis=1), fast_out)


def solution(mesh):
    tokens = P("seq", "head")
    weights = P(None, "head")
    return jax.shard_map(
        body,
        mesh=mesh,
        in_specs=(tokens,) * 6 + (P("seq"),) + (weights,) * 3,
        out_specs=(tokens, tokens),
        check_vma=False,
    )
```

```python
import functools
import math

import jax
import jax.numpy as jnp
from jax import lax
from jax.experimental import pallas as pl
from jax.experimental.pallas import tpu as pltpu
from jax.sharding import PartitionSpec as P

WINDOW = 1024
HEAD_DIM = 128
norm_eps = 1e-06
f32 = jnp.float32
bf16 = jnp.bfloat16

SMEM = pl.BlockSpec(memory_space=pltpu.SMEM)
VMEM = pl.BlockSpec(memory_space=pltpu.VMEM)
HBM = pl.BlockSpec(memory_space=pltpu.HBM)
ANY = pl.BlockSpec(memory_space=pl.ANY)
PARAMS = pltpu.CompilerParams(vmem_limit_bytes=16 << 20)


def swapped(value, bit):
    count = lax.axis_size("seq")
    return lax.ppermute(value, "seq", [(at, at ^ bit) for at in range(count)])


def kernel_call(kernel, operands, tied=(), in_specs=None, name=None, **rest):
    given = len(operands)

    def run(*refs):
        kernel(*refs[:given], *refs[given + len(tied) :])

    return pl.pallas_call(
        run, in_specs=list(in_specs) + [ANY] * len(tied), name=name, **rest
    )(*operands, *tied)


def cost(flops, moved_bytes, exps=0):
    return pl.CostEstimate(flops=flops, bytes_accessed=moved_bytes, transcendentals=exps)


def attention_kernel(
    place_ref, q_ref, own_k, own_v, back2_k, back2_v, back4_k, back4_v, pair_ref, out_ref
):
    keys = [own_k, back4_k, pair_ref.at[0, 0], back2_k, pair_ref.at[1, 0]]
    vals = [own_v, back4_v, pair_ref.at[0, 1], back2_v, pair_ref.at[1, 1]]
    rows, width = q_ref.shape
    place = place_ref[0]
    factor = HEAD_DIM ** (-0.5) * math.log2(math.e)
    q_at = lax.broadcasted_iota(jnp.int32, (rows, rows), 0)
    k_at = lax.broadcasted_iota(jnp.int32, (rows, rows), 1)
    inside = k_at <= q_at

    def attend(cols, masked):
        query = q_ref[:, cols]

        def score(at):
            return lax.dot_general(
                query, keys[at][:, cols], (((1,), (1,)), ((), ())), preferred_element_type=f32
            )

        def seen(part, back):
            return jnp.where(place >= back, part, -1e30) if masked else part

        parts = [jnp.where(inside, score(0), seen(score(1), 4))]
        parts += [seen(score(at), at - 1) for at in range(2, 5)]
        row_max = functools.reduce(
            jnp.maximum, [jnp.max(part, axis=1, keepdims=True) for part in parts]
        )
        shift = row_max * factor
        parts = [jnp.exp2(part * factor - shift) for part in parts]
        total = functools.reduce(jnp.add, [jnp.sum(e, axis=1, keepdims=True) for e in parts])
        scale = 1.0 / total
        parts = [(part * scale).astype(bf16) for part in parts]
        zero = jnp.zeros_like(parts[0])
        parts = [jnp.where(inside, parts[0], zero), jnp.where(inside, zero, parts[0])] + parts[1:]
        result = jnp.zeros((rows, HEAD_DIM), f32)
        for part, val in zip(parts, vals):
            result += jnp.dot(part, val[:, cols], preferred_element_type=f32)
        out_ref[:, cols] = result.astype(bf16)

    def every(masked):
        for head in range(width // HEAD_DIM):
            attend(slice(head * HEAD_DIM, (head + 1) * HEAD_DIM), masked)

    pl.when(place >= 4)(lambda: every(False))
    pl.when(place < 4)(lambda: every(True))


def attention(place, query, blocks, pair):
    rows, width = query.shape
    return pl.pallas_call(
        attention_kernel,
        out_shape=jax.ShapeDtypeStruct((rows, width), bf16),
        in_specs=[SMEM] + [VMEM] * 8,
        out_specs=VMEM,
        compiler_params=PARAMS,
        cost_estimate=cost(20 * rows * rows * width, 24 * rows * width, 5 * rows * rows * 5),
        name="attention",
    )(place[None], query, *blocks, pair)


def prepare_kernel(place_ref, gate_ref, up_ref, down_ref, out_ref, hold):
    hidden = gate_ref.shape[1]
    half = hidden // 2
    window = hold.shape[0]
    core = place_ref[0] % 2
    low = pl.multiple_of(core * (hidden - window), 128)
    off = pl.multiple_of(core * (half - hidden + window), 64)
    for at, ref in enumerate((gate_ref, up_ref, down_ref)):
        hold[...] = ref[:, pl.ds(low, window)].T
        out_ref[at] = hold[pl.ds(off, half), :]


def prepared(place, w_gate, w_up, w_down):
    feats, hidden = w_gate.shape
    half = hidden // 2
    window = -(-half // 128) * 128
    return pl.pallas_call(
        prepare_kernel,
        out_shape=jax.ShapeDtypeStruct((3, half, feats), bf16),
        in_specs=[SMEM] + [VMEM] * 3,
        out_specs=VMEM,
        scratch_shapes=[pltpu.VMEM((window, feats), bf16)],
        compiler_params=PARAMS,
        cost_estimate=cost(0, 9 * feats * hidden),
        name="prepare",
    )(place[None], w_gate, w_up, w_down)


def grad_kernel(
    place_ref, turned_ref, k0_ref, k1_ref, v0_ref, v1_ref, r0_ref, r1_ref, key_ref, val_ref,
    send_p, send_q, keep_p, keep_q, own_k, own_v, hold,
):
    own_k[...] = key_ref[...]
    own_v[...] = val_ref[...]

    def project(at, rows):
        return lax.dot_general(
            turned_ref[at], rows, (((1,), (1,)), ((), ())), preferred_element_type=f32
        )

    terms = []
    for keys, vals, rate_ref in ((k0_ref, v0_ref, r0_ref), (k1_ref, v1_ref, r1_ref)):
        rate = rate_ref[...]
        pre_gate = project(0, keys[...])
        pre_up = project(1, keys[...])
        back = rate * project(2, vals[...])
        sigmoid_v = jax.nn.sigmoid(pre_gate)
        silu = pre_gate * sigmoid_v
        slope = sigmoid_v * (1.0 + pre_gate * (1.0 - sigmoid_v))
        terms.append(
            (
                (back * pre_up * slope).astype(bf16),
                (back * silu).astype(bf16),
                (rate * silu * pre_up).astype(bf16),
            )
        )
    sources = ((k0_ref, k1_ref), (k0_ref, k1_ref), (v0_ref, v1_ref))
    for at in range(3):
        hold[at] = jnp.dot(
            terms[0][at], sources[at][0][...], preferred_element_type=f32
        ) + jnp.dot(terms[1][at], sources[at][1][...], preferred_element_type=f32)
    quart = send_p.shape[2]
    row = (place_ref[0] // 2) % 2
    for at in range(3):
        send, keep = (send_p.at[at], keep_p.at[at]) if at < 2 else (send_q.at[0], keep_q.at[0])
        for other in range(2):
            there = pl.multiple_of((2 * (1 - row) + other) * quart, 8)
            here = pl.multiple_of((2 * row + other) * quart, 8)
            send[other] = hold[at, pl.ds(there, quart), :].astype(bf16)
            keep[other] = hold[at, pl.ds(here, quart), :]


def gradients(place, turned_w, k0, k1, v0, v1, r0, r1, att_k, att_v):
    _, half, feats = turned_w.shape
    rows = k0.shape[0]
    return pl.pallas_call(
        grad_kernel,
        out_shape=[
            jax.ShapeDtypeStruct((count, 2, half // 4, feats), kind)
            for kind in (bf16, f32)
            for count in (2, 1)
        ]
        + [jax.ShapeDtypeStruct(att_k.shape, bf16)] * 2,
        in_specs=[SMEM] + [VMEM] * 9,
        out_specs=[VMEM] * 6,
        scratch_shapes=[pltpu.VMEM((3, half, feats), f32)],
        compiler_params=PARAMS,
        cost_estimate=cost(24 * rows * half * feats, 20 * half * feats, 2 * half * rows),
        name="gradients",
    )(place[None], turned_w, k0, k1, v0, v1, r0, r1, att_k, att_v)


def stage(kernel, operands, outs, name, *tied):
    return kernel_call(
        kernel,
        (operands[0][None], *operands[1:]),
        tied,
        out_shape=[jax.ShapeDtypeStruct(shape, kind) for shape, kind in outs],
        in_specs=[SMEM] + [VMEM] * (len(operands) - 1),
        out_specs=[VMEM] * len(outs),
        compiler_params=PARAMS,
        cost_estimate=cost(0, 0),
        name=name,
    )


def halve(place_ref, keep, got, send, kept):
    row = (place_ref[0] // 4) % 2
    for at in range(keep.shape[0]):
        send[at] = (keep[at, 1 - row] + got[at, 1 - row].astype(f32)).astype(bf16)
        kept[at] = keep[at, row] + got[at, row].astype(f32)


def add(place_ref, keep, got, send, total):
    for at in range(keep.shape[0]):
        summed = keep[at] + got[at].astype(f32)
        total[at] = summed
        send[at] = summed.astype(bf16)


def window_kernel(place_ref, own_k, own_v, back_k, back_v, out_k, out_v):
    early = (place_ref[0] // 2) % 2 == 0

    @pl.when(early)
    def _():
        out_k[...] = own_k[...]
        out_v[...] = own_v[...]

    @pl.when(jnp.logical_not(early))
    def _():
        out_k[...] = back_k[...]
        out_v[...] = back_v[...]


def renorm_kernel(place_ref, old_ref, keep_p, got_p, keep_q, got_q, part_a, part_b):
    rows = part_a.shape[1]
    for at in range(3):
        keep, got = (keep_p[at], got_p[at]) if at < 2 else (keep_q[0], got_q[0])
        old = old_ref[at].astype(f32)
        updated = old + (keep + got.astype(f32))
        old_norm = jnp.sqrt(jnp.sum(old * old, axis=1, keepdims=True))
        squares = jnp.sum(updated * updated, axis=1, keepdims=True)
        fresh = updated * (old_norm / jnp.sqrt(squares + norm_eps))
        part_a[at] = fresh[:rows].astype(bf16)
        part_b[at] = fresh[rows:].astype(bf16)


def near_kernel(
    place_ref, part_a, got_a, part_b, got_b, own_k, own_v, back2_k, back2_v, back4_k, back4_v,
    near_a, near_b, near, pair,
):
    rows = part_a.shape[1]
    for at in range(3):
        for part, got, out, low in (
            (part_a, got_a, near_a, 0),
            (part_b, got_b, near_b, 2 * rows),
        ):
            both = jnp.concatenate([part[at].astype(f32), got[at].astype(f32)], axis=0)
            out[at] = both.astype(bf16)
            near[at, low : low + 2 * rows] = both.astype(bf16)
    even = place_ref[0] % 2 == 0

    @pl.when(even)
    def _():
        pair[0, 0] = own_k[...]
        pair[0, 1] = own_v[...]
        pair[1, 0] = back2_k[...]
        pair[1, 1] = back2_v[...]

    @pl.when(jnp.logical_not(even))
    def _():
        pair[0, 0] = back2_k[...]
        pair[0, 1] = back2_v[...]
        pair[1, 0] = back4_k[...]
        pair[1, 1] = back4_v[...]


def near_rows(place, part_a, got_a, part_b, got_b, blocks):
    rows, feats = part_a.shape[1:]
    return pl.pallas_call(
        near_kernel,
        out_shape=[
            jax.ShapeDtypeStruct((3, size * rows, feats), bf16) for size in (2, 2, 4)
        ]
        + [jax.ShapeDtypeStruct((2, 2) + blocks[0].shape, bf16)],
        in_specs=[SMEM] + [VMEM] * 10,
        out_specs=[VMEM] * 4,
        compiler_params=PARAMS,
        cost_estimate=cost(0, part_a.size * 14 + blocks[0].size * 8),
        name="near",
    )(place[None], part_a, got_a, part_b, got_b, *blocks)


def fast_output(query, hold):
    gate_q = lax.dot_general(
        query, hold[0], (((1,), (1,)), ((), ())), preferred_element_type=f32
    )
    up_q = lax.dot_general(query, hold[1], (((1,), (1,)), ((), ())), preferred_element_type=f32)
    hidden_q = (gate_q * jax.nn.sigmoid(gate_q) * up_q).astype(bf16)
    return jnp.dot(hidden_q, hold[2], preferred_element_type=f32)


def first_kernel(q_ref, near, near_other, out_ref, hold):
    rows = near.shape[1]
    hold[:, :rows] = near[...]
    hold[:, rows:] = near_other[...]
    out_ref[...] = fast_output(q_ref[...], hold)


def first_half(query, near, near_other):
    rows, feats = query.shape
    units = 2 * near.shape[1]
    return pl.pallas_call(
        first_kernel,
        out_shape=jax.ShapeDtypeStruct((rows, feats), f32),
        in_specs=[VMEM] * 3,
        out_specs=VMEM,
        scratch_shapes=[pltpu.VMEM((3, units, feats), bf16)],
        compiler_params=PARAMS,
        cost_estimate=cost(6 * rows * units * feats, 12 * units * feats, units * rows),
        name="first_half",
    )(query, near, near_other)


def far_kernel(got_a, got_b, attended, half_out, far, passed, passed_half):
    del attended, half_out, passed, passed_half
    rows = got_a.shape[1]
    far[:, :rows] = got_a[...]
    far[:, rows:] = got_b[...]


def far_rows(got_a, got_b, attended, half_out):
    shape = (3, 2 * got_a.shape[1], got_a.shape[2])
    return pl.pallas_call(
        far_kernel,
        out_shape=[
            jax.ShapeDtypeStruct(shape, bf16),
            jax.ShapeDtypeStruct(attended.shape, bf16),
            jax.ShapeDtypeStruct(half_out.shape, f32),
        ],
        in_specs=[VMEM] * 2 + [ANY] * 2,
        out_specs=[VMEM, ANY, ANY],
        input_output_aliases={2: 1, 3: 2},
        compiler_params=PARAMS,
        cost_estimate=cost(0, got_a.size * 8),
        name="far",
    )(got_a, got_b, attended, half_out)


def part_kernel(q_ref, before, rows_ref, out_ref):
    out_ref[...] = (before[...] + fast_output(q_ref[...], rows_ref)).astype(out_ref.dtype)


def part_step(query, before, weights, kind, name):
    rows, feats = query.shape
    units = weights.shape[1]
    return pl.pallas_call(
        part_kernel,
        out_shape=jax.ShapeDtypeStruct((rows, feats), kind),
        in_specs=[VMEM] * 3,
        out_specs=VMEM,
        compiler_params=PARAMS,
        cost_estimate=cost(6 * rows * units * feats, 6 * units * feats, units * rows),
        name=name,
    )(query, before, weights)


def body(att_q, att_k, att_v, fast_q, fast_k, fast_v, learn_rates, w_gate, w_up, w_down):
    count = lax.axis_size("seq")
    place = lax.axis_index("seq")
    feats, hidden = w_gate.shape
    quart = hidden // 8
    later = [1 << at for at in range(3, count.bit_length() - 1)]
    own_bit = {bit: (place // bit) % 2 for bit in [2, 4] + later}

    other_k, other_v = swapped(fast_k, 1), swapped(fast_v, 1)
    other_r = swapped(learn_rates, 1)
    turned_w = prepared(place, w_gate, w_up, w_down)
    send_p, send_q, keep_p, keep_q, own_k, own_v = gradients(
        place, turned_w, fast_k, other_k, fast_v, other_v,
        learn_rates[None, :], other_r[None, :], att_k, att_v,
    )
    around = [(at, (at + 4) % count) for at in range(count)]
    back4_k, back4_v = (lax.ppermute(part, "seq", around) for part in (own_k, own_v))
    rest = quart
    start = own_bit[2] * 2 * quart + own_bit[4] * quart
    for bit in later[:-1]:
        rest //= 2
        start += own_bit[bit] * rest
    old = lax.dynamic_slice_in_dim(turned_w, start, rest, 1)

    def shapes(matrices):
        return [((matrices, quart, feats), bf16), ((matrices, quart, feats), f32)]

    def scattered(send, total):
        for bit in later[:-1]:
            total = total.reshape(total.shape[0], 2, -1, feats)
            send = lax.dynamic_index_in_dim(total, 1 - own_bit[bit], 1, keepdims=False)
            total = lax.dynamic_index_in_dim(total, own_bit[bit], 1, keepdims=False)
            total = total + swapped(send.astype(bf16), bit).astype(f32)
            send = total.astype(bf16)
        return total, swapped(send, later[-1])

    got_p, got_q = swapped(send_p, 2), swapped(send_q, 2)
    send_p, keep_p = stage(halve, (place, keep_p, got_p), shapes(2), "second_p")
    got_p = swapped(send_p, 4)
    send_q, keep_q = stage(halve, (place, keep_q, got_q), shapes(1), "second_q", send_p)
    got_q = swapped(send_q, 4)
    send_p, total_p = stage(add, (place, keep_p, got_p), shapes(2), "third_p", send_q)
    windows = stage(
        window_kernel,
        (place, own_k, own_v, back4_k, back4_v),
        [(own_k.shape, bf16)] * 2,
        "window",
        send_p,
    )
    back2_k, back2_v = (swapped(part, 2) for part in windows)
    blocks = (own_k, own_v, back2_k, back2_v, back4_k, back4_v)
    total_p, got_p = scattered(send_p, total_p)
    send_q, total_q = stage(add, (place, keep_q, got_q), shapes(1), "third_q", send_p)
    total_q, got_q = scattered(send_q, total_q)
    part_a, part_b = stage(
        renorm_kernel,
        (place, old, total_p, got_p, total_q, got_q),
        [((3, rest // 2, feats), bf16)] * 2,
        "renorm",
    )

    for bit in reversed(later[:-1]):
        part_a = jnp.concatenate([part_a, swapped(part_a, bit)], axis=1)
        part_b = jnp.concatenate([part_b, swapped(part_b, bit)], axis=1)
    near_a, near_b, near, pair = near_rows(
        place, part_a, swapped(part_a, 4), part_b, swapped(part_b, 2), blocks
    )
    got_a, got_b = swapped(near_a, 2), swapped(near_b, 4)
    near_other = swapped(near, 1)
    pair = swapped(pair, 1)
    attended = attention(place, att_q, blocks, pair)
    half_out = first_half(fast_q, near, near_other)
    far, attended, half_out = far_rows(got_a, got_b, attended, half_out)
    half_out = part_step(fast_q, half_out, far, f32, "own_far")
    fast_out = part_step(fast_q, half_out, swapped(far, 1), bf16, "last")
    return (attended, fast_out)


def solution(mesh):
    tokens = P("seq", "head")
    weights = P(None, "head")
    return jax.shard_map(
        body,
        mesh=mesh,
        in_specs=(tokens,) * 6 + (P("seq"),) + (weights,) * 3,
        out_specs=(tokens, tokens),
        check_vma=False,
    )
```

```python
import functools
import math

import jax
import jax.numpy as jnp
from jax import lax
from jax.experimental import pallas as pl
from jax.experimental.pallas import tpu as pltpu
from jax.sharding import PartitionSpec as P

WINDOW = 1024
HEAD_DIM = 128
norm_eps = 1e-06
f32 = jnp.float32
bf16 = jnp.bfloat16

SMEM = pl.BlockSpec(memory_space=pltpu.SMEM)
VMEM = pl.BlockSpec(memory_space=pltpu.VMEM)
HBM = pl.BlockSpec(memory_space=pltpu.HBM)
ANY = pl.BlockSpec(memory_space=pl.ANY)
PARAMS = pltpu.CompilerParams(vmem_limit_bytes=16 << 20)


def swapped(value, bit):
    count = lax.axis_size("seq")
    return lax.ppermute(value, "seq", [(at, at ^ bit) for at in range(count)])


def kernel_call(kernel, operands, tied=(), in_specs=None, name=None, **rest):
    given = len(operands)

    def run(*refs):
        kernel(*refs[:given], *refs[given + len(tied) :])

    return pl.pallas_call(
        run, in_specs=list(in_specs) + [ANY] * len(tied), name=name, **rest
    )(*operands, *tied)


def cost(flops, moved_bytes, exps=0):
    return pl.CostEstimate(flops=flops, bytes_accessed=moved_bytes, transcendentals=exps)


def attention_kernel(
    place_ref, q_ref, own_k, own_v, back2_k, back2_v, back4_k, back4_v, pair_ref, out_ref
):
    keys = [own_k, back4_k, pair_ref.at[0, 0], back2_k, pair_ref.at[1, 0]]
    vals = [own_v, back4_v, pair_ref.at[0, 1], back2_v, pair_ref.at[1, 1]]
    rows, width = q_ref.shape
    place = place_ref[0]
    factor = HEAD_DIM ** (-0.5) * math.log2(math.e)
    q_at = lax.broadcasted_iota(jnp.int32, (rows, rows), 0)
    k_at = lax.broadcasted_iota(jnp.int32, (rows, rows), 1)
    inside = k_at <= q_at

    def attend(cols, masked):
        query = q_ref[:, cols]

        def score(at):
            return lax.dot_general(
                query, keys[at][:, cols], (((1,), (1,)), ((), ())), preferred_element_type=f32
            )

        def seen(part, back):
            return jnp.where(place >= back, part, -1e30) if masked else part

        parts = [jnp.where(inside, score(0), seen(score(1), 4))]
        parts += [seen(score(at), at - 1) for at in range(2, 5)]
        row_max = functools.reduce(
            jnp.maximum, [jnp.max(part, axis=1, keepdims=True) for part in parts]
        )
        shift = row_max * factor
        parts = [jnp.exp2(part * factor - shift) for part in parts]
        total = functools.reduce(jnp.add, [jnp.sum(e, axis=1, keepdims=True) for e in parts])
        scale = 1.0 / total
        parts = [(part * scale).astype(bf16) for part in parts]
        zero = jnp.zeros_like(parts[0])
        parts = [jnp.where(inside, parts[0], zero), jnp.where(inside, zero, parts[0])] + parts[1:]
        result = jnp.zeros((rows, HEAD_DIM), f32)
        for part, val in zip(parts, vals):
            result += jnp.dot(part, val[:, cols], preferred_element_type=f32)
        out_ref[:, cols] = result.astype(bf16)

    def every(masked):
        for head in range(width // HEAD_DIM):
            attend(slice(head * HEAD_DIM, (head + 1) * HEAD_DIM), masked)

    pl.when(place >= 4)(lambda: every(False))
    pl.when(place < 4)(lambda: every(True))


def attention(place, query, blocks, pair):
    rows, width = query.shape
    return pl.pallas_call(
        attention_kernel,
        out_shape=jax.ShapeDtypeStruct((rows, width), bf16),
        in_specs=[SMEM] + [VMEM] * 8,
        out_specs=VMEM,
        compiler_params=PARAMS,
        cost_estimate=cost(20 * rows * rows * width, 24 * rows * width, 5 * rows * rows * 5),
        name="attention",
    )(place[None], query, *blocks, pair)


def prepare_kernel(place_ref, gate_ref, up_ref, down_ref, out_ref, hold):
    hidden = gate_ref.shape[1]
    half = hidden // 2
    window = hold.shape[0]
    core = place_ref[0] % 2
    low = pl.multiple_of(core * (hidden - window), 128)
    off = pl.multiple_of(core * (half - hidden + window), 64)
    for at, ref in enumerate((gate_ref, up_ref, down_ref)):
        hold[...] = ref[:, pl.ds(low, window)].T
        out_ref[at] = hold[pl.ds(off, half), :]


def prepared(place, w_gate, w_up, w_down):
    feats, hidden = w_gate.shape
    half = hidden // 2
    window = -(-half // 128) * 128
    return pl.pallas_call(
        prepare_kernel,
        out_shape=jax.ShapeDtypeStruct((3, half, feats), bf16),
        in_specs=[SMEM] + [VMEM] * 3,
        out_specs=VMEM,
        scratch_shapes=[pltpu.VMEM((window, feats), bf16)],
        compiler_params=PARAMS,
        cost_estimate=cost(0, 9 * feats * hidden),
        name="prepare",
    )(place[None], w_gate, w_up, w_down)


def grad_kernel(
    place_ref, turned_ref, k0_ref, k1_ref, v0_ref, v1_ref, r0_ref, r1_ref, key_ref, val_ref,
    send_p, send_q, keep_p, keep_q, own_k, own_v, hold,
):
    own_k[...] = key_ref[...]
    own_v[...] = val_ref[...]

    def project(at, rows):
        return lax.dot_general(
            turned_ref[at], rows, (((1,), (1,)), ((), ())), preferred_element_type=f32
        )

    terms = []
    for keys, vals, rate_ref in ((k0_ref, v0_ref, r0_ref), (k1_ref, v1_ref, r1_ref)):
        rate = rate_ref[...]
        pre_gate = project(0, keys[...])
        pre_up = project(1, keys[...])
        back = rate * project(2, vals[...])
        sigmoid_v = jax.nn.sigmoid(pre_gate)
        silu = pre_gate * sigmoid_v
        slope = sigmoid_v * (1.0 + pre_gate * (1.0 - sigmoid_v))
        terms.append(
            (
                (back * pre_up * slope).astype(bf16),
                (back * silu).astype(bf16),
                (rate * silu * pre_up).astype(bf16),
            )
        )
    sources = ((k0_ref, k1_ref), (k0_ref, k1_ref), (v0_ref, v1_ref))
    for at in range(3):
        hold[at] = jnp.dot(
            terms[0][at], sources[at][0][...], preferred_element_type=f32
        ) + jnp.dot(terms[1][at], sources[at][1][...], preferred_element_type=f32)
    quart = send_p.shape[2]
    row = (place_ref[0] // 2) % 2
    for at in range(3):
        send, keep = (send_p.at[at], keep_p.at[at]) if at < 2 else (send_q.at[0], keep_q.at[0])
        for other in range(2):
            there = pl.multiple_of((2 * (1 - row) + other) * quart, 8)
            here = pl.multiple_of((2 * row + other) * quart, 8)
            send[other] = hold[at, pl.ds(there, quart), :].astype(bf16)
            keep[other] = hold[at, pl.ds(here, quart), :]


def gradients(place, turned_w, k0, k1, v0, v1, r0, r1, att_k, att_v):
    _, half, feats = turned_w.shape
    rows = k0.shape[0]
    return pl.pallas_call(
        grad_kernel,
        out_shape=[
            jax.ShapeDtypeStruct((count, 2, half // 4, feats), kind)
            for kind in (bf16, f32)
            for count in (2, 1)
        ]
        + [jax.ShapeDtypeStruct(att_k.shape, bf16)] * 2,
        in_specs=[SMEM] + [VMEM] * 9,
        out_specs=[VMEM] * 6,
        scratch_shapes=[pltpu.VMEM((3, half, feats), f32)],
        compiler_params=PARAMS,
        cost_estimate=cost(24 * rows * half * feats, 20 * half * feats, 2 * half * rows),
        name="gradients",
    )(place[None], turned_w, k0, k1, v0, v1, r0, r1, att_k, att_v)


def stage(kernel, operands, outs, name, *tied):
    return kernel_call(
        kernel,
        (operands[0][None], *operands[1:]),
        tied,
        out_shape=[jax.ShapeDtypeStruct(shape, kind) for shape, kind in outs],
        in_specs=[SMEM] + [VMEM] * (len(operands) - 1),
        out_specs=[VMEM] * len(outs),
        compiler_params=PARAMS,
        cost_estimate=cost(0, 0),
        name=name,
    )


def halve(place_ref, keep, got, send, kept):
    row = (place_ref[0] // 4) % 2
    for at in range(keep.shape[0]):
        send[at] = (keep[at, 1 - row] + got[at, 1 - row].astype(f32)).astype(bf16)
        kept[at] = keep[at, row] + got[at, row].astype(f32)


def add(place_ref, keep, got, send, total):
    for at in range(keep.shape[0]):
        summed = keep[at] + got[at].astype(f32)
        total[at] = summed
        send[at] = summed.astype(bf16)


def window_kernel(place_ref, own_k, own_v, back_k, back_v, out_k, out_v):
    early = (place_ref[0] // 2) % 2 == 0

    @pl.when(early)
    def _():
        out_k[...] = own_k[...]
        out_v[...] = own_v[...]

    @pl.when(jnp.logical_not(early))
    def _():
        out_k[...] = back_k[...]
        out_v[...] = back_v[...]


def renorm_kernel(place_ref, old_ref, keep_p, got_p, keep_q, got_q, part_a, part_b):
    rows = part_a.shape[1]
    units = 2 * rows
    first = 0
    if old_ref.shape[1] > units:
        quart = old_ref.shape[1] // 4
        first = (place_ref[0] // 2) % 2 * (2 * quart) + (place_ref[0] // 4) % 2 * quart
        first = pl.multiple_of(first, 16)
    for at in range(3):
        keep, got = (keep_p[at], got_p[at]) if at < 2 else (keep_q[0], got_q[0])
        old = old_ref[at, pl.ds(first, units), :].astype(f32)
        updated = old + (keep + got.astype(f32))
        old_norm = jnp.sqrt(jnp.sum(old * old, axis=1, keepdims=True))
        squares = jnp.sum(updated * updated, axis=1, keepdims=True)
        fresh = updated * (old_norm / jnp.sqrt(squares + norm_eps))
        part_a[at] = fresh[:rows].astype(bf16)
        part_b[at] = fresh[rows:].astype(bf16)


def near_kernel(
    place_ref, part_a, got_a, part_b, got_b, own_k, own_v, back2_k, back2_v, back4_k, back4_v,
    near_a, near_b, near, pair,
):
    rows = part_a.shape[1]
    for at in range(3):
        for part, got, out, low in (
            (part_a, got_a, near_a, 0),
            (part_b, got_b, near_b, 2 * rows),
        ):
            both = jnp.concatenate([part[at].astype(f32), got[at].astype(f32)], axis=0)
            out[at] = both.astype(bf16)
            near[at, low : low + 2 * rows] = both.astype(bf16)
    even = place_ref[0] % 2 == 0

    @pl.when(even)
    def _():
        pair[0, 0] = own_k[...]
        pair[0, 1] = own_v[...]
        pair[1, 0] = back2_k[...]
        pair[1, 1] = back2_v[...]

    @pl.when(jnp.logical_not(even))
    def _():
        pair[0, 0] = back2_k[...]
        pair[0, 1] = back2_v[...]
        pair[1, 0] = back4_k[...]
        pair[1, 1] = back4_v[...]


def near_rows(place, part_a, got_a, part_b, got_b, blocks):
    rows, feats = part_a.shape[1:]
    return pl.pallas_call(
        near_kernel,
        out_shape=[
            jax.ShapeDtypeStruct((3, size * rows, feats), bf16) for size in (2, 2, 4)
        ]
        + [jax.ShapeDtypeStruct((2, 2) + blocks[0].shape, bf16)],
        in_specs=[SMEM] + [VMEM] * 10,
        out_specs=[VMEM] * 4,
        compiler_params=PARAMS,
        cost_estimate=cost(0, part_a.size * 14 + blocks[0].size * 8),
        name="near",
    )(place[None], part_a, got_a, part_b, got_b, *blocks)


def fast_output(query, hold):
    gate_q = lax.dot_general(
        query, hold[0], (((1,), (1,)), ((), ())), preferred_element_type=f32
    )
    up_q = lax.dot_general(query, hold[1], (((1,), (1,)), ((), ())), preferred_element_type=f32)
    hidden_q = (gate_q * jax.nn.sigmoid(gate_q) * up_q).astype(bf16)
    return jnp.dot(hidden_q, hold[2], preferred_element_type=f32)


def first_kernel(q_ref, near, near_other, out_ref, hold):
    rows = near.shape[1]
    hold[:, :rows] = near[...]
    hold[:, rows:] = near_other[...]
    out_ref[...] = fast_output(q_ref[...], hold)


def first_half(query, near, near_other):
    rows, feats = query.shape
    units = 2 * near.shape[1]
    return pl.pallas_call(
        first_kernel,
        out_shape=jax.ShapeDtypeStruct((rows, feats), f32),
        in_specs=[VMEM] * 3,
        out_specs=VMEM,
        scratch_shapes=[pltpu.VMEM((3, units, feats), bf16)],
        compiler_params=PARAMS,
        cost_estimate=cost(6 * rows * units * feats, 12 * units * feats, units * rows),
        name="first_half",
    )(query, near, near_other)


def far_kernel(got_a, got_b, attended, half_out, far, passed, passed_half):
    del attended, half_out, passed, passed_half
    rows = got_a.shape[1]
    far[:, :rows] = got_a[...]
    far[:, rows:] = got_b[...]


def far_rows(got_a, got_b, attended, half_out):
    shape = (3, 2 * got_a.shape[1], got_a.shape[2])
    return pl.pallas_call(
        far_kernel,
        out_shape=[
            jax.ShapeDtypeStruct(shape, bf16),
            jax.ShapeDtypeStruct(attended.shape, bf16),
            jax.ShapeDtypeStruct(half_out.shape, f32),
        ],
        in_specs=[VMEM] * 2 + [ANY] * 2,
        out_specs=[VMEM, ANY, ANY],
        input_output_aliases={2: 1, 3: 2},
        compiler_params=PARAMS,
        cost_estimate=cost(0, got_a.size * 8),
        name="far",
    )(got_a, got_b, attended, half_out)


def part_kernel(q_ref, before, rows_ref, out_ref):
    out_ref[...] = (before[...] + fast_output(q_ref[...], rows_ref)).astype(out_ref.dtype)


def part_step(query, before, weights, kind, name):
    rows, feats = query.shape
    units = weights.shape[1]
    return pl.pallas_call(
        part_kernel,
        out_shape=jax.ShapeDtypeStruct((rows, feats), kind),
        in_specs=[VMEM] * 3,
        out_specs=VMEM,
        compiler_params=PARAMS,
        cost_estimate=cost(6 * rows * units * feats, 6 * units * feats, units * rows),
        name=name,
    )(query, before, weights)


def body(att_q, att_k, att_v, fast_q, fast_k, fast_v, learn_rates, w_gate, w_up, w_down):
    count = lax.axis_size("seq")
    place = lax.axis_index("seq")
    feats, hidden = w_gate.shape
    quart = hidden // 8
    later = [1 << at for at in range(3, count.bit_length() - 1)]
    own_bit = {bit: (place // bit) % 2 for bit in [2, 4] + later}

    other_k, other_v = swapped(fast_k, 1), swapped(fast_v, 1)
    other_r = swapped(learn_rates, 1)
    turned_w = prepared(place, w_gate, w_up, w_down)
    send_p, send_q, keep_p, keep_q, own_k, own_v = gradients(
        place, turned_w, fast_k, other_k, fast_v, other_v,
        learn_rates[None, :], other_r[None, :], att_k, att_v,
    )
    around = [(at, (at + 4) % count) for at in range(count)]
    back4_k, back4_v = (lax.ppermute(part, "seq", around) for part in (own_k, own_v))
    rest = quart
    start = own_bit[2] * 2 * quart + own_bit[4] * quart
    for bit in later[:-1]:
        rest //= 2
        start += own_bit[bit] * rest
    old = turned_w
    if len(later) > 1 or quart % 16 > 0:
        old = lax.dynamic_slice_in_dim(turned_w, start, rest, 1)

    def shapes(matrices):
        return [((matrices, quart, feats), bf16), ((matrices, quart, feats), f32)]

    def scattered(send, total):
        for bit in later[:-1]:
            total = total.reshape(total.shape[0], 2, -1, feats)
            send = lax.dynamic_index_in_dim(total, 1 - own_bit[bit], 1, keepdims=False)
            total = lax.dynamic_index_in_dim(total, own_bit[bit], 1, keepdims=False)
            total = total + swapped(send.astype(bf16), bit).astype(f32)
            send = total.astype(bf16)
        return total, swapped(send, later[-1])

    got_p, got_q = swapped(send_p, 2), swapped(send_q, 2)
    send_p, keep_p = stage(halve, (place, keep_p, got_p), shapes(2), "second_p")
    got_p = swapped(send_p, 4)
    send_q, keep_q = stage(halve, (place, keep_q, got_q), shapes(1), "second_q", send_p)
    got_q = swapped(send_q, 4)
    send_p, total_p = stage(add, (place, keep_p, got_p), shapes(2), "third_p", send_q)
    windows = stage(
        window_kernel,
        (place, own_k, own_v, back4_k, back4_v),
        [(own_k.shape, bf16)] * 2,
        "window",
        send_p,
    )
    back2_k, back2_v = (swapped(part, 2) for part in windows)
    blocks = (own_k, own_v, back2_k, back2_v, back4_k, back4_v)
    total_p, got_p = scattered(send_p, total_p)
    send_q, total_q = stage(add, (place, keep_q, got_q), shapes(1), "third_q", send_p)
    total_q, got_q = scattered(send_q, total_q)
    part_a, part_b = stage(
        renorm_kernel,
        (place, old, total_p, got_p, total_q, got_q),
        [((3, rest // 2, feats), bf16)] * 2,
        "renorm",
    )

    for bit in reversed(later[:-1]):
        part_a = jnp.concatenate([part_a, swapped(part_a, bit)], axis=1)
        part_b = jnp.concatenate([part_b, swapped(part_b, bit)], axis=1)
    near_a, near_b, near, pair = near_rows(
        place, part_a, swapped(part_a, 4), part_b, swapped(part_b, 2), blocks
    )
    got_a, got_b = swapped(near_a, 2), swapped(near_b, 4)
    near_other = swapped(near, 1)
    pair = swapped(pair, 1)
    attended = attention(place, att_q, blocks, pair)
    half_out = first_half(fast_q, near, near_other)
    far, attended, half_out = far_rows(got_a, got_b, attended, half_out)
    half_out = part_step(fast_q, half_out, far, f32, "own_far")
    fast_out = part_step(fast_q, half_out, swapped(far, 1), bf16, "last")
    return (attended, fast_out)


def solution(mesh):
    tokens = P("seq", "head")
    weights = P(None, "head")
    return jax.shard_map(
        body,
        mesh=mesh,
        in_specs=(tokens,) * 6 + (P("seq"),) + (weights,) * 3,
        out_specs=(tokens, tokens),
        check_vma=False,
    )
```

```python
import functools
import math

import jax
import jax.numpy as jnp
from jax import lax
from jax.experimental import pallas as pl
from jax.experimental.pallas import tpu as pltpu
from jax.sharding import PartitionSpec as P

WINDOW = 1024
HEAD_DIM = 128
norm_eps = 1e-06
f32 = jnp.float32
bf16 = jnp.bfloat16

SMEM = pl.BlockSpec(memory_space=pltpu.SMEM)
VMEM = pl.BlockSpec(memory_space=pltpu.VMEM)
HBM = pl.BlockSpec(memory_space=pltpu.HBM)
ANY = pl.BlockSpec(memory_space=pl.ANY)
PARAMS = pltpu.CompilerParams(vmem_limit_bytes=16 << 20)


def swapped(value, bit):
    count = lax.axis_size("seq")
    return lax.ppermute(value, "seq", [(at, at ^ bit) for at in range(count)])


def kernel_call(kernel, operands, tied=(), in_specs=None, name=None, **rest):
    given = len(operands)

    def run(*refs):
        kernel(*refs[:given], *refs[given + len(tied) :])

    return pl.pallas_call(
        run, in_specs=list(in_specs) + [ANY] * len(tied), name=name, **rest
    )(*operands, *tied)


def cost(flops, moved_bytes, exps=0):
    return pl.CostEstimate(flops=flops, bytes_accessed=moved_bytes, transcendentals=exps)


def attention_kernel(
    place_ref, q_ref, own_k, own_v, back2_k, back2_v, back4_ref, pair_ref, out_ref
):
    back4_k, back4_v = back4_ref.at[0], back4_ref.at[1]
    keys = [own_k, back4_k, pair_ref.at[0, 0], back2_k, pair_ref.at[1, 0]]
    vals = [own_v, back4_v, pair_ref.at[0, 1], back2_v, pair_ref.at[1, 1]]
    rows, width = q_ref.shape
    place = place_ref[0]
    factor = HEAD_DIM ** (-0.5) * math.log2(math.e)
    q_at = lax.broadcasted_iota(jnp.int32, (rows, rows), 0)
    k_at = lax.broadcasted_iota(jnp.int32, (rows, rows), 1)
    inside = k_at <= q_at

    def attend(cols, masked):
        query = q_ref[:, cols]

        def score(at):
            return lax.dot_general(
                query, keys[at][:, cols], (((1,), (1,)), ((), ())), preferred_element_type=f32
            )

        def seen(part, back):
            return jnp.where(place >= back, part, -1e30) if masked else part

        parts = [jnp.where(inside, score(0), seen(score(1), 4))]
        parts += [seen(score(at), at - 1) for at in range(2, 5)]
        row_max = functools.reduce(
            jnp.maximum, [jnp.max(part, axis=1, keepdims=True) for part in parts]
        )
        shift = row_max * factor
        parts = [jnp.exp2(part * factor - shift) for part in parts]
        total = functools.reduce(jnp.add, [jnp.sum(e, axis=1, keepdims=True) for e in parts])
        scale = 1.0 / total
        parts = [(part * scale).astype(bf16) for part in parts]
        zero = jnp.zeros_like(parts[0])
        parts = [jnp.where(inside, parts[0], zero), jnp.where(inside, zero, parts[0])] + parts[1:]
        result = jnp.zeros((rows, HEAD_DIM), f32)
        for part, val in zip(parts, vals):
            result += jnp.dot(part, val[:, cols], preferred_element_type=f32)
        out_ref[:, cols] = result.astype(bf16)

    def every(masked):
        for head in range(width // HEAD_DIM):
            attend(slice(head * HEAD_DIM, (head + 1) * HEAD_DIM), masked)

    pl.when(place >= 4)(lambda: every(False))
    pl.when(place < 4)(lambda: every(True))


def attention(place, query, blocks, pair):
    rows, width = query.shape
    return pl.pallas_call(
        attention_kernel,
        out_shape=jax.ShapeDtypeStruct((rows, width), bf16),
        in_specs=[SMEM] + [VMEM] * 7,
        out_specs=VMEM,
        compiler_params=PARAMS,
        cost_estimate=cost(20 * rows * rows * width, 24 * rows * width, 5 * rows * rows * 5),
        name="attention",
    )(place[None], query, *blocks, pair)


def prepare_kernel(place_ref, gate_ref, up_ref, down_ref, out_ref, hold):
    hidden = gate_ref.shape[1]
    half = hidden // 2
    window = hold.shape[0]
    core = place_ref[0] % 2
    low = pl.multiple_of(core * (hidden - window), 128)
    off = pl.multiple_of(core * (half - hidden + window), 64)
    for at, ref in enumerate((gate_ref, up_ref, down_ref)):
        hold[...] = ref[:, pl.ds(low, window)].T
        out_ref[at] = hold[pl.ds(off, half), :]


def prepared(place, w_gate, w_up, w_down):
    feats, hidden = w_gate.shape
    half = hidden // 2
    window = -(-half // 128) * 128
    return pl.pallas_call(
        prepare_kernel,
        out_shape=jax.ShapeDtypeStruct((3, half, feats), bf16),
        in_specs=[SMEM] + [VMEM] * 3,
        out_specs=VMEM,
        scratch_shapes=[pltpu.VMEM((window, feats), bf16)],
        compiler_params=PARAMS,
        cost_estimate=cost(0, 9 * feats * hidden),
        name="prepare",
    )(place[None], w_gate, w_up, w_down)


def pack_kernel(key_ref, val_ref, own_ref):
    own_ref[0] = key_ref[...]
    own_ref[1] = val_ref[...]


def packed(att_k, att_v, *tied):
    return kernel_call(
        pack_kernel,
        (att_k, att_v),
        tied,
        out_shape=jax.ShapeDtypeStruct((2,) + att_k.shape, bf16),
        in_specs=[VMEM] * 2,
        out_specs=VMEM,
        compiler_params=PARAMS,
        cost_estimate=cost(0, 0),
        name="pack",
    )


def grad_kernel(
    place_ref, turned_ref, k0_ref, k1_ref, v0_ref, v1_ref, r0_ref, r1_ref,
    send_p, send_q, keep_p, keep_q, hold,
):
    def project(at, rows):
        return lax.dot_general(
            turned_ref[at], rows, (((1,), (1,)), ((), ())), preferred_element_type=f32
        )

    terms = []
    for keys, vals, rate_ref in ((k0_ref, v0_ref, r0_ref), (k1_ref, v1_ref, r1_ref)):
        rate = rate_ref[...]
        pre_gate = project(0, keys[...])
        pre_up = project(1, keys[...])
        back = rate * project(2, vals[...])
        sigmoid_v = jax.nn.sigmoid(pre_gate)
        silu = pre_gate * sigmoid_v
        slope = sigmoid_v * (1.0 + pre_gate * (1.0 - sigmoid_v))
        terms.append(
            (
                (back * pre_up * slope).astype(bf16),
                (back * silu).astype(bf16),
                (rate * silu * pre_up).astype(bf16),
            )
        )
    sources = ((k0_ref, k1_ref), (k0_ref, k1_ref), (v0_ref, v1_ref))
    for at in range(3):
        hold[at] = jnp.dot(
            terms[0][at], sources[at][0][...], preferred_element_type=f32
        ) + jnp.dot(terms[1][at], sources[at][1][...], preferred_element_type=f32)
    quart = send_p.shape[2]
    row = (place_ref[0] // 2) % 2
    for at in range(3):
        send, keep = (send_p.at[at], keep_p.at[at]) if at < 2 else (send_q.at[0], keep_q.at[0])
        for other in range(2):
            there = pl.multiple_of((2 * (1 - row) + other) * quart, 8)
            here = pl.multiple_of((2 * row + other) * quart, 8)
            send[other] = hold[at, pl.ds(there, quart), :].astype(bf16)
            keep[other] = hold[at, pl.ds(here, quart), :]


def gradients(place, turned_w, k0, k1, v0, v1, r0, r1, *tied):
    _, half, feats = turned_w.shape
    rows = k0.shape[0]
    return kernel_call(
        grad_kernel,
        (place[None], turned_w, k0, k1, v0, v1, r0, r1),
        tied,
        out_shape=[
            jax.ShapeDtypeStruct((count, 2, half // 4, feats), kind)
            for kind in (bf16, f32)
            for count in (2, 1)
        ],
        in_specs=[SMEM] + [VMEM] * 7,
        out_specs=[VMEM] * 4,
        scratch_shapes=[pltpu.VMEM((3, half, feats), f32)],
        compiler_params=PARAMS,
        cost_estimate=cost(24 * rows * half * feats, 20 * half * feats, 2 * half * rows),
        name="gradients",
    )


def stage(kernel, operands, outs, name, *tied):
    return kernel_call(
        kernel,
        (operands[0][None], *operands[1:]),
        tied,
        out_shape=[jax.ShapeDtypeStruct(shape, kind) for shape, kind in outs],
        in_specs=[SMEM] + [VMEM] * (len(operands) - 1),
        out_specs=[VMEM] * len(outs),
        compiler_params=PARAMS,
        cost_estimate=cost(0, 0),
        name=name,
    )


def halve(place_ref, keep, got, send, kept):
    row = (place_ref[0] // 4) % 2
    for at in range(keep.shape[0]):
        send[at] = (keep[at, 1 - row] + got[at, 1 - row].astype(f32)).astype(bf16)
        kept[at] = keep[at, row] + got[at, row].astype(f32)


def add(place_ref, keep, got, send, total):
    for at in range(keep.shape[0]):
        summed = keep[at] + got[at].astype(f32)
        total[at] = summed
        send[at] = summed.astype(bf16)


def window_kernel(place_ref, own_k, own_v, back_ref, out_k, out_v):
    back_k, back_v = back_ref.at[0], back_ref.at[1]
    early = (place_ref[0] // 2) % 2 == 0

    @pl.when(early)
    def _():
        out_k[...] = own_k[...]
        out_v[...] = own_v[...]

    @pl.when(jnp.logical_not(early))
    def _():
        out_k[...] = back_k[...]
        out_v[...] = back_v[...]


def renorm_kernel(place_ref, old_ref, keep_p, got_p, keep_q, got_q, part_a, part_b):
    rows = part_a.shape[1]
    units = 2 * rows
    first = 0
    if old_ref.shape[1] > units:
        quart = old_ref.shape[1] // 4
        first = (place_ref[0] // 2) % 2 * (2 * quart) + (place_ref[0] // 4) % 2 * quart
        first = pl.multiple_of(first, 16)
    for at in range(3):
        keep, got = (keep_p[at], got_p[at]) if at < 2 else (keep_q[0], got_q[0])
        old = old_ref[at, pl.ds(first, units), :].astype(f32)
        updated = old + (keep + got.astype(f32))
        old_norm = jnp.sqrt(jnp.sum(old * old, axis=1, keepdims=True))
        squares = jnp.sum(updated * updated, axis=1, keepdims=True)
        fresh = updated * (old_norm / jnp.sqrt(squares + norm_eps))
        part_a[at] = fresh[:rows].astype(bf16)
        part_b[at] = fresh[rows:].astype(bf16)


def near_kernel(
    place_ref, part_a, got_a, part_b, got_b, own_k, own_v, back2_k, back2_v, back4_ref,
    near_a, near_b, near, pair,
):
    back4_k, back4_v = back4_ref.at[0], back4_ref.at[1]
    rows = part_a.shape[1]
    for at in range(3):
        for part, got, out, low in (
            (part_a, got_a, near_a, 0),
            (part_b, got_b, near_b, 2 * rows),
        ):
            both = jnp.concatenate([part[at].astype(f32), got[at].astype(f32)], axis=0)
            out[at] = both.astype(bf16)
            near[at, low : low + 2 * rows] = both.astype(bf16)
    even = place_ref[0] % 2 == 0

    @pl.when(even)
    def _():
        pair[0, 0] = own_k[...]
        pair[0, 1] = own_v[...]
        pair[1, 0] = back2_k[...]
        pair[1, 1] = back2_v[...]

    @pl.when(jnp.logical_not(even))
    def _():
        pair[0, 0] = back2_k[...]
        pair[0, 1] = back2_v[...]
        pair[1, 0] = back4_k[...]
        pair[1, 1] = back4_v[...]


def near_rows(place, part_a, got_a, part_b, got_b, blocks):
    rows, feats = part_a.shape[1:]
    return pl.pallas_call(
        near_kernel,
        out_shape=[
            jax.ShapeDtypeStruct((3, size * rows, feats), bf16) for size in (2, 2, 4)
        ]
        + [jax.ShapeDtypeStruct((2, 2) + blocks[0].shape, bf16)],
        in_specs=[SMEM] + [VMEM] * 9,
        out_specs=[VMEM] * 4,
        compiler_params=PARAMS,
        cost_estimate=cost(0, part_a.size * 14 + blocks[0].size * 8),
        name="near",
    )(place[None], part_a, got_a, part_b, got_b, *blocks)


def fast_output(query, hold):
    gate_q = lax.dot_general(
        query, hold[0], (((1,), (1,)), ((), ())), preferred_element_type=f32
    )
    up_q = lax.dot_general(query, hold[1], (((1,), (1,)), ((), ())), preferred_element_type=f32)
    hidden_q = (gate_q * jax.nn.sigmoid(gate_q) * up_q).astype(bf16)
    return jnp.dot(hidden_q, hold[2], preferred_element_type=f32)


def first_kernel(q_ref, near, near_other, out_ref, hold):
    rows = near.shape[1]
    hold[:, :rows] = near[...]
    hold[:, rows:] = near_other[...]
    out_ref[...] = fast_output(q_ref[...], hold)


def first_half(query, near, near_other):
    rows, feats = query.shape
    units = 2 * near.shape[1]
    return pl.pallas_call(
        first_kernel,
        out_shape=jax.ShapeDtypeStruct((rows, feats), f32),
        in_specs=[VMEM] * 3,
        out_specs=VMEM,
        scratch_shapes=[pltpu.VMEM((3, units, feats), bf16)],
        compiler_params=PARAMS,
        cost_estimate=cost(6 * rows * units * feats, 12 * units * feats, units * rows),
        name="first_half",
    )(query, near, near_other)


def far_kernel(got_a, got_b, attended, half_out, far, passed, passed_half):
    del attended, half_out, passed, passed_half
    rows = got_a.shape[1]
    far[:, :rows] = got_a[...]
    far[:, rows:] = got_b[...]


def far_rows(got_a, got_b, attended, half_out):
    shape = (3, 2 * got_a.shape[1], got_a.shape[2])
    return pl.pallas_call(
        far_kernel,
        out_shape=[
            jax.ShapeDtypeStruct(shape, bf16),
            jax.ShapeDtypeStruct(attended.shape, bf16),
            jax.ShapeDtypeStruct(half_out.shape, f32),
        ],
        in_specs=[VMEM] * 2 + [ANY] * 2,
        out_specs=[VMEM, ANY, ANY],
        input_output_aliases={2: 1, 3: 2},
        compiler_params=PARAMS,
        cost_estimate=cost(0, got_a.size * 8),
        name="far",
    )(got_a, got_b, attended, half_out)


def part_kernel(q_ref, before, rows_ref, out_ref):
    out_ref[...] = (before[...] + fast_output(q_ref[...], rows_ref)).astype(out_ref.dtype)


def part_step(query, before, weights, kind, name):
    rows, feats = query.shape
    units = weights.shape[1]
    return pl.pallas_call(
        part_kernel,
        out_shape=jax.ShapeDtypeStruct((rows, feats), kind),
        in_specs=[VMEM] * 3,
        out_specs=VMEM,
        compiler_params=PARAMS,
        cost_estimate=cost(6 * rows * units * feats, 6 * units * feats, units * rows),
        name=name,
    )(query, before, weights)


def body(att_q, att_k, att_v, fast_q, fast_k, fast_v, learn_rates, w_gate, w_up, w_down):
    count = lax.axis_size("seq")
    place = lax.axis_index("seq")
    feats, hidden = w_gate.shape
    quart = hidden // 8
    later = [1 << at for at in range(3, count.bit_length() - 1)]
    own_bit = {bit: (place // bit) % 2 for bit in [2, 4] + later}

    other_k, other_v = swapped(fast_k, 1), swapped(fast_v, 1)
    other_r = swapped(learn_rates, 1)
    turned_w = prepared(place, w_gate, w_up, w_down)
    own = packed(att_k, att_v, turned_w, other_r)
    back4 = lax.ppermute(own, "seq", [(at, (at + 4) % count) for at in range(count)])
    send_p, send_q, keep_p, keep_q = gradients(
        place, turned_w, fast_k, other_k, fast_v, other_v,
        learn_rates[None, :], other_r[None, :], own,
    )
    rest = quart
    start = own_bit[2] * 2 * quart + own_bit[4] * quart
    for bit in later[:-1]:
        rest //= 2
        start += own_bit[bit] * rest
    old = turned_w
    if len(later) > 1 or quart % 16 > 0:
        old = lax.dynamic_slice_in_dim(turned_w, start, rest, 1)

    def shapes(matrices):
        return [((matrices, quart, feats), bf16), ((matrices, quart, feats), f32)]

    def scattered(send, total):
        for bit in later[:-1]:
            total = total.reshape(total.shape[0], 2, -1, feats)
            send = lax.dynamic_index_in_dim(total, 1 - own_bit[bit], 1, keepdims=False)
            total = lax.dynamic_index_in_dim(total, own_bit[bit], 1, keepdims=False)
            total = total + swapped(send.astype(bf16), bit).astype(f32)
            send = total.astype(bf16)
        return total, swapped(send, later[-1])

    got_p, got_q = swapped(send_p, 2), swapped(send_q, 2)
    send_p, keep_p = stage(halve, (place, keep_p, got_p), shapes(2), "second_p")
    got_p = swapped(send_p, 4)
    send_q, keep_q = stage(halve, (place, keep_q, got_q), shapes(1), "second_q", send_p)
    got_q = swapped(send_q, 4)
    send_p, total_p = stage(add, (place, keep_p, got_p), shapes(2), "third_p", send_q)
    windows = stage(
        window_kernel,
        (place, att_k, att_v, back4),
        [(att_k.shape, bf16)] * 2,
        "window",
        send_p,
    )
    back2_k, back2_v = (swapped(part, 2) for part in windows)
    blocks = (att_k, att_v, back2_k, back2_v, back4)
    total_p, got_p = scattered(send_p, total_p)
    send_q, total_q = stage(add, (place, keep_q, got_q), shapes(1), "third_q", send_p)
    total_q, got_q = scattered(send_q, total_q)
    part_a, part_b = stage(
        renorm_kernel,
        (place, old, total_p, got_p, total_q, got_q),
        [((3, rest // 2, feats), bf16)] * 2,
        "renorm",
    )

    for bit in reversed(later[:-1]):
        part_a = jnp.concatenate([part_a, swapped(part_a, bit)], axis=1)
        part_b = jnp.concatenate([part_b, swapped(part_b, bit)], axis=1)
    near_a, near_b, near, pair = near_rows(
        place, part_a, swapped(part_a, 4), part_b, swapped(part_b, 2), blocks
    )
    got_a, got_b = swapped(near_a, 2), swapped(near_b, 4)
    near_other = swapped(near, 1)
    pair = swapped(pair, 1)
    attended = attention(place, att_q, blocks, pair)
    half_out = first_half(fast_q, near, near_other)
    far, attended, half_out = far_rows(got_a, got_b, attended, half_out)
    half_out = part_step(fast_q, half_out, far, f32, "own_far")
    fast_out = part_step(fast_q, half_out, swapped(far, 1), bf16, "last")
    return (attended, fast_out)


def solution(mesh):
    tokens = P("seq", "head")
    weights = P(None, "head")
    return jax.shard_map(
        body,
        mesh=mesh,
        in_specs=(tokens,) * 6 + (P("seq"),) + (weights,) * 3,
        out_specs=(tokens, tokens),
        check_vma=False,
    )
```

```python
import functools
import math

import jax
import jax.numpy as jnp
from jax import lax
from jax.experimental import pallas as pl
from jax.experimental.pallas import tpu as pltpu
from jax.sharding import PartitionSpec as P

WINDOW = 1024
HEAD_DIM = 128
norm_eps = 1e-06
f32 = jnp.float32
bf16 = jnp.bfloat16

SMEM = pl.BlockSpec(memory_space=pltpu.SMEM)
VMEM = pl.BlockSpec(memory_space=pltpu.VMEM)
HBM = pl.BlockSpec(memory_space=pltpu.HBM)
ANY = pl.BlockSpec(memory_space=pl.ANY)
PARAMS = pltpu.CompilerParams(vmem_limit_bytes=16 << 20)


def swapped(value, bit):
    count = lax.axis_size("seq")
    return lax.ppermute(value, "seq", [(at, at ^ bit) for at in range(count)])


def kernel_call(kernel, operands, tied=(), in_specs=None, name=None, **rest):
    given = len(operands)

    def run(*refs):
        kernel(*refs[:given], *refs[given + len(tied) :])

    return pl.pallas_call(
        run, in_specs=list(in_specs) + [ANY] * len(tied), name=name, **rest
    )(*operands, *tied)


def cost(flops, moved_bytes, exps=0):
    return pl.CostEstimate(flops=flops, bytes_accessed=moved_bytes, transcendentals=exps)


def attention_kernel(
    place_ref, q_ref, own_k, own_v, back2_k, back2_v, back4_ref, pair_ref, out_ref
):
    back4_k, back4_v = back4_ref.at[0], back4_ref.at[1]
    keys = [own_k, back4_k, pair_ref.at[0, 0], back2_k, pair_ref.at[1, 0]]
    vals = [own_v, back4_v, pair_ref.at[0, 1], back2_v, pair_ref.at[1, 1]]
    rows, width = q_ref.shape
    place = place_ref[0]
    factor = HEAD_DIM ** (-0.5) * math.log2(math.e)
    q_at = lax.broadcasted_iota(jnp.int32, (rows, rows), 0)
    k_at = lax.broadcasted_iota(jnp.int32, (rows, rows), 1)
    inside = k_at <= q_at

    def attend(cols, masked):
        query = q_ref[:, cols]

        def score(at):
            return lax.dot_general(
                query, keys[at][:, cols], (((1,), (1,)), ((), ())), preferred_element_type=f32
            )

        def seen(part, back):
            return jnp.where(place >= back, part, -1e30) if masked else part

        parts = [jnp.where(inside, score(0), seen(score(1), 4))]
        parts += [seen(score(at), at - 1) for at in range(2, 5)]
        row_max = functools.reduce(
            jnp.maximum, [jnp.max(part, axis=1, keepdims=True) for part in parts]
        )
        shift = row_max * factor
        parts = [jnp.exp2(part * factor - shift) for part in parts]
        total = functools.reduce(jnp.add, [jnp.sum(e, axis=1, keepdims=True) for e in parts])
        scale = 1.0 / total
        parts = [(part * scale).astype(bf16) for part in parts]
        zero = jnp.zeros_like(parts[0])
        parts = [jnp.where(inside, parts[0], zero), jnp.where(inside, zero, parts[0])] + parts[1:]
        result = jnp.zeros((rows, HEAD_DIM), f32)
        for part, val in zip(parts, vals):
            result += jnp.dot(part, val[:, cols], preferred_element_type=f32)
        out_ref[:, cols] = result.astype(bf16)

    def every(masked):
        for head in range(width // HEAD_DIM):
            attend(slice(head * HEAD_DIM, (head + 1) * HEAD_DIM), masked)

    pl.when(place >= 4)(lambda: every(False))
    pl.when(place < 4)(lambda: every(True))


def attention(place, query, blocks, pair):
    rows, width = query.shape
    return pl.pallas_call(
        attention_kernel,
        out_shape=jax.ShapeDtypeStruct((rows, width), bf16),
        in_specs=[SMEM] + [VMEM] * 7,
        out_specs=VMEM,
        compiler_params=PARAMS,
        cost_estimate=cost(20 * rows * rows * width, 24 * rows * width, 5 * rows * rows * 5),
        name="attention",
    )(place[None], query, *blocks, pair)


def prepare_kernel(place_ref, gate_ref, up_ref, down_ref, out_ref, hold):
    hidden = gate_ref.shape[1]
    half = hidden // 2
    window = hold.shape[0]
    core = place_ref[0] % 2
    low = pl.multiple_of(core * (hidden - window), 128)
    off = pl.multiple_of(core * (half - hidden + window), 64)
    for at, ref in enumerate((gate_ref, up_ref, down_ref)):
        hold[...] = ref[:, pl.ds(low, window)].T
        out_ref[at] = hold[pl.ds(off, half), :]


def prepared(place, w_gate, w_up, w_down):
    feats, hidden = w_gate.shape
    half = hidden // 2
    window = -(-half // 128) * 128
    return pl.pallas_call(
        prepare_kernel,
        out_shape=jax.ShapeDtypeStruct((3, half, feats), bf16),
        in_specs=[SMEM] + [VMEM] * 3,
        out_specs=VMEM,
        scratch_shapes=[pltpu.VMEM((window, feats), bf16)],
        compiler_params=PARAMS,
        cost_estimate=cost(0, 9 * feats * hidden),
        name="prepare",
    )(place[None], w_gate, w_up, w_down)


def pack_kernel(key_ref, val_ref, own_ref):
    own_ref[0] = key_ref[...]
    own_ref[1] = val_ref[...]


def packed(att_k, att_v, *tied):
    return kernel_call(
        pack_kernel,
        (att_k, att_v),
        tied,
        out_shape=jax.ShapeDtypeStruct((2,) + att_k.shape, bf16),
        in_specs=[VMEM] * 2,
        out_specs=VMEM,
        compiler_params=PARAMS,
        cost_estimate=cost(0, 0),
        name="pack",
    )


def grad_kernel(
    place_ref, turned_ref, k0_ref, k1_ref, v0_ref, v1_ref, r0_ref, r1_ref,
    send_p, send_q, keep_p, keep_q, hold,
):
    def project(at, rows):
        return lax.dot_general(
            turned_ref[at], rows, (((1,), (1,)), ((), ())), preferred_element_type=f32
        )

    terms = []
    for keys, vals, rate_ref in ((k0_ref, v0_ref, r0_ref), (k1_ref, v1_ref, r1_ref)):
        rate = rate_ref[...]
        pre_gate = project(0, keys[...])
        pre_up = project(1, keys[...])
        back = rate * project(2, vals[...])
        sigmoid_v = jax.nn.sigmoid(pre_gate)
        silu = pre_gate * sigmoid_v
        slope = sigmoid_v * (1.0 + pre_gate * (1.0 - sigmoid_v))
        terms.append(
            (
                (back * pre_up * slope).astype(bf16),
                (back * silu).astype(bf16),
                (rate * silu * pre_up).astype(bf16),
            )
        )
    sources = ((k0_ref, k1_ref), (k0_ref, k1_ref), (v0_ref, v1_ref))
    for at in range(3):
        hold[at] = jnp.dot(
            terms[0][at], sources[at][0][...], preferred_element_type=f32
        ) + jnp.dot(terms[1][at], sources[at][1][...], preferred_element_type=f32)
    quart = send_p.shape[2]
    row = (place_ref[0] // 2) % 2
    for at in range(3):
        send, keep = (send_p.at[at], keep_p.at[at]) if at < 2 else (send_q.at[0], keep_q.at[0])
        for other in range(2):
            there = pl.multiple_of((2 * (1 - row) + other) * quart, 8)
            here = pl.multiple_of((2 * row + other) * quart, 8)
            send[other] = hold[at, pl.ds(there, quart), :].astype(bf16)
            keep[other] = hold[at, pl.ds(here, quart), :]


def gradients(place, turned_w, k0, k1, v0, v1, r0, r1, *tied):
    _, half, feats = turned_w.shape
    rows = k0.shape[0]
    return kernel_call(
        grad_kernel,
        (place[None], turned_w, k0, k1, v0, v1, r0, r1),
        tied,
        out_shape=[
            jax.ShapeDtypeStruct((count, 2, half // 4, feats), kind)
            for kind in (bf16, f32)
            for count in (2, 1)
        ],
        in_specs=[SMEM] + [VMEM] * 7,
        out_specs=[VMEM] * 4,
        scratch_shapes=[pltpu.VMEM((3, half, feats), f32)],
        compiler_params=PARAMS,
        cost_estimate=cost(24 * rows * half * feats, 20 * half * feats, 2 * half * rows),
        name="gradients",
    )


def stage(kernel, operands, outs, name, *tied):
    return kernel_call(
        kernel,
        (operands[0][None], *operands[1:]),
        tied,
        out_shape=[jax.ShapeDtypeStruct(shape, kind) for shape, kind in outs],
        in_specs=[SMEM] + [VMEM] * (len(operands) - 1),
        out_specs=[VMEM] * len(outs),
        compiler_params=PARAMS,
        cost_estimate=cost(0, 0),
        name=name,
    )


def halve(place_ref, keep, got, send, kept):
    row = (place_ref[0] // 4) % 2
    for at in range(keep.shape[0]):
        send[at] = (keep[at, 1 - row] + got[at, 1 - row].astype(f32)).astype(bf16)
        kept[at] = keep[at, row] + got[at, row].astype(f32)


def add(place_ref, keep, got, send, total):
    for at in range(keep.shape[0]):
        summed = keep[at] + got[at].astype(f32)
        total[at] = summed
        send[at] = summed.astype(bf16)


def window_kernel(place_ref, own_k, own_v, back_ref, out_k, out_v):
    back_k, back_v = back_ref.at[0], back_ref.at[1]
    early = (place_ref[0] // 2) % 2 == 0

    @pl.when(early)
    def _():
        out_k[...] = own_k[...]
        out_v[...] = own_v[...]

    @pl.when(jnp.logical_not(early))
    def _():
        out_k[...] = back_k[...]
        out_v[...] = back_v[...]


def renorm_kernel(place_ref, old_ref, keep_p, got_p, keep_q, got_q, part_a, part_b):
    rows = part_a.shape[1]
    units = 2 * rows
    first = 0
    if old_ref.shape[1] > units:
        quart = old_ref.shape[1] // 4
        first = (place_ref[0] // 2) % 2 * (2 * quart) + (place_ref[0] // 4) % 2 * quart
        first = pl.multiple_of(first, 16)
    for at in range(3):
        keep, got = (keep_p[at], got_p[at]) if at < 2 else (keep_q[0], got_q[0])
        old = old_ref[at, pl.ds(first, units), :].astype(f32)
        updated = old + (keep + got.astype(f32))
        old_norm = jnp.sqrt(jnp.sum(old * old, axis=1, keepdims=True))
        squares = jnp.sum(updated * updated, axis=1, keepdims=True)
        fresh = updated * (old_norm / jnp.sqrt(squares + norm_eps))
        part_a[at] = fresh[:rows].astype(bf16)
        part_b[at] = fresh[rows:].astype(bf16)


def near_kernel(
    place_ref, part_a, got_a, part_b, got_b, own_k, own_v, back2_k, back2_v, back4_ref,
    near_a, near_b, near, pair,
):
    back4_k, back4_v = back4_ref.at[0], back4_ref.at[1]
    rows = part_a.shape[1]
    for at in range(3):
        for part, got, out, low in (
            (part_a, got_a, near_a, 0),
            (part_b, got_b, near_b, 2 * rows),
        ):
            both = jnp.concatenate([part[at].astype(f32), got[at].astype(f32)], axis=0)
            out[at] = both.astype(bf16)
            near[at, low : low + 2 * rows] = both.astype(bf16)
    even = place_ref[0] % 2 == 0

    @pl.when(even)
    def _():
        pair[0, 0] = own_k[...]
        pair[0, 1] = own_v[...]
        pair[1, 0] = back2_k[...]
        pair[1, 1] = back2_v[...]

    @pl.when(jnp.logical_not(even))
    def _():
        pair[0, 0] = back2_k[...]
        pair[0, 1] = back2_v[...]
        pair[1, 0] = back4_k[...]
        pair[1, 1] = back4_v[...]


def near_rows(place, part_a, got_a, part_b, got_b, blocks):
    rows, feats = part_a.shape[1:]
    return pl.pallas_call(
        near_kernel,
        out_shape=[
            jax.ShapeDtypeStruct((3, size * rows, feats), bf16) for size in (2, 2, 4)
        ]
        + [jax.ShapeDtypeStruct((2, 2) + blocks[0].shape, bf16)],
        in_specs=[SMEM] + [VMEM] * 9,
        out_specs=[VMEM] * 4,
        compiler_params=PARAMS,
        cost_estimate=cost(0, part_a.size * 14 + blocks[0].size * 8),
        name="near",
    )(place[None], part_a, got_a, part_b, got_b, *blocks)


def fast_output(query, hold):
    gate_q = lax.dot_general(
        query, hold[0], (((1,), (1,)), ((), ())), preferred_element_type=f32
    )
    up_q = lax.dot_general(query, hold[1], (((1,), (1,)), ((), ())), preferred_element_type=f32)
    hidden_q = (gate_q * jax.nn.sigmoid(gate_q) * up_q).astype(bf16)
    return jnp.dot(hidden_q, hold[2], preferred_element_type=f32)


def first_kernel(q_ref, near, near_other, out_ref, hold):
    rows = near.shape[1]
    hold[:, :rows] = near[...]
    hold[:, rows:] = near_other[...]
    out_ref[...] = fast_output(q_ref[...], hold)


def first_half(query, near, near_other):
    rows, feats = query.shape
    units = 2 * near.shape[1]
    return pl.pallas_call(
        first_kernel,
        out_shape=jax.ShapeDtypeStruct((rows, feats), f32),
        in_specs=[VMEM] * 3,
        out_specs=VMEM,
        scratch_shapes=[pltpu.VMEM((3, units, feats), bf16)],
        compiler_params=PARAMS,
        cost_estimate=cost(6 * rows * units * feats, 12 * units * feats, units * rows),
        name="first_half",
    )(query, near, near_other)


def far_kernel(got_a, got_b, attended, half_out, far, passed, passed_half):
    del attended, half_out, passed, passed_half
    rows = got_a.shape[1]
    far[:, :rows] = got_a[...]
    far[:, rows:] = got_b[...]


def far_rows(got_a, got_b, attended, half_out):
    shape = (3, 2 * got_a.shape[1], got_a.shape[2])
    return pl.pallas_call(
        far_kernel,
        out_shape=[
            jax.ShapeDtypeStruct(shape, bf16),
            jax.ShapeDtypeStruct(attended.shape, bf16),
            jax.ShapeDtypeStruct(half_out.shape, f32),
        ],
        in_specs=[VMEM] * 2 + [ANY] * 2,
        out_specs=[VMEM, ANY, ANY],
        input_output_aliases={2: 1, 3: 2},
        compiler_params=PARAMS,
        cost_estimate=cost(0, got_a.size * 8),
        name="far",
    )(got_a, got_b, attended, half_out)


def part_kernel(q_ref, before, rows_ref, out_ref):
    out_ref[...] = (before[...] + fast_output(q_ref[...], rows_ref)).astype(out_ref.dtype)


def part_step(query, before, weights, kind, name):
    rows, feats = query.shape
    units = weights.shape[1]
    return pl.pallas_call(
        part_kernel,
        out_shape=jax.ShapeDtypeStruct((rows, feats), kind),
        in_specs=[VMEM] * 3,
        out_specs=VMEM,
        compiler_params=PARAMS,
        cost_estimate=cost(6 * rows * units * feats, 6 * units * feats, units * rows),
        name=name,
    )(query, before, weights)


def body(att_q, att_k, att_v, fast_q, fast_k, fast_v, learn_rates, w_gate, w_up, w_down):
    count = lax.axis_size("seq")
    place = lax.axis_index("seq")
    feats, hidden = w_gate.shape
    quart = hidden // 8
    later = [1 << at for at in range(3, count.bit_length() - 1)]
    own_bit = {bit: (place // bit) % 2 for bit in [2, 4] + later}

    other_k, other_v = swapped(fast_k, 1), swapped(fast_v, 1)
    other_r = swapped(learn_rates, 1)
    turned_w = prepared(place, w_gate, w_up, w_down)
    own = packed(att_k, att_v, other_r)
    back4 = lax.ppermute(own, "seq", [(at, (at + 4) % count) for at in range(count)])
    send_p, send_q, keep_p, keep_q = gradients(
        place, turned_w, fast_k, other_k, fast_v, other_v,
        learn_rates[None, :], other_r[None, :], own,
    )
    rest = quart
    start = own_bit[2] * 2 * quart + own_bit[4] * quart
    for bit in later[:-1]:
        rest //= 2
        start += own_bit[bit] * rest
    old = turned_w
    if len(later) > 1 or quart % 16 > 0:
        old = lax.dynamic_slice_in_dim(turned_w, start, rest, 1)

    def shapes(matrices):
        return [((matrices, quart, feats), bf16), ((matrices, quart, feats), f32)]

    def scattered(send, total):
        for bit in later[:-1]:
            total = total.reshape(total.shape[0], 2, -1, feats)
            send = lax.dynamic_index_in_dim(total, 1 - own_bit[bit], 1, keepdims=False)
            total = lax.dynamic_index_in_dim(total, own_bit[bit], 1, keepdims=False)
            total = total + swapped(send.astype(bf16), bit).astype(f32)
            send = total.astype(bf16)
        return total, swapped(send, later[-1])

    got_p, got_q = swapped(send_p, 2), swapped(send_q, 2)
    send_p, keep_p = stage(halve, (place, keep_p, got_p), shapes(2), "second_p")
    got_p = swapped(send_p, 4)
    send_q, keep_q = stage(halve, (place, keep_q, got_q), shapes(1), "second_q", send_p)
    got_q = swapped(send_q, 4)
    send_p, total_p = stage(add, (place, keep_p, got_p), shapes(2), "third_p", send_q)
    windows = stage(
        window_kernel,
        (place, att_k, att_v, back4),
        [(att_k.shape, bf16)] * 2,
        "window",
        send_p,
    )
    back2_k, back2_v = (swapped(part, 2) for part in windows)
    blocks = (att_k, att_v, back2_k, back2_v, back4)
    total_p, got_p = scattered(send_p, total_p)
    send_q, total_q = stage(add, (place, keep_q, got_q), shapes(1), "third_q", send_p)
    total_q, got_q = scattered(send_q, total_q)
    part_a, part_b = stage(
        renorm_kernel,
        (place, old, total_p, got_p, total_q, got_q),
        [((3, rest // 2, feats), bf16)] * 2,
        "renorm",
    )

    for bit in reversed(later[:-1]):
        part_a = jnp.concatenate([part_a, swapped(part_a, bit)], axis=1)
        part_b = jnp.concatenate([part_b, swapped(part_b, bit)], axis=1)
    near_a, near_b, near, pair = near_rows(
        place, part_a, swapped(part_a, 4), part_b, swapped(part_b, 2), blocks
    )
    got_a, got_b = swapped(near_a, 2), swapped(near_b, 4)
    near_other = swapped(near, 1)
    pair = swapped(pair, 1)
    attended = attention(place, att_q, blocks, pair)
    half_out = first_half(fast_q, near, near_other)
    far, attended, half_out = far_rows(got_a, got_b, attended, half_out)
    half_out = part_step(fast_q, half_out, far, f32, "own_far")
    fast_out = part_step(fast_q, half_out, swapped(far, 1), bf16, "last")
    return (attended, fast_out)


def solution(mesh):
    tokens = P("seq", "head")
    weights = P(None, "head")
    return jax.shard_map(
        body,
        mesh=mesh,
        in_specs=(tokens,) * 6 + (P("seq"),) + (weights,) * 3,
        out_specs=(tokens, tokens),
        check_vma=False,
    )
```
